512 devices in a mesh: box: 128 (over z, x, core), slab: 4 (over y).
Axes of the slice: x: 4, y: 4, z: 16, core: 2. Of those that a mesh axis runs over, the one named last changes fastest.
Arguments:
- particle_volume: float32 [1048576], P(('box', 'slab')), may hold values from 0.02 to 0.2
- drag_coeff: float32 [1048576], P(('box', 'slab')), may hold values from 0.1 to 1
- drag_momentum: float32 [2, 1048576], P(None, ('box', 'slab')), may hold values from -6 to 6
- offsets: float32 [3, 1048576], P(None, ('box', 'slab')), may hold values from -0.5 to 0.5
- cell_index: int32 [1048576], P(('box', 'slab')), may hold values from 0 to 16383
- destinations: int32 [1048576, 1], P(('box', 'slab')), may hold values from 0 to 127; in each aligned block of 2048 rows (0 to 2047, 2048 to 4095, ...) at most 32 rows name the same one
- fluid_rhs: float32 [2048, 32, 128], P('box', 'slab'), may hold values from -5 to 7
- wall_mask: int32 [2048, 32, 128], P('box', 'slab'), may hold values from 0 to 1, as said below
Outputs:
- coupled: float32 [4, 2048, 32, 128], P(None, 'box', 'slab')
- pressure: float32 [2048, 32, 128], P('box', 'slab')
The draws below stay inside these ranges and needn't reach their ends.
Inputs may be any that keep to these rules, and one draw needn't show every extreme that they name: `cell_index`: entries encode (x * 8 + y) * 128 + z. `destinations`: A particle keeps its slab. Among one device's 2048 rows no box index is named by more than 32 rows, and some box index by exactly 32 rows. `wall_mask`: obstacle cells fill whole aligned blocks of 4 x 4 x 4 cells.
All inputs are finite; a program needn't handle non-finite values.
Results may differ from the reference program's by a relative error of at most 0.0038.
Values sent between devices are 32-bit elements; how exact they have to be, the bound alone decides.
No kernel may reach another device: no remote copies, remote signals or barrier semaphores. Data moves between devices by JAX's collectives and lax.ppermute only.
A program may use at most 64 MiB of HBM per device.

```python
import math
import jax
import jax.numpy as jnp
import numpy as np

CX = 16
CY = 8
NZ = 128
PART_DEV = 2048
CHANNELS = 4
LEVELS = 3
SWEEPS = 2
BOTTOM = 4
CYCLES = 2
CAP = 32
PARTICLES = 1048576
NX = 2048
NY = 32
N_BOX = 128
N_SLAB = 4


def draw_fluid_rhs(key, part):
    key = jax.random.fold_in(key, 7)
    rough_key = jax.random.fold_in(key, 0)
    rough = jnp.clip(jax.random.normal(rough_key, (NX, NY, NZ), jnp.float32), -5.0, 5.0)
    smooth = 0.5 * jnp.ones((NX,), jnp.float32)
    return (rough + smooth[:, None, None]).astype(jnp.float32)


def draw_wall_mask(key, part):
    key = jax.random.fold_in(key, 11)
    blocks = jax.random.randint(key, (NX // 4, NY // 4, NZ // 4), 0, 16)
    opened = (blocks != 0).astype(jnp.int32)
    opened = jnp.repeat(jnp.repeat(jnp.repeat(opened, 4, axis=0), 4, axis=1), 4, axis=2)
    return opened.astype(jnp.int32)


def touch_ends(entries, stream_key, low, largest):
    spot = [jax.random.randint(jax.random.fold_in(stream_key, axis), (), 0, length) for axis, length in enumerate(entries.shape)]
    longest = entries.shape.index(max(entries.shape))
    beside = spot[:longest] + [(spot[longest] + 1) % entries.shape[longest]] + spot[longest + 1:]
    return entries.at[tuple(spot)].set(low).at[tuple(beside)].set(largest)


def shard_levels(stream_key, shape, shards, low, top_value):
    loudness, own = 1.0, jax.random.fold_in(stream_key, 6)
    for axis_at, shards_of in shards:
        heights = jnp.exp(jax.random.uniform(jax.random.fold_in(own, axis_at), (shards_of,), jnp.float32, low / len(shards), top_value / len(shards)))
        loudness = loudness * jnp.repeat(heights, shape[axis_at] // shards_of).reshape([-1 if axis == axis_at else 1 for axis in range(len(shape))])
    return loudness


def routed_block(stream_key, own, number, rows, amount, top, limit, lean):
    order = jax.random.permutation(stream_key, amount)
    heavy_load, usual = load_shares(amount, rows * top, limit, lean, True), load_shares(amount, rows * top, limit, lean, False)
    places = jnp.arange(amount)

    def named(tallies, offset_by):
        used = int((tallies > 0).sum())
        fixed = max(1, used // 4)
        passed = fixed + (places - fixed + offset_by * (used - fixed)) % max(1, amount - fixed)
        return jnp.zeros((amount,), jnp.int32).at[order[jnp.where(places < fixed, places, passed)]].set(jnp.asarray(tallies, jnp.int32))

    tallies = jnp.where(number % 4 == 0, named(heavy_load, number // 4), named(usual, number - number // 4 - 1))
    mixed = jax.random.permutation(jax.random.fold_in(own, 3), amount)
    donor, sink = mixed[0:amount // 2 * 2:2], mixed[1:amount // 2 * 2:2]
    margin = jnp.minimum(tallies[donor] - 1, limit - tallies[sink]) // 2
    margin = jnp.where((donor == order[0]) | (sink == order[0]) | (tallies[sink] == 0), 0, jnp.maximum(margin, 0))
    passed = jax.random.randint(jax.random.fold_in(own, 4), (amount // 2,), 0, 1 << 20) % (margin + 1)
    tallies = tallies.at[donor].add(-passed).at[sink].add(passed)
    items = jnp.searchsorted(jnp.cumsum(tallies), jnp.arange(rows * top), side="right").astype(jnp.int32)
    listing = items.reshape(top, rows).T
    listing = listing[jax.random.permutation(jax.random.fold_in(own, 1), rows)]
    offset_by = jax.random.randint(jax.random.fold_in(own, 2), (rows, 1), 0, top)
    return jnp.take_along_axis(listing, (jnp.arange(top)[None, :] + offset_by) % top, axis=1)


def load_shares(amount, total, limit, skew, full):
    weights = [(1 << 20) // math.isqrt(grade ** skew) + 1 for grade in range(1, amount + 1)]
    largest = limit if full else min(limit, max(-(-total // amount), total * weights[0] // sum(weights)))
    least = 1 if total - largest >= amount - 1 else 0
    given, spare = [largest] + [least] * (amount - 1), total - largest - least * (amount - 1)
    while spare > 0:
        free = [i for i in range(1, amount) if given[i] < largest] or [i for i in range(1, amount) if given[i] < limit]
        whole, budget = sum([weights[i] for i in free]), spare
        for i in free:
            extra = min(limit - given[i], max(1, budget * weights[i] // whole), spare)
            given[i] = given[i] + extra
            spare = spare - extra
    return np.array(given)


def noise(own_key, dims, spread, reach, cuts=(), held_as=jnp.bfloat16):
    loudness = shard_levels(own_key, dims, cuts, -0.22, 0.18) if cuts else 1.0
    result = jax.random.normal(own_key, dims, jnp.float32) * spread * loudness
    return jnp.minimum(jnp.maximum(result, -reach), reach).astype(held_as)


def setup_inputs(seed: int = 0) -> dict:
    keys = jax.random.split(jax.random.key(seed), 9)
    particle_volume = jnp.clip(jnp.exp(math.log(0.2) - 2.3025851 * jax.random.uniform(keys[0], (PARTICLES,), jnp.float32) ** shard_levels(keys[0], (PARTICLES,), ((0, 512),), -0.2, 0.2)), 0.02, 0.2)
    drag_coeff = jnp.clip(jnp.exp(math.log(1.0) - 2.3025851 * jax.random.uniform(keys[1], (PARTICLES,), jnp.float32) ** shard_levels(keys[1], (PARTICLES,), ((0, 512),), -0.2, 0.2)), 0.1, 1.0)
    drag_momentum = noise(keys[2], (2, PARTICLES), 1.0, 6.0, ((1, 512),), jnp.float32)
    offsets = jnp.clip(jax.random.uniform(keys[3], (3, PARTICLES), jnp.float32, -0.5, 0.5) * shard_levels(keys[3], (3, PARTICLES), ((1, 512),), -0.4, 0.0), -0.5, 0.5)
    cell_index = touch_ends(jax.random.randint(keys[4], (PARTICLES,), 0, CX * CY * NZ), jax.random.fold_in(keys[4], 1), 0, (CX * CY * NZ) - 1).astype(jnp.int32)
    destinations_keys = jax.random.split(jax.random.fold_in(keys[5], 1), PARTICLES // PART_DEV)
    destinations_turns = jax.random.permutation(jax.random.fold_in(keys[5], 3), PARTICLES // PART_DEV)
    destinations = jax.vmap(lambda own, number: routed_block(jax.random.fold_in(keys[5], 2), own, number, PART_DEV, N_BOX, 1, CAP, 2))(destinations_keys, destinations_turns).reshape((PARTICLES, 1))
    fluid_rhs = draw_fluid_rhs(jax.random.fold_in(keys[8], 71), 0)
    wall_mask = draw_wall_mask(jax.random.fold_in(keys[8], 71), 0)
    return dict(particle_volume=particle_volume, drag_coeff=drag_coeff, drag_momentum=drag_momentum, offsets=offsets, cell_index=cell_index, destinations=destinations, fluid_rhs=fluid_rhs, wall_mask=wall_mask)


OMEGA = 0.8


def tap_weights(frac):
    return [0.5 * (0.5 - frac) * (0.5 - frac), 0.75 - frac * frac, 0.5 * (0.5 + frac) * (0.5 + frac)]


def neighbours(extended):
    beside = extended[2:, 1:-1, 1:-1] + extended[:-2, 1:-1, 1:-1]
    beside = beside + extended[1:-1, 2:, 1:-1] + extended[1:-1, :-2, 1:-1]
    beside = beside + extended[1:-1, 1:-1, 2:] + extended[1:-1, 1:-1, :-2]
    return beside


def applied_op(extended, damping, spacing):
    current = extended[1:-1, 1:-1, 1:-1]
    return spacing * (6.0 * current - neighbours(extended)) + damping * current


def relax_cells(extended, source, damping, opened, spacing):
    current = extended[1:-1, 1:-1, 1:-1]
    applied = spacing * (6.0 * current - neighbours(extended)) + damping * current
    return current + OMEGA * opened * (source - applied) / (6.0 * spacing + damping)


def extend_field(field):
    wrapped = jnp.pad(field, ((1, 1), (1, 1), (0, 0)), mode="wrap")
    return jnp.pad(wrapped, ((0, 0), (0, 0), (1, 1)))


def coarsen(field):
    sx, sy, sz = field.shape
    return field.reshape(sx // 2, 2, sy // 2, 2, sz // 2, 2).mean(axis=(1, 3, 5))


def coarsen_min(field):
    sx, sy, sz = field.shape
    return field.reshape(sx // 2, 2, sy // 2, 2, sz // 2, 2).min(axis=(1, 3, 5))


def prolong(field):
    return jnp.repeat(jnp.repeat(jnp.repeat(field, 2, axis=0), 2, axis=1), 2, axis=2)


def vcycle(stratum, current, source, levels):
    damping, opened, spacing = levels[stratum]
    if stratum == len(levels) - 1:
        for repeat in range(BOTTOM):
            current = relax_cells(extend_field(current), source, damping, opened, spacing)
        return current
    for repeat in range(SWEEPS):
        current = relax_cells(extend_field(current), source, damping, opened, spacing)
    residue = opened * (source - applied_op(extend_field(current), damping, spacing))
    coarse_source = coarsen(residue)
    correction = vcycle(stratum + 1, jnp.zeros_like(coarse_source), coarse_source, levels)
    current = current + opened * prolong(correction)
    for repeat in range(SWEEPS):
        current = relax_cells(extend_field(current), source, damping, opened, spacing)
    return current


def reference(particle_volume, drag_coeff, drag_momentum, offsets, cell_index, destinations, fluid_rhs, wall_mask):
    particle_count = particle_volume.shape[0]
    owner_box = destinations[:, 0]
    slab_of = (jnp.arange(particle_count, dtype=jnp.int32) // PART_DEV) % N_SLAB
    z_cell = cell_index % NZ
    y_cell = (cell_index // NZ) % CY
    x_cell = cell_index // (NZ * CY)
    x_centre = owner_box * CX - CX // 2 + x_cell
    y_centre = slab_of * CY + y_cell
    values = jnp.stack([particle_volume, drag_coeff, drag_momentum[0], drag_momentum[1]])
    weight_x = tap_weights(offsets[0])
    weight_y = tap_weights(offsets[1])
    weight_z = tap_weights(offsets[2])
    deposit = jnp.zeros((CHANNELS, NX * NY * NZ), jnp.float32)
    for i in range(3):
        x_global = (x_centre + i - 1) % NX
        for j in range(3):
            y_global = (y_centre + j - 1) % NY
            planar = (values * (weight_x[i] * weight_y[j])[None, :]).astype(jnp.bfloat16).astype(jnp.float32)
            for k in range(3):
                z_global = z_cell + k - 1
                inside = ((z_global >= 0) & (z_global < NZ)).astype(jnp.float32)
                vertical = weight_z[k].astype(jnp.bfloat16).astype(jnp.float32) * inside
                flat_index = (x_global * NY + y_global) * NZ + jnp.clip(z_global, 0, NZ - 1)
                deposit = deposit.at[:, flat_index].add(planar * vertical[None, :])
    coupled = deposit.reshape(CHANNELS, NX, NY, NZ)
    opened = wall_mask.astype(jnp.float32)
    source = opened * ((1.0 - coupled[0]) * fluid_rhs + coupled[2] + coupled[3])
    levels = [(coupled[1], opened, 1.0)]
    for stratum in range(1, LEVELS):
        damping, opened_now, spacing = levels[-1]
        levels.append((coarsen(damping), coarsen_min(opened_now), spacing * 0.25))
    pressure = jnp.zeros_like(source)
    for repeat in range(CYCLES):
        pressure = vcycle(0, pressure, source, levels)
    return coupled, pressure
```

```python
import jax
import jax.numpy as jnp
from jax import lax
from jax.experimental import pallas as pl
from jax.experimental.pallas import tpu as pltpu
from jax.sharding import PartitionSpec as P

F32 = jnp.float32
BF16 = jnp.bfloat16
I32 = jnp.int32

CX, CY, NZ = 16, 8, 128
PART = 2048
N_BOX = 128
CAP = 32
SLOTS = N_BOX * CAP
XE = CX + 2
OMEGA = 0.8

T0, T1, T2 = 30, 40, 20

LIMIT = 48 * 1024 * 1024

NT = (((1,), (1,)), ((), ()))


def tap_weights(frac):
    return (
        0.5 * (0.5 - frac) * (0.5 - frac),
        0.75 - frac * frac,
        0.5 * (0.5 + frac) * (0.5 + frac),
    )


def spread(index, at, taps):
    return jnp.where(
        index == at,
        taps[0],
        jnp.where(index == at + 1, taps[1], jnp.where(index == at + 2, taps[2], 0.0)),
    )


def route_kernel(vol, drag, mom, off, cell, dest, out, picked):
    target = dest[...]
    hot = lax.broadcasted_iota(I32, (N_BOX, PART), 0) == target
    hot_f = jnp.where(hot, 1.0, 0.0)
    hot_b = hot_f.astype(BF16)
    width = 256
    above = lax.broadcasted_iota(I32, (width, width), 0) < lax.broadcasted_iota(I32, (width, width), 1)
    before = jnp.where(above, 1.0, 0.0).astype(BF16)
    carry = jnp.zeros((N_BOX, 1), F32)
    places = []
    for k in range(PART // width):
        cut = slice(k * width, (k + 1) * width)
        rank = jnp.dot(hot_b[:, cut], before, preferred_element_type=F32) + carry
        places.append(jnp.sum(rank * hot_f[:, cut], axis=0, keepdims=True))
        carry = carry + jnp.sum(hot_f[:, cut], axis=1, keepdims=True)
    place = jnp.concatenate(places, axis=1).astype(I32)
    at_place = lax.broadcasted_iota(I32, (CAP, PART), 0) == place
    fields = [vol[...], drag[...], mom[0:1, :], mom[1:2, :]]
    fields += [off[0:1, :], off[1:2, :], off[2:3, :], cell[...].astype(F32)]
    for f, left in enumerate(fields):
        for part in range(3):
            rounded = left.astype(BF16).astype(F32)
            row = (part * 8 + f) * CAP
            picked[row : row + CAP, :] = jnp.where(at_place, rounded, 0.0).astype(BF16)
            left = left - rounded
    sums = lax.dot_general(picked[...], hot_b, NT, preferred_element_type=F32)
    half = 8 * CAP
    sums = sums[:half] + sums[half : 2 * half] + sums[2 * half :]
    out[...] = sums.T


def deposit_kernel(recv, rhs, wall, prev, pay, craw, par, cells, xs, amat, vmat, acc):
    fields = recv[...].T
    for c in range(4):
        par[c] = fields[c * CAP : (c + 1) * CAP]
    cell = fields[7 * CAP :].astype(I32)
    x_cell = cell // (NZ * CY)
    cells[0] = x_cell
    cells[1] = (cell // NZ) % CY
    cells[2] = cell % NZ
    for d in range(3):
        for k, tap in enumerate(tap_weights(fields[(4 + d) * CAP : (5 + d) * CAP])):
            par[4 + 3 * d + k] = tap
    for x in range(XE):
        xs[x] = spread(x, x_cell, (par[4], par[5], par[6]))
    sub24 = lax.broadcasted_iota(I32, (24, NZ), 0)
    sub8 = lax.broadcasted_iota(I32, (8, NZ), 0)
    sub128 = lax.broadcasted_iota(I32, (NZ, NZ), 0)

    def one(w):
        def row(k):
            return par[k, pl.ds(w, 1), :]

        lanes = pl.ds(pl.multiple_of(w * NZ, NZ), NZ)
        vals = [row(c) for c in range(4)]
        wx = [row(4 + k) for k in range(3)]
        wy = [row(7 + k) for k in range(3)]
        wz = [row(10 + k) for k in range(3)]
        xc, yc, zc = [cells[d, pl.ds(w, 1), :] for d in range(3)]
        y_tile = spread(sub8, yc - 1, wy)
        low = jnp.where(yc == 0, wy[0], 0.0)
        high = jnp.where(yc == CY - 1, wy[2], 0.0)
        x_tile = spread(sub24, xc, wx)
        edge = jnp.concatenate([x_tile * low, x_tile * high], axis=0)
        for c in range(4):
            amat[576 + 48 * c : 576 + 48 * (c + 1), lanes] = (vals[c] * edge).astype(BF16)
        for pair in range(XE // 2):
            plane = jnp.concatenate([xs[2 * pair + k, pl.ds(w, 1), :] * y_tile for k in range(2)], axis=0)
            for c in range(4):
                r = 144 * c + 16 * pair
                amat[r : r + 16, lanes] = (vals[c] * plane).astype(BF16)
        vmat[:, lanes] = spread(sub128, zc - 1, wz).astype(BF16)

    def pair_step(p, carry):
        one(2 * p)
        one(2 * p + 1)
        return carry

    lax.fori_loop(0, CAP // 2, pair_step, 0)
    acc[...] = lax.dot_general(amat[...], vmat[...], NT, preferred_element_type=F32)
    for x in range(XE):
        c = [acc[144 * k + 8 * x : 144 * k + 8 * x + 8, :] for k in range(4)]
        for k in range(4):
            craw[k, x] = c[k]
        if x < 9:
            right, opened = prev[x], prev[9 + x]
        else:
            right, opened = rhs[x - 9], wall[x - 9].astype(F32)
        whole = right - c[0] * right if x < CX else -(c[0] * right)
        pay[x] = opened * (whole + c[2] + c[3])
        pay[XE + x] = c[1]
        pay[2 * XE + x] = acc[pl.ds(576 + x, 8, stride=24), :]
        extra = jnp.concatenate([right[0:1], right[7:8], opened[0:1], opened[4:5]], axis=0)
        pay[3 * XE + x // 2, (x % 2) * 4 : (x % 2) * 4 + 4, :] = extra


def slab_kernel(slab, got, craw, send, keep, ssum, dsum, osum):
    s_me = slab[0]
    sub = lax.broadcasted_iota(I32, (8, NZ), 0)
    first, last = sub == 0, sub == 7

    def edges(tile, to_first, to_last):
        return tile + jnp.where(first, to_first, 0.0) + jnp.where(last, to_last, 0.0)

    for x in range(XE):
        g_row = (x % 2) * 4
        halos = [got[s, 2 * XE + x] for s in range(4)]
        for s in range(4):
            below, above = halos[(s + 3) % 4], halos[(s + 1) % 4]
            extra = got[s, 3 * XE + x // 2]
            rhs_f, rhs_l = extra[g_row : g_row + 1], extra[g_row + 1 : g_row + 2]
            o_f, o_l = extra[g_row + 2 : g_row + 3], extra[g_row + 3 : g_row + 4]
            from_below = o_f * (below[5:6] + below[7:8] - below[1:2] * rhs_f)
            from_above = o_l * (above[4:5] + above[6:7] - above[0:1] * rhs_l)
            at = x * 32 + s * 8
            ssum[at : at + 8, :] = edges(got[s, x], from_below, from_above)
            dsum[at : at + 8, :] = edges(got[s, XE + x], below[3:4], above[2:3])
            osum[x, 2 * s : 2 * s + 2, :] = extra[g_row + 2 : g_row + 4]
        below = got[(s_me + 3) % 4, 2 * XE + x]
        above = got[(s_me + 1) % 4, 2 * XE + x]
        for c in range(4):
            tile = edges(craw[c, x], below[2 * c + 1 : 2 * c + 2], above[2 * c : 2 * c + 1])
            if x < 9:
                send[128 + 9 * c + x] = tile
            else:
                keep[128 + 9 * c + x - 9] = tile
        for q in range(4):
            s_tile = ssum[pl.ds(x * 32 + q, 8, stride=4), :]
            d_tile = dsum[pl.ds(x * 32 + q, 8, stride=4), :]
            if x < CX:
                send[4 * x + q] = s_tile
                send[64 + 4 * x + q] = d_tile
            if x >= 2:
                keep[4 * (x - 2) + q] = s_tile
                keep[64 + 4 * (x - 2) + q] = d_tile
    for k, x in enumerate((1, 5, 9, 13)):
        send[164 + k] = osum[x]
    for k, x in enumerate((2, 5, 9, 13)):
        keep[164 + k] = osum[x]


def lane_index():
    return lax.broadcasted_iota(I32, (8, NZ), 1)


def take(tile, index):
    return jnp.take_along_axis(tile, index, axis=1)


def neighbour_sum(ref, t, count, whole_lanes):
    lane = lane_index()
    cur = [ref[t, q] for q in range(count)]
    sums = []
    for q in range(count):
        after = cur[q + 1] if q + 1 < count else pltpu.roll(cur[0], 7, 0)
        before = cur[q - 1] if q else pltpu.roll(cur[count - 1], 1, 0)
        left = pltpu.roll(cur[q], 1, 1)
        right = pltpu.roll(cur[q], NZ - 1, 1)
        if whole_lanes:
            left = jnp.where(lane == 0, 0.0, left)
            right = jnp.where(lane == NZ - 1, 0.0, right)
        beside = (ref[t - 1, q] + ref[t + 1, q]) + (after + before) + (left + right)
        sums.append(beside)
    return cur, sums


def rows_loop(low, high, step, body):
    passes = (high - low) // step
    assert low + passes * step == high

    def one(k, carry):
        for r in range(step):
            body(low + k * step + r)
        return carry

    lax.fori_loop(0, passes, one, 0)


def sweep(src, dst, coef, base, low, high, step, count, whole_lanes):
    def body(t):
        cur, sums = neighbour_sum(src, t, count, whole_lanes)
        for q in range(count):
            dst[t, q] = (1.0 - OMEGA) * cur[q] + base[t, q] + coef[t, q] * sums[q]

    rows_loop(low, high, step, body)


def residue_row(src, coef, base, weight, t, wt, count, whole_lanes):
    cur, sums = neighbour_sum(src, t, count, whole_lanes)
    return [weight[wt, q] * (base[t, q] + coef[t, q] * sums[q] - OMEGA * cur[q]) for q in range(count)]


def pair_lanes(tile):
    return tile + pltpu.roll(tile, NZ - 1, 1)


def start_kernel(keep, got, coupled, cc, cb, gg, v2, blocks, send, dk):
    for c in range(4):
        for x in range(CX):
            if x < 7:
                tile = keep[128 + 9 * c + x]
            elif x < 9:
                tile = keep[128 + 9 * c + x] + got[128 + 9 * c + x - 7]
            else:
                tile = got[128 + 9 * c + x - 7]
            coupled[c, x] = tile
    for k in range(4):
        blocks[k] = keep[164 + k]
        blocks[4 + k] = got[164 + k]

    def prepare(t, s_tile, d_tile, q, block):
        diag = 6.0 + d_tile
        coef = OMEGA * blocks[block] / diag
        cc[t, q] = coef
        cb[t, q] = coef * s_tile
        dk[t, q] = d_tile

    def from_keep(t):
        for q in range(4):
            prepare(t, keep[4 * t + q], keep[64 + 4 * t + q], q, (t + 1) // 4)

    def from_got(t):
        for q in range(4):
            at = 4 * (t - 14) + q
            prepare(t, got[at], got[64 + at], q, (t + 1) // 4)

    rows_loop(0, 14, 2, from_keep)
    for t in (14, 15):
        for q in range(4):
            own, at = 4 * t + q, 4 * (t - 14) + q
            prepare(t, keep[own] + got[at], keep[64 + own] + got[64 + at], q, (t + 1) // 4)
    rows_loop(16, 30, 2, from_got)
    sweep(cb, v2, cc, cb, 1, 29, 4, 4, True)

    lane = lane_index()
    even = (2 * lane) % NZ

    def coarse(k):
        b_sum, d_sum = [0.0, 0.0], [0.0, 0.0]
        for dx in range(2):
            t = 7 + 2 * k + dx
            for q in range(4):
                gg[2 * k + dx, q] = (1.0 / OMEGA) * (6.0 + dk[t, q])
                d_sum[q // 2] = d_sum[q // 2] + dk[t, q]
            for q, tile in enumerate(residue_row(v2, cc, cb, gg, t, 2 * k + dx, 4, True)):
                b_sum[q // 2] = b_sum[q // 2] + tile
        for q in range(2):
            b_tile = take(pair_lanes(b_sum[q]), even)
            d_tile = take(pair_lanes(d_sum[q]), even)
            send[2 * k + q] = 0.125 * jnp.where(lane < 64, b_tile, d_tile)

    rows_loop(0, 8, 2, coarse)
    for k in range(4):
        send[16 + k] = blocks[2 + k]


def levels_setup(parts, c1, g1, o1, c2, cb1):
    lane = lane_index()
    even = (2 * lane) % NZ
    for n, part in enumerate(parts):
        def block_step(blk, carry):
            half = jnp.where(lane < 64, take(part[16 + blk], even), 0.0)
            o1[4 * n + blk] = half
            o2 = jnp.where(lane < 32, take(half, even), 0.0)
            d_sum = 0.0
            for dx in range(2):
                for q in range(2):
                    tile = part[4 * blk + 2 * dx + q]
                    damp = jnp.where(lane < 64, pltpu.roll(tile, 64, 1), 0.0)
                    diag = 1.5 + damp
                    coef = OMEGA * half / diag
                    a = 8 * n + 2 * blk + dx
                    c1[a, q] = 0.25 * coef
                    cb1[a, q] = coef * jnp.where(lane < 64, tile, 0.0)
                    g1[a, q] = (1.0 / OMEGA) * diag
                    d_sum = d_sum + damp
            damp = jnp.where(lane < 32, 0.125 * take(pair_lanes(d_sum), even), 0.0)
            c2[4 * n + blk, 0] = 0.0625 * (OMEGA * o2 / (0.375 + damp))
            return carry

        lax.fori_loop(0, 4, block_step, 0)


def levels_solve(c1, g1, o1, c2, cb1, w_a, w_b, cb2, u_a, u_b):
    lane = lane_index()
    even, halved = (2 * lane) % NZ, lane // 2
    sweep(cb1, w_a, c1, cb1, 2, 38, 4, 2, False)

    def coarse(m):
        total = 0.0
        for dx in range(2):
            for tile in residue_row(w_a, c1, cb1, g1, 2 * m + dx, 2 * m + dx, 2, False):
                total = total + tile
        b2 = 0.125 * take(pair_lanes(total), even)
        cb2[m, 0] = 16.0 * c2[m, 0] * b2

    rows_loop(2, 18, 4, coarse)
    sweep(cb2, u_a, c2, cb2, 3, 17, 7, 1, False)
    sweep(u_a, u_b, c2, cb2, 4, 16, 6, 1, False)
    sweep(u_b, u_a, c2, cb2, 5, 15, 5, 1, False)

    def correct(m):
        step = take(u_a[m, 0], halved) * o1[m]
        for dx in range(2):
            for q in range(2):
                w_a[2 * m + dx, q] = w_a[2 * m + dx, q] + step

    rows_loop(5, 15, 2, correct)
    sweep(w_a, w_b, c1, cb1, 11, 29, 6, 2, False)
    sweep(w_b, w_a, c1, cb1, 13, 27, 7, 2, False)


def correct_fine(v_in, v_out, w, blocks, low, high):
    halved = lane_index() // 2

    def body(a):
        opened = blocks[(a - 12) // 2]
        for q in range(2):
            step = take(w[a, q], halved) * opened
            for dx in range(2):
                for k in range(2):
                    t = 2 * a - 25 + dx
                    v_out[t, 2 * q + k] = v_in[t, 2 * q + k] + step

    rows_loop(low, high, 2, body)


def middle_kernel(p0, p1, p2, p3, p4, cc, cb, gg, v2, blocks, v_out, c1, g1, o1, c2, send,
                  cb1, w_a, w_b, cb2, u_a, u_b, v_a, v_b):
    levels_setup((p0, p1, p2, p3, p4), c1, g1, o1, c2, cb1)
    levels_solve(c1, g1, o1, c2, cb1, w_a, w_b, cb2, u_a, u_b)
    correct_fine(v2, v_a, w_a, blocks, 13, 27)
    sweep(v_a, v_b, cc, cb, 2, 28, 2, 4, True)
    sweep(v_b, v_a, cc, cb, 3, 27, 4, 4, True)
    sweep(v_a, v_b, cc, cb, 4, 26, 2, 4, True)
    sweep(v_b, v_out, cc, cb, 5, 25, 4, 4, True)
    lane = lane_index()
    even = (2 * lane) % NZ

    def coarse(k):
        b_sum = [0.0, 0.0]
        for dx in range(2):
            for q, tile in enumerate(residue_row(v_out, cc, cb, gg, 7 + 2 * k + dx, 2 * k + dx, 4, True)):
                b_sum[q // 2] = b_sum[q // 2] + tile
        tiles = [take(pair_lanes(b_sum[q]), even) for q in range(2)]
        send[k] = 0.125 * jnp.where(lane < 64, tiles[0], tiles[1])

    rows_loop(0, 8, 2, coarse)


def last_kernel(slab, p0, p1, p2, p3, p4, cc, cb, v2, blocks, c1, g1, o1, c2, out,
                cb1, w_a, w_b, cb2, u_a, u_b, v_a, v_b, flat):
    lane = lane_index()
    for n, part in enumerate((p0, p1, p2, p3, p4)):
        for k in range(8):
            tile = part[k]
            a = 8 * n + k
            for q, cut in enumerate((tile, pltpu.roll(tile, 64, 1))):
                cb1[a, q] = 4.0 * c1[a, q] * jnp.where(lane < 64, cut, 0.0)
    levels_solve(c1, g1, o1, c2, cb1, w_a, w_b, cb2, u_a, u_b)
    correct_fine(v2, v_a, w_a, blocks, 15, 25)
    sweep(v_a, v_b, cc, cb, 6, 24, 3, 4, True)
    sweep(v_b, v_a, cc, cb, 7, 23, 4, 4, True)
    s_me = slab[0]
    for x in range(CX):
        for q in range(4):
            flat[pl.ds(x * 32 + q, 8, stride=4), :] = v_a[7 + x, q]
    for x in range(CX):
        out[x] = flat[pl.ds(pl.multiple_of(x * 32 + 8 * s_me, 8), 8), :]


def call(kernel, outs, scratch, operands, smem_first=False, cost=1000000):
    specs = [pl.BlockSpec(memory_space=pltpu.VMEM) for _ in operands]
    if smem_first:
        specs[0] = pl.BlockSpec(memory_space=pltpu.SMEM)
    shapes = [jax.ShapeDtypeStruct(shape, F32) for shape in outs]
    return pl.pallas_call(
        kernel,
        out_shape=shapes,
        in_specs=specs,
        out_specs=[pl.BlockSpec(memory_space=pltpu.VMEM) for _ in outs],
        scratch_shapes=[pltpu.VMEM(shape, kind) for shape, kind in scratch],
        compiler_params=pltpu.CompilerParams(vmem_limit_bytes=LIMIT),
        cost_estimate=pl.CostEstimate(flops=cost, bytes_accessed=cost, transcendentals=0),
    )(*operands)


def fetch(block, distance):
    count = lax.axis_size("box")
    return lax.ppermute(block, "box", [((i + distance) % count, i) for i in range(count)])


def shards(volume, drag, momentum, offsets, cell_index, destinations, rhs, wall):
    slab = lax.axis_index("slab").astype(I32).reshape(1)
    prev = fetch(jnp.concatenate([rhs[7:], wall[7:].astype(F32)], axis=0), -1)
    (outgoing,) = call(
        route_kernel,
        [(N_BOX, 8 * CAP)],
        [((24 * CAP, PART), BF16)],
        [volume.reshape(1, PART), drag.reshape(1, PART), momentum, offsets,
         cell_index.reshape(1, PART), destinations.reshape(1, PART)],
    )
    incoming = lax.all_to_all(outgoing, "box", split_axis=0, concat_axis=0, tiled=True)
    pay, craw = call(
        deposit_kernel,
        [(3 * XE + XE // 2, 8, NZ), (4, XE, 8, NZ)],
        [((13, CAP, NZ), F32), ((3, CAP, NZ), I32), ((XE, CAP, NZ), F32), ((768, SLOTS), BF16),
         ((NZ, SLOTS), BF16), ((768, NZ), F32)],
        [incoming, rhs, wall, prev],
    )
    slabs = lax.all_gather(pay, "slab")
    send, keep = call(
        slab_kernel,
        [(168, 8, NZ), (168, 8, NZ)],
        [((XE * 32, NZ), F32), ((XE * 32, NZ), F32), ((XE, 8, NZ), F32)],
        [slab, slabs, craw],
        smem_first=True,
    )
    got = fetch(send, 1)
    coupled, cc, cb, gg, v2, blocks, first = call(
        start_kernel,
        [(4, CX, 8, NZ), (T0, 4, 8, NZ), (T0, 4, 8, NZ), (CX, 4, 8, NZ), (T0, 4, 8, NZ), (8, 8, NZ), (20, 8, NZ)],
        [((T0, 4, 8, NZ), F32)],
        [keep, got],
    )
    parts = [fetch(first, -2), fetch(first, -1), first, fetch(first, 1), fetch(first, 2)]
    level_scratch = [
        ((T1, 2, 8, NZ), F32), ((T1, 2, 8, NZ), F32), ((T1, 2, 8, NZ), F32),
        ((T2, 1, 8, NZ), F32), ((T2, 1, 8, NZ), F32), ((T2, 1, 8, NZ), F32),
        ((T0, 4, 8, NZ), F32), ((T0, 4, 8, NZ), F32),
    ]
    v3, c1, g1, o1, c2, second = call(
        middle_kernel,
        [(T0, 4, 8, NZ), (T1, 2, 8, NZ), (T1, 2, 8, NZ), (T2, 8, NZ), (T2, 1, 8, NZ), (8, 8, NZ)],
        level_scratch,
        parts + [cc, cb, gg, v2, blocks],
    )
    parts = [fetch(second, -2), fetch(second, -1), second, fetch(second, 1), fetch(second, 2)]
    (pressure,) = call(
        last_kernel,
        [(CX, 8, NZ)],
        level_scratch + [((CX * 32, NZ), F32)],
        [slab] + parts + [cc, cb, v3, blocks, c1, g1, o1, c2],
        smem_first=True,
    )
    return coupled, pressure


def solution(mesh):
    in_specs = (
        P(("box", "slab")),
        P(("box", "slab")),
        P(None, ("box", "slab")),
        P(None, ("box", "slab")),
        P(("box", "slab")),
        P(("box", "slab"), None),
        P("box", "slab", None),
        P("box", "slab", None),
    )
    out_specs = (P(None, "box", "slab", None), P("box", "slab", None))
    return jax.shard_map(shards, mesh=mesh, in_specs=in_specs, out_specs=out_specs, check_vma=False)
```

```python
import jax
import jax.numpy as jnp
from jax import lax
from jax.experimental import pallas as pl
from jax.experimental.pallas import tpu as pltpu
from jax.sharding import PartitionSpec as P

F32 = jnp.float32
BF16 = jnp.bfloat16
I32 = jnp.int32

CX, CY, NZ = 16, 8, 128
PART = 2048
N_BOX = 128
CAP = 32
SLOTS = N_BOX * CAP
XE = CX + 2
OMEGA = 0.8

T0, T1, T2 = 30, 40, 20

CHUNKS = 4

LIMIT = 48 * 1024 * 1024

NT = (((1,), (1,)), ((), ()))


def tap_weights(frac):
    return (
        0.5 * (0.5 - frac) * (0.5 - frac),
        0.75 - frac * frac,
        0.5 * (0.5 + frac) * (0.5 + frac),
    )


def spread(index, at, taps):
    return jnp.where(
        index == at,
        taps[0],
        jnp.where(index == at + 1, taps[1], jnp.where(index == at + 2, taps[2], 0.0)),
    )


def route_kernel(vol_in, drag_in, mom_in, off_in, cell_in, dest_in, out, vol, drag, mom, off, cell, dest, picked, ordered, sems):
    pairs = ((dest_in, dest), (vol_in, vol), (drag_in, drag), (mom_in, mom), (off_in, off), (cell_in, cell))
    copies = [pltpu.make_async_copy(a, b, sems.at[k]) for k, (a, b) in enumerate(pairs)]
    for copy in copies:
        copy.start()
    for copy in copies:
        copy.wait()
    target = dest[...]
    hot = lax.broadcasted_iota(I32, (N_BOX, PART), 0) == target
    hot_f = jnp.where(hot, 1.0, 0.0)
    hot_b = hot_f.astype(BF16)
    width = 256
    above = lax.broadcasted_iota(I32, (width, width), 0) < lax.broadcasted_iota(I32, (width, width), 1)
    before = jnp.where(above, 1.0, 0.0).astype(BF16)
    carry = jnp.zeros((N_BOX, 1), F32)
    places = []
    for k in range(PART // width):
        cut = slice(k * width, (k + 1) * width)
        rank = jnp.dot(hot_b[:, cut], before, preferred_element_type=F32) + carry
        places.append(jnp.sum(rank * hot_f[:, cut], axis=0, keepdims=True))
        carry = carry + jnp.sum(hot_f[:, cut], axis=1, keepdims=True)
    place = jnp.concatenate(places, axis=1).astype(I32)
    at_place = lax.broadcasted_iota(I32, (CAP, PART), 0) == place
    fields = [vol[...], drag[...], mom[0:1, :], mom[1:2, :]]
    fields += [off[0:1, :], off[1:2, :], off[2:3, :], cell[...].astype(F32)]
    for f, left in enumerate(fields):
        for part in range(3):
            rounded = left.astype(BF16).astype(F32)
            row = (part * 8 + f) * CAP
            picked[row : row + CAP, :] = jnp.where(at_place, rounded, 0.0).astype(BF16)
            left = left - rounded
    sums = lax.dot_general(picked[...], hot_b, NT, preferred_element_type=F32)
    half = 8 * CAP
    sums = sums[:half] + sums[half : 2 * half] + sums[2 * half :]
    ordered[...] = sums.T
    for r in range(N_BOX):
        out[r] = ordered[r : r + 1, :]


def deposit_kernel(recv, rhs, wall, prev, pay, craw, par, cells, xs, acc, *mats):
    amats, vmats = mats[:CHUNKS], mats[CHUNKS:]
    fields = recv[...].T
    for c in range(4):
        par[c] = fields[c * CAP : (c + 1) * CAP]
    cell = fields[7 * CAP :].astype(I32)
    x_cell = cell // (NZ * CY)
    cells[0] = x_cell
    cells[1] = (cell // NZ) % CY
    cells[2] = cell % NZ
    for d in range(3):
        for k, tap in enumerate(tap_weights(fields[(4 + d) * CAP : (5 + d) * CAP])):
            par[4 + 3 * d + k] = tap
    for x in range(XE):
        xs[x] = spread(x, x_cell, (par[4], par[5], par[6]))
    sub24 = lax.broadcasted_iota(I32, (24, NZ), 0)
    sub8 = lax.broadcasted_iota(I32, (8, NZ), 0)
    sub128 = lax.broadcasted_iota(I32, (NZ, NZ), 0)

    def one(w, amat, vmat, at):
        def row(k):
            return par[k, w : w + 1, :]

        lanes = slice(at, at + NZ)
        vals = [row(c) for c in range(4)]
        wx = [row(4 + k) for k in range(3)]
        wy = [row(7 + k) for k in range(3)]
        wz = [row(10 + k) for k in range(3)]
        xc, yc, zc = [cells[d, w : w + 1, :] for d in range(3)]
        y_tile = spread(sub8, yc - 1, wy)
        low = jnp.where(yc == 0, wy[0], 0.0)
        high = jnp.where(yc == CY - 1, wy[2], 0.0)
        x_tile = spread(sub24, xc, wx)
        edge = jnp.concatenate([x_tile * low, x_tile * high], axis=0)
        for c in range(4):
            amat[576 + 48 * c : 576 + 48 * (c + 1), lanes] = (vals[c] * edge).astype(BF16)
        for pair in range(XE // 2):
            plane = jnp.concatenate([xs[2 * pair + k, w : w + 1, :] * y_tile for k in range(2)], axis=0)
            for c in range(4):
                r = 144 * c + 16 * pair
                amat[r : r + 16, lanes] = (vals[c] * plane).astype(BF16)
        vmat[:, lanes] = spread(sub128, zc - 1, wz).astype(BF16)

    each = CAP // CHUNKS
    for n in range(CHUNKS):
        for k in range(each):
            one(n * each + k, amats[n], vmats[n], k * NZ)
        part = lax.dot_general(amats[n][...], vmats[n][...], NT, preferred_element_type=F32)
        acc[...] = part if n == 0 else acc[...] + part
    for x in range(XE):
        c = [acc[144 * k + 8 * x : 144 * k + 8 * x + 8, :] for k in range(4)]
        for k in range(4):
            craw[k, x] = c[k]
        if x < 9:
            right, opened = prev[x], prev[9 + x]
        else:
            right, opened = rhs[x - 9], wall[x - 9].astype(F32)
        whole = right - c[0] * right if x < CX else -(c[0] * right)
        pay[x] = opened * (whole + c[2] + c[3])
        pay[XE + x] = c[1]
        pay[2 * XE + x] = acc[pl.ds(576 + x, 8, stride=24), :]
        extra = jnp.concatenate([right[0:1], right[7:8], opened[0:1], opened[4:5]], axis=0)
        pay[3 * XE + x // 2, (x % 2) * 4 : (x % 2) * 4 + 4, :] = extra


def slab_kernel(slab, got, craw, send, keep, ssum, dsum, osum):
    s_me = slab[0]
    sub = lax.broadcasted_iota(I32, (8, NZ), 0)
    first, last = sub == 0, sub == 7

    def edges(tile, to_first, to_last):
        return tile + jnp.where(first, to_first, 0.0) + jnp.where(last, to_last, 0.0)

    for x in range(XE):
        g_row = (x % 2) * 4
        halos = [got[s, 2 * XE + x] for s in range(4)]
        for s in range(4):
            below, above = halos[(s + 3) % 4], halos[(s + 1) % 4]
            extra = got[s, 3 * XE + x // 2]
            rhs_f, rhs_l = extra[g_row : g_row + 1], extra[g_row + 1 : g_row + 2]
            o_f, o_l = extra[g_row + 2 : g_row + 3], extra[g_row + 3 : g_row + 4]
            from_below = o_f * (below[5:6] + below[7:8] - below[1:2] * rhs_f)
            from_above = o_l * (above[4:5] + above[6:7] - above[0:1] * rhs_l)
            at = x * 32 + s * 8
            ssum[at : at + 8, :] = edges(got[s, x], from_below, from_above)
            dsum[at : at + 8, :] = edges(got[s, XE + x], below[3:4], above[2:3])
            osum[x, 2 * s : 2 * s + 2, :] = extra[g_row + 2 : g_row + 4]
        below = got[(s_me + 3) % 4, 2 * XE + x]
        above = got[(s_me + 1) % 4, 2 * XE + x]
        for c in range(4):
            tile = edges(craw[c, x], below[2 * c + 1 : 2 * c + 2], above[2 * c : 2 * c + 1])
            if x < 9:
                send[128 + 9 * c + x] = tile
            else:
                keep[128 + 9 * c + x - 9] = tile
        for q in range(4):
            s_tile = ssum[pl.ds(x * 32 + q, 8, stride=4), :]
            d_tile = dsum[pl.ds(x * 32 + q, 8, stride=4), :]
            if x < CX:
                send[4 * x + q] = s_tile
                send[64 + 4 * x + q] = d_tile
            if x >= 2:
                keep[4 * (x - 2) + q] = s_tile
                keep[64 + 4 * (x - 2) + q] = d_tile
    for k, x in enumerate((1, 5, 9, 13)):
        send[164 + k] = osum[x]
    for k, x in enumerate((2, 5, 9, 13)):
        keep[164 + k] = osum[x]


def lane_index():
    return lax.broadcasted_iota(I32, (8, NZ), 1)


def take(tile, index):
    return jnp.take_along_axis(tile, index, axis=1)


def pair_lanes(tile):
    return tile + pltpu.roll(tile, NZ - 1, 1)


def fine_sums(ref, t):
    lane = lane_index()
    cur = [ref[t, q] for q in range(4)]
    sums = []
    for q in range(4):
        after = cur[q + 1] if q < 3 else pltpu.roll(cur[0], 7, 0)
        before = cur[q - 1] if q else pltpu.roll(cur[3], 1, 0)
        left = jnp.where(lane == 0, 0.0, pltpu.roll(cur[q], 1, 1))
        right = jnp.where(lane == NZ - 1, 0.0, pltpu.roll(cur[q], NZ - 1, 1))
        sums.append((ref[t - 1, q] + ref[t + 1, q]) + (after + before) + (left + right))
    return cur, sums


def fine_sweep(src, dst, coef, base, low, high):
    for t in range(low, high):
        cur, sums = fine_sums(src, t)
        for q in range(4):
            dst[t, q] = (1.0 - OMEGA) * cur[q] + base[t, q] + coef[t, q] * sums[q]


def fine_residue(src, coef, base, weight, k):
    total = [0.0, 0.0]
    for dx in range(2):
        t = 7 + 2 * k + dx
        cur, sums = fine_sums(src, t)
        for q in range(4):
            tile = weight[2 * k + dx, q] * (base[t, q] + coef[t, q] * sums[q] - OMEGA * cur[q])
            total[q // 2] = total[q // 2] + tile
    return 0.125 * pack(total)


def pack(total):
    lane = lane_index()
    even = (2 * lane) % NZ
    return jnp.where(lane < 64, take(pair_lanes(total[0]), even), take(pair_lanes(total[1]), even))


def fine_correct(v_in, v_out, w, coef, low, high):
    lane = lane_index()
    for a in range(low, high):
        for half in range(2):
            step = take(w[a], lane // 2 + 64 * half)
            for dx in range(2):
                t = 2 * a - 25 + dx
                for q in (2 * half, 2 * half + 1):
                    v_out[t, q] = v_in[t, q] + jnp.where(coef[t, q] > 0.0, step, 0.0)


def mid_sums(ref, a):
    lane = lane_index()
    cur = ref[a]
    turned = pltpu.roll(cur, 64, 1)
    beside = turned + jnp.where(lane < 64, pltpu.roll(turned, 1, 0), pltpu.roll(turned, 7, 0))
    left = jnp.where(lane % 64 == 0, 0.0, pltpu.roll(cur, 1, 1))
    right = jnp.where(lane % 64 == 63, 0.0, pltpu.roll(cur, NZ - 1, 1))
    return cur, (ref[a - 1] + ref[a + 1]) + beside + (left + right)


def mid_sweep(src, dst, coef, base, low, high):
    for a in range(low, high):
        cur, total = mid_sums(src, a)
        dst[a] = (1.0 - OMEGA) * cur + base[a] + coef[a] * total


def low_sweep(src, dst, coef, base, low, high):
    for m in range(low, high):
        cur = src[m]
        total = (src[m - 1] + src[m + 1]) + (pltpu.roll(cur, 1, 0) + pltpu.roll(cur, 7, 0))
        total = total + (pltpu.roll(cur, 1, 1) + pltpu.roll(cur, NZ - 1, 1))
        dst[m] = (1.0 - OMEGA) * cur + base[m] + coef[m] * total


def levels_solve(c1, g1, c2, cb1, w_a, w_b, cb2, u_a, u_b):
    lane = lane_index()
    even = (2 * lane) % NZ
    mid_sweep(cb1, w_a, c1, cb1, 3, 37)
    for m in range(2, 18):
        total = 0.0
        for a in (2 * m, 2 * m + 1):
            cur, beside = mid_sums(w_a, a)
            total = total + g1[a] * (cb1[a] + c1[a] * beside - OMEGA * cur)
        total = total + pltpu.roll(total, 64, 1)
        cb2[m] = 2.0 * c2[m] * take(pair_lanes(total), even)
    low_sweep(cb2, u_a, c2, cb2, 3, 17)
    low_sweep(u_a, u_b, c2, cb2, 4, 16)
    low_sweep(u_b, u_a, c2, cb2, 5, 15)
    for m in range(5, 15):
        step = take(u_a[m], (lane % 64) // 2)
        for a in (2 * m, 2 * m + 1):
            w_a[a] = w_a[a] + jnp.where(c1[a] > 0.0, step, 0.0)
    mid_sweep(w_a, w_b, c1, cb1, 12, 28)
    mid_sweep(w_b, w_a, c1, cb1, 13, 27)


def coupled_kernel(keep, got, coupled):
    for c in range(4):
        for x in range(CX):
            if x < 7:
                tile = keep[128 + 9 * c + x]
            elif x < 9:
                tile = keep[128 + 9 * c + x] + got[128 + 9 * c + x - 7]
            else:
                tile = got[128 + 9 * c + x - 7]
            coupled[c, x] = tile


def start_kernel(keep, got, cc, cb, gg, v2, send, dk):
    for t in range(T0):
        block = (t + 1) // 4
        opened = keep[164 + block] if block < 4 else got[160 + block]
        for q in range(4):
            at = 4 * (t - 14) + q
            if t < 14:
                s_tile, d_tile = keep[4 * t + q], keep[64 + 4 * t + q]
            elif t < 16:
                s_tile, d_tile = keep[4 * t + q] + got[at], keep[64 + 4 * t + q] + got[64 + at]
            else:
                s_tile, d_tile = got[at], got[64 + at]
            diag = 6.0 + d_tile
            coef = OMEGA * opened / diag
            cc[t, q] = coef
            cb[t, q] = coef * s_tile
            if 7 <= t < 23:
                dk[t - 7, q] = d_tile
                gg[t - 7, q] = (1.0 / OMEGA) * diag
    fine_sweep(cb, v2, cc, cb, 1, 29)
    lane = lane_index()
    even = (2 * lane) % NZ
    for k in range(8):
        block = 2 + k // 2
        opened = take(keep[164 + block] if block < 4 else got[160 + block], even)
        d_sum = [0.0, 0.0]
        for dx in range(2):
            for q in range(4):
                d_sum[q // 2] = d_sum[q // 2] + dk[2 * k + dx, q]
        damp = 0.125 * pack(d_sum)
        diag = 1.5 + damp
        coef = OMEGA * opened / diag
        send[k] = coef * fine_residue(v2, cc, cb, gg, k)
        send[8 + k] = 0.25 * coef
        send[16 + k] = (1.0 / OMEGA) * diag
        if k % 2 == 0:
            above = damp
        else:
            total = above + damp
            total = total + pltpu.roll(total, 64, 1)
            low = 0.375 + 0.125 * take(pair_lanes(total), even)
            send[24 + k // 2] = jnp.where(lane < 32, 0.0625 * (OMEGA * take(opened, even) / low), 0.0)


def window(core, far_low, second, own, first, far_high):
    even = core == 0

    def part(n, k):
        if n == 1:
            return jnp.where(even, second[k], first[k])
        if n == 3:
            return jnp.where(even, first[k], second[k])
        return (far_low, None, own, None, far_high)[n][k]

    return part


def middle_kernel(place, far_low, second, own, first, far_high, cc, cb, gg, v2, v_out, c1, g1, c2, send,
                  cb1, w_a, w_b, cb2, u_a, u_b, v_a, v_b):
    part = window(place[1], far_low, second, own, first, far_high)
    for n in range(5):
        for k in range(8):
            cb1[8 * n + k] = part(n, k)
            c1[8 * n + k] = part(n, 8 + k)
            g1[8 * n + k] = part(n, 16 + k)
        for k in range(4):
            c2[4 * n + k] = part(n, 24 + k)
    levels_solve(c1, g1, c2, cb1, w_a, w_b, cb2, u_a, u_b)
    fine_correct(v2, v_a, w_a, cc, 13, 27)
    fine_sweep(v_a, v_b, cc, cb, 2, 28)
    fine_sweep(v_b, v_a, cc, cb, 3, 27)
    fine_sweep(v_a, v_b, cc, cb, 4, 26)
    fine_sweep(v_b, v_out, cc, cb, 5, 25)
    for k in range(8):
        send[k] = 4.0 * c1[16 + k] * fine_residue(v_out, cc, cb, gg, k)


def last_kernel(place, far_low, second, own, first, far_high, cc, cb, v2, c1, g1, c2, out,
                cb1, w_a, w_b, cb2, u_a, u_b, v_a, v_b, flat):
    part = window(place[1], far_low, second, own, first, far_high)
    for n in range(5):
        for k in range(8):
            cb1[8 * n + k] = part(n, k)
    levels_solve(c1, g1, c2, cb1, w_a, w_b, cb2, u_a, u_b)
    fine_correct(v2, v_a, w_a, cc, 15, 25)
    fine_sweep(v_a, v_b, cc, cb, 6, 24)
    fine_sweep(v_b, v_a, cc, cb, 7, 23)
    for x in range(CX):
        for q in range(4):
            flat[pl.ds(x * 32 + q, 8, stride=4), :] = v_a[7 + x, q]
    for x in range(CX):
        out[x] = flat[pl.ds(pl.multiple_of(x * 32 + 8 * place[0], 8), 8), :]


def call(kernel, outs, scratch, operands, smem_first=False, in_hbm=False, cost=1000000, limit=LIMIT):
    kind = pltpu.HBM if in_hbm else pltpu.VMEM
    specs = [pl.BlockSpec(memory_space=kind) for _ in operands]
    if smem_first:
        specs[0] = pl.BlockSpec(memory_space=pltpu.SMEM)
    shapes = [jax.ShapeDtypeStruct(shape, F32) for shape in outs]
    return pl.pallas_call(
        kernel,
        out_shape=shapes,
        in_specs=specs,
        out_specs=[pl.BlockSpec(memory_space=pltpu.VMEM) for _ in outs],
        scratch_shapes=[pltpu.VMEM(*piece) if isinstance(piece, tuple) else piece for piece in scratch],
        compiler_params=pltpu.CompilerParams(vmem_limit_bytes=limit),
        cost_estimate=pl.CostEstimate(flops=cost, bytes_accessed=cost, transcendentals=0),
    )(*operands)


def fetch(block, distance):
    count = lax.axis_size("box")
    return lax.ppermute(block, "box", [((i + distance) % count, i) for i in range(count)])


def swap(block):
    return lax.ppermute(block, "box", [(i ^ 1, i) for i in range(lax.axis_size("box"))])


def around(block, core):
    far_low, far_high = fetch(block, -2), fetch(block, 2)
    first = swap(block)
    second = swap(jnp.where(core == 0, far_high, far_low))
    return [far_low, second, block, first, far_high]


def shards(volume, drag, momentum, offsets, cell_index, destinations, rhs, wall):
    core = lax.axis_index("box").astype(I32) % 2
    place = jnp.stack([lax.axis_index("slab").astype(I32), core])
    prev = fetch(jnp.concatenate([rhs[7:], wall[7:].astype(F32)], axis=0), -1)
    one = (1, PART)
    (outgoing,) = call(
        route_kernel,
        [(N_BOX, 1, 8 * CAP)],
        [(one, F32), (one, F32), ((2, PART), F32), ((3, PART), F32), (one, I32), (one, I32),
         ((24 * CAP, PART), BF16), ((N_BOX, 8 * CAP), F32), pltpu.SemaphoreType.DMA((6,))],
        [volume.reshape(one), drag.reshape(one), momentum, offsets, cell_index.reshape(one), destinations.reshape(one)],
        in_hbm=True,
        limit=62 * 1024 * 1024,
    )
    incoming = lax.all_to_all(outgoing, "box", split_axis=0, concat_axis=0, tiled=True)
    pay, craw = call(
        deposit_kernel,
        [(3 * XE + XE // 2, 8, NZ), (4, XE, 8, NZ)],
        [((13, CAP, NZ), F32), ((3, CAP, NZ), I32), ((XE, CAP, NZ), F32), ((768, NZ), F32)]
        + [((768, SLOTS // CHUNKS), BF16)] * CHUNKS + [((NZ, SLOTS // CHUNKS), BF16)] * CHUNKS,
        [incoming.reshape(N_BOX, 8 * CAP), rhs, wall, prev],
    )
    slabs = lax.all_gather(pay, "slab")
    send, keep = call(
        slab_kernel,
        [(168, 8, NZ), (168, 8, NZ)],
        [((XE * 32, NZ), F32), ((XE * 32, NZ), F32), ((XE, 8, NZ), F32)],
        [place, slabs, craw],
        smem_first=True,
    )
    got = fetch(send, 1)
    fine, mid, low = (T0, 4, 8, NZ), (T1, 8, NZ), (T2, 8, NZ)
    cc, cb, gg, v2, first = call(
        start_kernel, [fine, fine, (CX, 4, 8, NZ), fine, (28, 8, NZ)], [((CX, 4, 8, NZ), F32)], [keep, got]
    )
    (coupled,) = call(coupled_kernel, [(4, CX, 8, NZ)], [], [keep, got])
    scratch = [(mid, F32), (mid, F32), (mid, F32), (low, F32), (low, F32), (low, F32), (fine, F32), (fine, F32)]
    v3, c1, g1, c2, second = call(
        middle_kernel,
        [fine, mid, mid, low, (8, 8, NZ)],
        scratch,
        [place] + around(first, core) + [cc, cb, gg, v2],
        smem_first=True,
    )
    (pressure,) = call(
        last_kernel,
        [(CX, 8, NZ)],
        scratch + [((CX * 32, NZ), F32)],
        [place] + around(second, core) + [cc, cb, v3, c1, g1, c2],
        smem_first=True,
    )
    return coupled, pressure


def solution(mesh):
    in_specs = (
        P(("box", "slab")),
        P(("box", "slab")),
        P(None, ("box", "slab")),
        P(None, ("box", "slab")),
        P(("box", "slab")),
        P(("box", "slab"), None),
        P("box", "slab", None),
        P("box", "slab", None),
    )
    out_specs = (P(None, "box", "slab", None), P("box", "slab", None))
    return jax.shard_map(shards, mesh=mesh, in_specs=in_specs, out_specs=out_specs, check_vma=False)
```

```python
import jax
import jax.numpy as jnp
from jax import lax
from jax.experimental import pallas as pl
from jax.experimental.pallas import tpu as pltpu
from jax.sharding import PartitionSpec as P

F32 = jnp.float32
BF16 = jnp.bfloat16
I32 = jnp.int32

CX, CY, NZ = 16, 8, 128
PART = 2048
N_BOX = 128
CAP = 32
SLOTS = N_BOX * CAP
XE = CX + 2
OMEGA = 0.8

T0, T1, T2 = 30, 40, 20

OTHERS = (0, 2, 3)
CHUNKS = 8

LIMIT = 48 * 1024 * 1024

NT = (((1,), (1,)), ((), ()))


def tap_weights(frac):
    return (
        0.5 * (0.5 - frac) * (0.5 - frac),
        0.75 - frac * frac,
        0.5 * (0.5 + frac) * (0.5 + frac),
    )


def spread(index, at, taps):
    return jnp.where(
        index == at,
        taps[0],
        jnp.where(index == at + 1, taps[1], jnp.where(index == at + 2, taps[2], 0.0)),
    )


def route_kernel(vol_in, drag_in, mom_in, off_in, cell_in, dest_in, out, vol, drag, mom, off, cell, dest, picked, ordered, sems):
    pairs = ((dest_in, dest), (vol_in, vol), (drag_in, drag), (mom_in, mom), (off_in, off), (cell_in, cell))
    copies = [pltpu.make_async_copy(a, b, sems.at[k]) for k, (a, b) in enumerate(pairs)]
    for copy in copies:
        copy.start()
    copies[0].wait()
    target = dest[...]
    hot = lax.broadcasted_iota(I32, (N_BOX, PART), 0) == target
    hot_f = jnp.where(hot, 1.0, 0.0)
    hot_b = hot_f.astype(BF16)
    width = 256
    above = lax.broadcasted_iota(I32, (width, width), 0) < lax.broadcasted_iota(I32, (width, width), 1)
    before = jnp.where(above, 1.0, 0.0).astype(BF16)
    carry = jnp.zeros((N_BOX, 1), F32)
    places = []
    for k in range(PART // width):
        cut = slice(k * width, (k + 1) * width)
        rank = jnp.dot(hot_b[:, cut], before, preferred_element_type=F32) + carry
        places.append(jnp.sum(rank * hot_f[:, cut], axis=0, keepdims=True))
        carry = carry + jnp.sum(hot_f[:, cut], axis=1, keepdims=True)
    place = jnp.concatenate(places, axis=1).astype(I32)
    at_place = lax.broadcasted_iota(I32, (CAP, PART), 0) == place
    for copy in copies[1:]:
        copy.wait()
    fields = [vol[...], drag[...], mom[0:1, :], mom[1:2, :]]
    fields += [off[0:1, :], off[1:2, :], off[2:3, :], cell[...].astype(F32)]
    for f, left in enumerate(fields):
        for part in range(3):
            rounded = left.astype(BF16).astype(F32)
            row = (part * 8 + f) * CAP
            picked[row : row + CAP, :] = jnp.where(at_place, rounded, 0.0).astype(BF16)
            left = left - rounded
    sums = lax.dot_general(picked[...], hot_b, NT, preferred_element_type=F32)
    half = 8 * CAP
    sums = sums[:half] + sums[half : 2 * half] + sums[2 * half :]
    ordered[...] = sums.T
    for r in range(N_BOX):
        out[r] = ordered[r : r + 1, :]


def deposit_kernel(recv, rhs, wall, prev, pay, craw, par, cells, xs, acc, *mats):
    amats, vmats = mats[:CHUNKS], mats[CHUNKS:]
    fields = recv[...].T
    for c in range(4):
        par[c] = fields[c * CAP : (c + 1) * CAP]
    cell = fields[7 * CAP :].astype(I32)
    x_cell = cell // (NZ * CY)
    cells[0] = x_cell
    cells[1] = (cell // NZ) % CY
    cells[2] = cell % NZ
    for d in range(3):
        for k, tap in enumerate(tap_weights(fields[(4 + d) * CAP : (5 + d) * CAP])):
            par[4 + 3 * d + k] = tap
    for x in range(XE):
        xs[x] = spread(x, x_cell, (par[4], par[5], par[6]))
    sub24 = lax.broadcasted_iota(I32, (24, NZ), 0)
    sub8 = lax.broadcasted_iota(I32, (8, NZ), 0)
    sub128 = lax.broadcasted_iota(I32, (NZ, NZ), 0)

    def one(w, amat, vmat, at):
        def row(k):
            return par[k, w : w + 1, :]

        lanes = slice(at, at + NZ)
        vals = [row(c) for c in range(4)]
        wx = [row(4 + k) for k in range(3)]
        wy = [row(7 + k) for k in range(3)]
        wz = [row(10 + k) for k in range(3)]
        xc, yc, zc = [cells[d, w : w + 1, :] for d in range(3)]
        y_tile = spread(sub8, yc - 1, wy)
        low = jnp.where(yc == 0, wy[0], 0.0)
        high = jnp.where(yc == CY - 1, wy[2], 0.0)
        x_tile = spread(sub24, xc, wx)
        edge = jnp.concatenate([x_tile * low, x_tile * high], axis=0)
        for c in range(4):
            amat[576 + 48 * c : 576 + 48 * (c + 1), lanes] = (vals[c] * edge).astype(BF16)
        for pair in range(XE // 2):
            plane = jnp.concatenate([xs[2 * pair + k, w : w + 1, :] * y_tile for k in range(2)], axis=0)
            for c in range(4):
                r = 144 * c + 16 * pair
                amat[r : r + 16, lanes] = (vals[c] * plane).astype(BF16)
        vmat[:, lanes] = spread(sub128, zc - 1, wz).astype(BF16)

    each = CAP // CHUNKS
    for n in range(CHUNKS):
        for k in range(each):
            one(n * each + k, amats[n], vmats[n], k * NZ)
        part = lax.dot_general(amats[n][...], vmats[n][...], NT, preferred_element_type=F32)
        acc[...] = part if n == 0 else acc[...] + part
    for x in range(XE):
        c = [acc[144 * k + 8 * x : 144 * k + 8 * x + 8, :] for k in range(4)]
        for k, channel in enumerate(OTHERS):
            craw[k, x] = c[channel]
        if x < 9:
            right, opened = prev[x], prev[9 + x]
        else:
            right, opened = rhs[x - 9], wall[x - 9].astype(F32)
        whole = right - c[0] * right if x < CX else -(c[0] * right)
        pay[x] = opened * (whole + c[2] + c[3])
        pay[XE + x] = c[1]
        pay[2 * XE + x] = acc[pl.ds(576 + x, 8, stride=24), :]
        extra = jnp.concatenate([right[0:1], right[7:8], opened[0:1], opened[4:5]], axis=0)
        pay[3 * XE + x // 2, (x % 2) * 4 : (x % 2) * 4 + 4, :] = extra


def slab_kernel(slab, got, craw, send, keep, ssum, dsum, osum):
    s_me = slab[0]
    sub = lax.broadcasted_iota(I32, (8, NZ), 0)
    first, last = sub == 0, sub == 7

    def edges(tile, to_first, to_last):
        return tile + jnp.where(first, to_first, 0.0) + jnp.where(last, to_last, 0.0)

    for x in range(XE):
        g_row = (x % 2) * 4
        halos = [got[s, 2 * XE + x] for s in range(4)]
        for s in range(4):
            below, above = halos[(s + 3) % 4], halos[(s + 1) % 4]
            extra = got[s, 3 * XE + x // 2]
            rhs_f, rhs_l = extra[g_row : g_row + 1], extra[g_row + 1 : g_row + 2]
            o_f, o_l = extra[g_row + 2 : g_row + 3], extra[g_row + 3 : g_row + 4]
            from_below = o_f * (below[5:6] + below[7:8] - below[1:2] * rhs_f)
            from_above = o_l * (above[4:5] + above[6:7] - above[0:1] * rhs_l)
            at = x * 32 + s * 8
            ssum[at : at + 8, :] = edges(got[s, x], from_below, from_above)
            dsum[at : at + 8, :] = edges(got[s, XE + x], below[3:4], above[2:3])
            osum[x, 2 * s : 2 * s + 2, :] = extra[g_row + 2 : g_row + 4]
        below = got[(s_me + 3) % 4, 2 * XE + x]
        above = got[(s_me + 1) % 4, 2 * XE + x]
        for k, c in enumerate(OTHERS):
            tile = edges(craw[k, x], below[2 * c + 1 : 2 * c + 2], above[2 * c : 2 * c + 1])
            if x < 9:
                send[128 + 9 * k + x] = tile
            else:
                keep[128 + 9 * k + x - 9] = tile
        for q in range(4):
            s_tile = ssum[pl.ds(x * 32 + q, 8, stride=4), :]
            d_tile = dsum[pl.ds(x * 32 + q, 8, stride=4), :]
            if x < CX:
                send[4 * x + q] = s_tile
                send[64 + 4 * x + q] = d_tile
            if x >= 2:
                keep[4 * (x - 2) + q] = s_tile
                keep[64 + 4 * (x - 2) + q] = d_tile
    for k, x in enumerate((1, 5, 9, 13)):
        send[155 + k] = osum[x]
    for k, x in enumerate((2, 5, 9, 13)):
        keep[155 + k] = osum[x]


def lane_index():
    return lax.broadcasted_iota(I32, (8, NZ), 1)


def take(tile, index):
    return jnp.take_along_axis(tile, index, axis=1)


def pair_lanes(tile):
    return tile + pltpu.roll(tile, NZ - 1, 1)


def fine_sums(ref, t):
    lane = lane_index()
    cur = [ref[t, q] for q in range(4)]
    sums = []
    for q in range(4):
        after = cur[q + 1] if q < 3 else pltpu.roll(cur[0], 7, 0)
        before = cur[q - 1] if q else pltpu.roll(cur[3], 1, 0)
        left = jnp.where(lane == 0, 0.0, pltpu.roll(cur[q], 1, 1))
        right = jnp.where(lane == NZ - 1, 0.0, pltpu.roll(cur[q], NZ - 1, 1))
        sums.append((ref[t - 1, q] + ref[t + 1, q]) + (after + before) + (left + right))
    return cur, sums


def fine_sweep(src, dst, coef, base, low, high):
    for t in range(low, high):
        cur, sums = fine_sums(src, t)
        for q in range(4):
            dst[t, q] = (1.0 - OMEGA) * cur[q] + base[t, q] + coef[t, q] * sums[q]


def fine_residue(src, coef, base, weight, k):
    total = [0.0, 0.0]
    for dx in range(2):
        t = 7 + 2 * k + dx
        cur, sums = fine_sums(src, t)
        for q in range(4):
            tile = weight[2 * k + dx, q] * (base[t, q] + coef[t, q] * sums[q] - OMEGA * cur[q])
            total[q // 2] = total[q // 2] + tile
    return 0.125 * pack(total)


def pack(total):
    lane = lane_index()
    even = (2 * lane) % NZ
    return jnp.where(lane < 64, take(pair_lanes(total[0]), even), take(pair_lanes(total[1]), even))


def fine_correct(v_in, v_out, w, coef, low, high):
    lane = lane_index()
    for a in range(low, high):
        for half in range(2):
            step = take(w[a], lane // 2 + 64 * half)
            for dx in range(2):
                t = 2 * a - 25 + dx
                for q in (2 * half, 2 * half + 1):
                    v_out[t, q] = v_in[t, q] + jnp.where(coef[t, q] > 0.0, step, 0.0)


def mid_sums(ref, a):
    lane = lane_index()
    cur = ref[a]
    turned = pltpu.roll(cur, 64, 1)
    beside = turned + jnp.where(lane < 64, pltpu.roll(turned, 1, 0), pltpu.roll(turned, 7, 0))
    left = jnp.where(lane % 64 == 0, 0.0, pltpu.roll(cur, 1, 1))
    right = jnp.where(lane % 64 == 63, 0.0, pltpu.roll(cur, NZ - 1, 1))
    return cur, (ref[a - 1] + ref[a + 1]) + beside + (left + right)


def mid_sweep(src, dst, coef, base, low, high):
    for a in range(low, high):
        cur, total = mid_sums(src, a)
        dst[a] = (1.0 - OMEGA) * cur + base[a] + coef[a] * total


def low_sweep(src, dst, coef, base, low, high):
    for m in range(low, high):
        cur = src[m]
        total = (src[m - 1] + src[m + 1]) + (pltpu.roll(cur, 1, 0) + pltpu.roll(cur, 7, 0))
        total = total + (pltpu.roll(cur, 1, 1) + pltpu.roll(cur, NZ - 1, 1))
        dst[m] = (1.0 - OMEGA) * cur + base[m] + coef[m] * total


def levels_solve(c1, g1, c2, cb1, w_a, w_b, cb2, u_a, u_b):
    lane = lane_index()
    even = (2 * lane) % NZ
    mid_sweep(cb1, w_a, c1, cb1, 3, 37)
    for m in range(2, 18):
        total = 0.0
        for a in (2 * m, 2 * m + 1):
            cur, beside = mid_sums(w_a, a)
            total = total + g1[a] * (cb1[a] + c1[a] * beside - OMEGA * cur)
        total = total + pltpu.roll(total, 64, 1)
        cb2[m] = 2.0 * c2[m] * take(pair_lanes(total), even)
    low_sweep(cb2, u_a, c2, cb2, 3, 17)
    low_sweep(u_a, u_b, c2, cb2, 4, 16)
    low_sweep(u_b, u_a, c2, cb2, 5, 15)
    for m in range(5, 15):
        step = take(u_a[m], (lane % 64) // 2)
        for a in (2 * m, 2 * m + 1):
            w_a[a] = w_a[a] + jnp.where(c1[a] > 0.0, step, 0.0)
    mid_sweep(w_a, w_b, c1, cb1, 12, 28)
    mid_sweep(w_b, w_a, c1, cb1, 13, 27)


def joined(keep, got, t, at):
    own, other = at + 4 * t, at + 4 * (t - 14)
    if t < 14:
        return keep[own]
    return keep[own] + got[other] if t < 16 else got[other]


def coupled_kernel(place, keep, got, coupled, flat):
    for k, c in enumerate(OTHERS):
        for x in range(CX):
            at = 128 + 9 * k + x
            if x < 7:
                tile = keep[at]
            elif x < 9:
                tile = keep[at] + got[at - 7]
            else:
                tile = got[at - 7]
            coupled[c, x] = tile
    for x in range(CX):
        for q in range(4):
            flat[pl.ds(x * 32 + q, 8, stride=4), :] = joined(keep, got, 7 + x, 64 + q)
    for x in range(CX):
        coupled[1, x] = flat[pl.ds(pl.multiple_of(x * 32 + 8 * place[0], 8), 8), :]


def start_kernel(keep, got, cc, cb, gg, v2, send, dk):
    for t in range(T0):
        block = (t + 1) // 4
        opened = keep[155 + block] if block < 4 else got[151 + block]
        for q in range(4):
            s_tile, d_tile = joined(keep, got, t, q), joined(keep, got, t, 64 + q)
            diag = 6.0 + d_tile
            coef = OMEGA * opened / diag
            cc[t, q] = coef
            cb[t, q] = coef * s_tile
            if 7 <= t < 23:
                dk[t - 7, q] = d_tile
                gg[t - 7, q] = (1.0 / OMEGA) * diag
    fine_sweep(cb, v2, cc, cb, 1, 29)
    lane = lane_index()
    even = (2 * lane) % NZ
    for k in range(8):
        block = 2 + k // 2
        opened = take(keep[155 + block] if block < 4 else got[151 + block], even)
        d_sum = [0.0, 0.0]
        for dx in range(2):
            for q in range(4):
                d_sum[q // 2] = d_sum[q // 2] + dk[2 * k + dx, q]
        damp = 0.125 * pack(d_sum)
        diag = 1.5 + damp
        coef = OMEGA * opened / diag
        send[k] = coef * fine_residue(v2, cc, cb, gg, k)
        send[8 + k] = 0.25 * coef
        send[16 + k] = (1.0 / OMEGA) * diag
        if k % 2 == 0:
            above = damp
        else:
            total = above + damp
            total = total + pltpu.roll(total, 64, 1)
            low = 0.375 + 0.125 * take(pair_lanes(total), even)
            send[24 + k // 2] = jnp.where(lane < 32, 0.0625 * (OMEGA * take(opened, even) / low), 0.0)


def window(core, far_low, second, own, first, far_high):
    even = core == 0

    def part(n, k):
        if n == 1:
            return jnp.where(even, second[k], first[k])
        if n == 3:
            return jnp.where(even, first[k], second[k])
        return (far_low, None, own, None, far_high)[n][k]

    return part


def middle_kernel(place, far_low, second, own, first, far_high, cc, cb, gg, v2, v_out, c1, g1, c2, send,
                  cb1, w_a, w_b, cb2, u_a, u_b, v_a, v_b):
    part = window(place[1], far_low, second, own, first, far_high)
    for n in range(5):
        for k in range(8):
            cb1[8 * n + k] = part(n, k)
            c1[8 * n + k] = part(n, 8 + k)
            g1[8 * n + k] = part(n, 16 + k)
        for k in range(4):
            c2[4 * n + k] = part(n, 24 + k)
    levels_solve(c1, g1, c2, cb1, w_a, w_b, cb2, u_a, u_b)
    fine_correct(v2, v_a, w_a, cc, 13, 27)
    fine_sweep(v_a, v_b, cc, cb, 2, 28)
    fine_sweep(v_b, v_a, cc, cb, 3, 27)
    fine_sweep(v_a, v_b, cc, cb, 4, 26)
    fine_sweep(v_b, v_out, cc, cb, 5, 25)
    for k in range(8):
        send[k] = 4.0 * c1[16 + k] * fine_residue(v_out, cc, cb, gg, k)


def last_kernel(place, far_low, second, own, first, far_high, cc, cb, v2, c1, g1, c2, out,
                cb1, w_a, w_b, cb2, u_a, u_b, v_a, v_b, flat):
    part = window(place[1], far_low, second, own, first, far_high)
    for n in range(5):
        for k in range(8):
            cb1[8 * n + k] = part(n, k)
    levels_solve(c1, g1, c2, cb1, w_a, w_b, cb2, u_a, u_b)
    fine_correct(v2, v_a, w_a, cc, 15, 25)
    fine_sweep(v_a, v_b, cc, cb, 6, 24)
    fine_sweep(v_b, v_a, cc, cb, 7, 23)
    for x in range(CX):
        for q in range(4):
            flat[pl.ds(x * 32 + q, 8, stride=4), :] = v_a[7 + x, q]
    for x in range(CX):
        out[x] = flat[pl.ds(pl.multiple_of(x * 32 + 8 * place[0], 8), 8), :]


def call(kernel, outs, scratch, operands, smem_first=False, in_hbm=False, cost=1000000, limit=LIMIT):
    kind = pltpu.HBM if in_hbm else pltpu.VMEM
    specs = [pl.BlockSpec(memory_space=kind) for _ in operands]
    if smem_first:
        specs[0] = pl.BlockSpec(memory_space=pltpu.SMEM)
    shapes = [jax.ShapeDtypeStruct(shape, F32) for shape in outs]
    return pl.pallas_call(
        kernel,
        out_shape=shapes,
        in_specs=specs,
        out_specs=[pl.BlockSpec(memory_space=pltpu.VMEM) for _ in outs],
        scratch_shapes=[pltpu.VMEM(*piece) if isinstance(piece, tuple) else piece for piece in scratch],
        compiler_params=pltpu.CompilerParams(vmem_limit_bytes=limit),
        cost_estimate=pl.CostEstimate(flops=cost, bytes_accessed=cost, transcendentals=0),
    )(*operands)


def fetch(block, distance):
    count = lax.axis_size("box")
    return lax.ppermute(block, "box", [((i + distance) % count, i) for i in range(count)])


def swap(block):
    return lax.ppermute(block, "box", [(i ^ 1, i) for i in range(lax.axis_size("box"))])


def around(block, core, beside=None):
    far_low, far_high = fetch(block, -2), fetch(block, 2)
    first = swap(block)
    onward = jnp.where(core == 0, far_high, far_low)
    if beside is not None:
        onward, beside = lax.optimization_barrier((onward, beside))
    return [far_low, swap(onward), block, first, far_high], beside


def shards(volume, drag, momentum, offsets, cell_index, destinations, rhs, wall):
    core = lax.axis_index("box").astype(I32) % 2
    place = jnp.stack([lax.axis_index("slab").astype(I32), core])
    prev = fetch(jnp.concatenate([rhs[7:], wall[7:].astype(F32)], axis=0), -1)
    one = (1, PART)
    (outgoing,) = call(
        route_kernel,
        [(N_BOX, 1, 8 * CAP)],
        [(one, F32), (one, F32), ((2, PART), F32), ((3, PART), F32), (one, I32), (one, I32),
         ((24 * CAP, PART), BF16), ((N_BOX, 8 * CAP), F32), pltpu.SemaphoreType.DMA((6,))],
        [volume.reshape(one), drag.reshape(one), momentum, offsets, cell_index.reshape(one), destinations.reshape(one)],
        in_hbm=True,
        limit=62 * 1024 * 1024,
    )
    incoming = lax.all_to_all(outgoing, "box", split_axis=0, concat_axis=0, tiled=True)
    pay, craw = call(
        deposit_kernel,
        [(3 * XE + XE // 2, 8, NZ), (3, XE, 8, NZ)],
        [((13, CAP, NZ), F32), ((3, CAP, NZ), I32), ((XE, CAP, NZ), F32), ((768, NZ), F32)]
        + [((768, SLOTS // CHUNKS), BF16)] * CHUNKS + [((NZ, SLOTS // CHUNKS), BF16)] * CHUNKS,
        [incoming.reshape(N_BOX, 8 * CAP), rhs, wall, prev],
    )
    slabs = lax.all_gather(pay, "slab")
    send, keep = call(
        slab_kernel,
        [(159, 8, NZ), (159, 8, NZ)],
        [((XE * 32, NZ), F32), ((XE * 32, NZ), F32), ((XE, 8, NZ), F32)],
        [place, slabs, craw],
        smem_first=True,
    )
    got = fetch(send, 1)
    fine, mid, low = (T0, 4, 8, NZ), (T1, 8, NZ), (T2, 8, NZ)
    cc, cb, gg, v2, first = call(
        start_kernel, [fine, fine, (CX, 4, 8, NZ), fine, (28, 8, NZ)], [((CX, 4, 8, NZ), F32)], [keep, got]
    )
    (coupled,) = call(
        coupled_kernel,
        [(4, CX, 8, NZ)],
        [((CX * 32, NZ), F32)],
        [place, keep, got],
        smem_first=True,
    )
    scratch = [(mid, F32), (mid, F32), (mid, F32), (low, F32), (low, F32), (low, F32), (fine, F32), (fine, F32)]
    parts, coupled = around(first, core, coupled)
    v3, c1, g1, c2, second = call(
        middle_kernel,
        [fine, mid, mid, low, (8, 8, NZ)],
        scratch,
        [place] + parts + [cc, cb, gg, v2],
        smem_first=True,
    )
    parts, _ = around(second, core)
    (pressure,) = call(
        last_kernel,
        [(CX, 8, NZ)],
        scratch + [((CX * 32, NZ), F32)],
        [place] + parts + [cc, cb, v3, c1, g1, c2],
        smem_first=True,
    )
    return coupled, pressure


def solution(mesh):
    in_specs = (
        P(("box", "slab")),
        P(("box", "slab")),
        P(None, ("box", "slab")),
        P(None, ("box", "slab")),
        P(("box", "slab")),
        P(("box", "slab"), None),
        P("box", "slab", None),
        P("box", "slab", None),
    )
    out_specs = (P(None, "box", "slab", None), P("box", "slab", None))
    return jax.shard_map(shards, mesh=mesh, in_specs=in_specs, out_specs=out_specs, check_vma=False)
```

```python
import jax
import jax.numpy as jnp
from jax import lax
from jax.experimental import pallas as pl
from jax.experimental.pallas import tpu as pltpu
from jax.sharding import PartitionSpec as P

F32 = jnp.float32
BF16 = jnp.bfloat16
I32 = jnp.int32

CX, CY, NZ = 16, 8, 128
PART = 2048
N_BOX = 128
CAP = 32
SLOTS = N_BOX * CAP
XE = CX + 2
OMEGA = 0.8

T0, T1, T2 = 30, 40, 20

OTHERS = (0, 2, 3)
CHUNKS = 8

LIMIT = 48 * 1024 * 1024

NT = (((1,), (1,)), ((), ()))


def tap_weights(frac):
    return (
        0.5 * (0.5 - frac) * (0.5 - frac),
        0.75 - frac * frac,
        0.5 * (0.5 + frac) * (0.5 + frac),
    )


def spread(index, at, taps):
    return jnp.where(
        index == at,
        taps[0],
        jnp.where(index == at + 1, taps[1], jnp.where(index == at + 2, taps[2], 0.0)),
    )


def route_kernel(vol_in, drag_in, mom_in, off_in, cell_in, dest_in, out, vol, drag, mom, off, cell, dest, picked, ordered, sems):
    pairs = ((dest_in, dest), (vol_in, vol), (drag_in, drag), (mom_in, mom), (off_in, off), (cell_in, cell))
    copies = [pltpu.make_async_copy(a, b, sems.at[k]) for k, (a, b) in enumerate(pairs)]
    for copy in copies:
        copy.start()
    copies[0].wait()
    target = dest[...]
    hot = lax.broadcasted_iota(I32, (N_BOX, PART), 0) == target
    hot_f = jnp.where(hot, 1.0, 0.0)
    hot_b = hot_f.astype(BF16)
    width = 256
    above = lax.broadcasted_iota(I32, (width, width), 0) < lax.broadcasted_iota(I32, (width, width), 1)
    before = jnp.where(above, 1.0, 0.0).astype(BF16)
    carry = jnp.zeros((N_BOX, 1), F32)
    places = []
    for k in range(PART // width):
        cut = slice(k * width, (k + 1) * width)
        rank = jnp.dot(hot_b[:, cut], before, preferred_element_type=F32) + carry
        places.append(jnp.sum(rank * hot_f[:, cut], axis=0, keepdims=True))
        carry = carry + jnp.sum(hot_f[:, cut], axis=1, keepdims=True)
    place = jnp.concatenate(places, axis=1).astype(I32)
    at_place = lax.broadcasted_iota(I32, (CAP, PART), 0) == place
    for copy in copies[1:]:
        copy.wait()
    fields = [vol[...], drag[...], mom[0:1, :], mom[1:2, :]]
    fields += [off[0:1, :], off[1:2, :], off[2:3, :], cell[...].astype(F32)]
    for f, left in enumerate(fields):
        for part in range(3):
            rounded = left.astype(BF16).astype(F32)
            row = (part * 8 + f) * CAP
            picked[row : row + CAP, :] = jnp.where(at_place, rounded, 0.0).astype(BF16)
            left = left - rounded
    sums = lax.dot_general(picked[...], hot_b, NT, preferred_element_type=F32)
    half = 8 * CAP
    sums = sums[:half] + sums[half : 2 * half] + sums[2 * half :]
    ordered[...] = sums.T
    for r in range(N_BOX):
        out[r] = ordered[r : r + 1, :]


def deposit_kernel(recv, rhs, wall, prev, pay, craw, par, cells, xs, acc, *mats):
    amats, vmats = mats[:CHUNKS], mats[CHUNKS:]
    fields = recv[...].T
    for c in range(4):
        par[c] = fields[c * CAP : (c + 1) * CAP]
    cell = fields[7 * CAP :].astype(I32)
    x_cell = cell // (NZ * CY)
    cells[0] = x_cell
    cells[1] = (cell // NZ) % CY
    cells[2] = cell % NZ
    for d in range(3):
        for k, tap in enumerate(tap_weights(fields[(4 + d) * CAP : (5 + d) * CAP])):
            par[4 + 3 * d + k] = tap
    for x in range(XE):
        xs[x] = spread(x, x_cell, (par[4], par[5], par[6]))
    sub24 = lax.broadcasted_iota(I32, (24, NZ), 0)
    sub8 = lax.broadcasted_iota(I32, (8, NZ), 0)
    sub128 = lax.broadcasted_iota(I32, (NZ, NZ), 0)

    def one(w, amat, vmat, at):
        def row(k):
            return par[k, w : w + 1, :]

        lanes = slice(at, at + NZ)
        vals = [row(c) for c in range(4)]
        wx = [row(4 + k) for k in range(3)]
        wy = [row(7 + k) for k in range(3)]
        wz = [row(10 + k) for k in range(3)]
        xc, yc, zc = [cells[d, w : w + 1, :] for d in range(3)]
        y_tile = spread(sub8, yc - 1, wy)
        low = jnp.where(yc == 0, wy[0], 0.0)
        high = jnp.where(yc == CY - 1, wy[2], 0.0)
        x_tile = spread(sub24, xc, wx)
        edge = jnp.concatenate([x_tile * low, x_tile * high], axis=0)
        for c in range(4):
            amat[576 + 48 * c : 576 + 48 * (c + 1), lanes] = (vals[c] * edge).astype(BF16)
        for pair in range(XE // 2):
            plane = jnp.concatenate([xs[2 * pair + k, w : w + 1, :] * y_tile for k in range(2)], axis=0)
            for c in range(4):
                r = 144 * c + 16 * pair
                amat[r : r + 16, lanes] = (vals[c] * plane).astype(BF16)
        vmat[:, lanes] = spread(sub128, zc - 1, wz).astype(BF16)

    each = CAP // CHUNKS
    for n in range(CHUNKS):
        for k in range(each):
            one(n * each + k, amats[n], vmats[n], k * NZ)
        part = lax.dot_general(amats[n][...], vmats[n][...], NT, preferred_element_type=F32)
        acc[...] = part if n == 0 else acc[...] + part
    for x in range(XE):
        c = [acc[144 * k + 8 * x : 144 * k + 8 * x + 8, :] for k in range(4)]
        for k, channel in enumerate(OTHERS):
            craw[k, x] = c[channel]
        if x < 9:
            right, opened = prev[x], prev[9 + x]
        else:
            right, opened = rhs[x - 9], wall[x - 9].astype(F32)
        whole = right - c[0] * right if x < CX else -(c[0] * right)
        pay[x] = opened * (whole + c[2] + c[3])
        pay[XE + x] = c[1]
        pay[2 * XE + x] = acc[pl.ds(576 + x, 8, stride=24), :]
        extra = jnp.concatenate([right[0:1], right[7:8], opened[0:1], opened[4:5]], axis=0)
        pay[3 * XE + x // 2, (x % 2) * 4 : (x % 2) * 4 + 4, :] = extra


HEAD = 11
LATE = CX - HEAD


def slab_sums(got, rows, ssum, dsum):
    sub = lax.broadcasted_iota(I32, (8, NZ), 0)
    for n, x in enumerate(rows):
        g_row = (x % 2) * 4
        halos = [got[s, 2 * XE + x] for s in range(4)]
        for s in range(4):
            below, above = halos[(s + 3) % 4], halos[(s + 1) % 4]
            extra = got[s, 3 * XE + x // 2]
            rhs_f, rhs_l = extra[g_row : g_row + 1], extra[g_row + 1 : g_row + 2]
            o_f, o_l = extra[g_row + 2 : g_row + 3], extra[g_row + 3 : g_row + 4]
            from_below = o_f * (below[5:6] + below[7:8] - below[1:2] * rhs_f)
            from_above = o_l * (above[4:5] + above[6:7] - above[0:1] * rhs_l)
            at = n * 32 + s * 8
            ssum[at : at + 8, :] = edges(sub, got[s, x], from_below, from_above)
            dsum[at : at + 8, :] = edges(sub, got[s, XE + x], below[3:4], above[2:3])


def edges(sub, tile, to_first, to_last):
    return tile + jnp.where(sub == 0, to_first, 0.0) + jnp.where(sub == 7, to_last, 0.0)


def opened_block(got, x, out, at):
    g_row = (x % 2) * 4
    for s in range(4):
        out[at, 2 * s : 2 * s + 2, :] = got[s, 3 * XE + x // 2, g_row + 2 : g_row + 4, :]


def head_kernel(got, head, ssum, dsum):
    slab_sums(got, range(HEAD), ssum, dsum)
    for x in range(HEAD):
        for q in range(4):
            head[4 * x + q] = ssum[pl.ds(x * 32 + q, 8, stride=4), :]
            head[4 * (HEAD + x) + q] = dsum[pl.ds(x * 32 + q, 8, stride=4), :]
    for k, x in enumerate((1, 5, 9)):
        opened_block(got, x, head, 8 * HEAD + k)


def late_kernel(place, got, craw, late, keep, ssum, dsum):
    s_me = place[0]
    sub = lax.broadcasted_iota(I32, (8, NZ), 0)
    slab_sums(got, range(HEAD, XE), ssum, dsum)
    for n in range(XE - HEAD):
        for q in range(4):
            s_tile = ssum[pl.ds(n * 32 + q, 8, stride=4), :]
            d_tile = dsum[pl.ds(n * 32 + q, 8, stride=4), :]
            if n < LATE:
                late[4 * n + q] = s_tile
                late[4 * (LATE + n) + q] = d_tile
            else:
                keep[4 * (n - LATE) + q] = s_tile
                keep[4 * (n - LATE + 2) + q] = d_tile
    for x in range(XE):
        below = got[(s_me + 3) % 4, 2 * XE + x]
        above = got[(s_me + 1) % 4, 2 * XE + x]
        for k, c in enumerate(OTHERS):
            tile = edges(sub, craw[k, x], below[2 * c + 1 : 2 * c + 2], above[2 * c : 2 * c + 1])
            if x < 9:
                late[8 * LATE + 9 * k + x] = tile
            else:
                keep[16 + 9 * k + x - 9] = tile
    opened_block(got, 13, late, 8 * LATE + 27)


class Parts:
    def __init__(self, own_head, own_late, keep, next_head, next_late=None):
        self.own = (own_head, own_late, keep)
        self.next = (next_head, next_late)

    @staticmethod
    def tile(parts, x, kind, q):
        if x < HEAD:
            return parts[0][4 * (HEAD * kind + x) + q]
        if x < CX:
            return parts[1][4 * (LATE * kind + x - HEAD) + q]
        return parts[2][4 * (2 * kind + x - CX) + q]

    def joined(self, t, kind, q):
        if t < 14:
            return self.tile(self.own, t + 2, kind, q)
        other = self.tile(self.next, t - 14, kind, q)
        return other if t > 15 else other + self.tile(self.own, t + 2, kind, q)

    def opened(self, block):
        head, late = (self.own if block < 4 else self.next)[:2]
        k = block % 4
        return head[8 * HEAD + k] if k < 3 else late[8 * LATE + 27]

    def coefficient(self, t, q):
        diag = 6.0 + self.joined(t, 1, q)
        coef = OMEGA * self.opened((t + 1) // 4) / diag
        return coef, coef * self.joined(t, 0, q), diag


class Rows:
    def __init__(self, mid, rest, low, high):
        self.mid, self.rest, self.low, self.high = mid, rest, low, high

    def place(self, index):
        t, q = index
        if self.low <= t < self.high:
            return self.mid, (t, q)
        return self.rest, (t if t < self.low else t - self.high + self.low, q)

    def __getitem__(self, index):
        ref, at = self.place(index)
        return ref[at]

    def __setitem__(self, index, tile):
        ref, at = self.place(index)
        ref[at] = tile


def lane_index():
    return lax.broadcasted_iota(I32, (8, NZ), 1)


def take(tile, index):
    return jnp.take_along_axis(tile, index, axis=1)


def pair_lanes(tile):
    return tile + pltpu.roll(tile, NZ - 1, 1)


def fine_sums(ref, t):
    lane = lane_index()
    cur = [ref[t, q] for q in range(4)]
    sums = []
    for q in range(4):
        after = cur[q + 1] if q < 3 else pltpu.roll(cur[0], 7, 0)
        before = cur[q - 1] if q else pltpu.roll(cur[3], 1, 0)
        left = jnp.where(lane == 0, 0.0, pltpu.roll(cur[q], 1, 1))
        right = jnp.where(lane == NZ - 1, 0.0, pltpu.roll(cur[q], NZ - 1, 1))
        sums.append((ref[t - 1, q] + ref[t + 1, q]) + (after + before) + (left + right))
    return cur, sums


def fine_sweep(src, dst, coef, base, low, high):
    for t in range(low, high):
        cur, sums = fine_sums(src, t)
        for q in range(4):
            dst[t, q] = (1.0 - OMEGA) * cur[q] + base[t, q] + coef[t, q] * sums[q]


def fine_residue(src, coef, base, weight, k):
    total = [0.0, 0.0]
    for dx in range(2):
        t = 7 + 2 * k + dx
        cur, sums = fine_sums(src, t)
        for q in range(4):
            tile = weight[2 * k + dx, q] * (base[t, q] + coef[t, q] * sums[q] - OMEGA * cur[q])
            total[q // 2] = total[q // 2] + tile
    return 0.125 * pack(total)


def pack(total):
    lane = lane_index()
    even = (2 * lane) % NZ
    return jnp.where(lane < 64, take(pair_lanes(total[0]), even), take(pair_lanes(total[1]), even))


def fine_correct(v_in, v_out, w, coef, low, high):
    lane = lane_index()
    for a in range(low, high):
        for half in range(2):
            step = take(w[a], lane // 2 + 64 * half)
            for dx in range(2):
                t = 2 * a - 25 + dx
                for q in (2 * half, 2 * half + 1):
                    v_out[t, q] = v_in[t, q] + jnp.where(coef[t, q] > 0.0, step, 0.0)


def mid_sums(ref, a):
    lane = lane_index()
    cur = ref[a]
    turned = pltpu.roll(cur, 64, 1)
    beside = turned + jnp.where(lane < 64, pltpu.roll(turned, 1, 0), pltpu.roll(turned, 7, 0))
    left = jnp.where(lane % 64 == 0, 0.0, pltpu.roll(cur, 1, 1))
    right = jnp.where(lane % 64 == 63, 0.0, pltpu.roll(cur, NZ - 1, 1))
    return cur, (ref[a - 1] + ref[a + 1]) + beside + (left + right)


def mid_sweep(src, dst, coef, base, low, high):
    for a in range(low, high):
        cur, total = mid_sums(src, a)
        dst[a] = (1.0 - OMEGA) * cur + base[a] + coef[a] * total


def low_sweep(src, dst, coef, base, low, high):
    for m in range(low, high):
        cur = src[m]
        total = (src[m - 1] + src[m + 1]) + (pltpu.roll(cur, 1, 0) + pltpu.roll(cur, 7, 0))
        total = total + (pltpu.roll(cur, 1, 1) + pltpu.roll(cur, NZ - 1, 1))
        dst[m] = (1.0 - OMEGA) * cur + base[m] + coef[m] * total


def levels_solve(c1, g1, c2, cb1, w_a, w_b, cb2, u_a, u_b):
    lane = lane_index()
    even = (2 * lane) % NZ
    mid_sweep(cb1, w_a, c1, cb1, 3, 37)
    for m in range(2, 18):
        total = 0.0
        for a in (2 * m, 2 * m + 1):
            cur, beside = mid_sums(w_a, a)
            total = total + g1[a] * (cb1[a] + c1[a] * beside - OMEGA * cur)
        total = total + pltpu.roll(total, 64, 1)
        cb2[m] = 2.0 * c2[m] * take(pair_lanes(total), even)
    low_sweep(cb2, u_a, c2, cb2, 3, 17)
    low_sweep(u_a, u_b, c2, cb2, 4, 16)
    low_sweep(u_b, u_a, c2, cb2, 5, 15)
    for m in range(5, 15):
        step = take(u_a[m], (lane % 64) // 2)
        for a in (2 * m, 2 * m + 1):
            w_a[a] = w_a[a] + jnp.where(c1[a] > 0.0, step, 0.0)
    mid_sweep(w_a, w_b, c1, cb1, 12, 28)
    mid_sweep(w_b, w_a, c1, cb1, 13, 27)


def rest_kernel(place, own_head, own_late, keep, next_head, next_late, cc, cb, coupled, cc_r, cb_r, v2_r, flat):
    parts = Parts(own_head, own_late, keep, next_head, next_late)
    for k, c in enumerate(OTHERS):
        for x in range(CX):
            own, other = 16 + 9 * k + x, 8 * LATE + 9 * k + x - 7
            if x < 7:
                tile = keep[own]
            elif x < 9:
                tile = keep[own] + next_late[other]
            else:
                tile = next_late[other]
            coupled[c, x] = tile
    for x in range(CX):
        for q in range(4):
            flat[pl.ds(x * 32 + q, 8, stride=4), :] = parts.joined(7 + x, 1, q)
    for x in range(CX):
        coupled[1, x] = flat[pl.ds(pl.multiple_of(x * 32 + 8 * place[0], 8), 8), :]
    coefs, bases, v2 = Rows(cc, cc_r, 5, 25), Rows(cb, cb_r, 5, 25), Rows(None, v2_r, 6, 24)
    for t in (*range(5), *range(25, T0)):
        for q in range(4):
            coefs[t, q], bases[t, q], _ = parts.coefficient(t, q)
    fine_sweep(bases, v2, coefs, bases, 1, 6)
    fine_sweep(bases, v2, coefs, bases, 24, 29)


def start_kernel(own_head, own_late, keep, next_head, cc, cb, gg, v2, send):
    parts = Parts(own_head, own_late, keep, next_head)
    for t in range(5, 25):
        for q in range(4):
            cc[t, q], cb[t, q], diag = parts.coefficient(t, q)
            if 7 <= t < 23:
                gg[t - 7, q] = (1.0 / OMEGA) * diag
    fine_sweep(cb, v2, cc, cb, 6, 24)
    lane = lane_index()
    even = (2 * lane) % NZ
    for k in range(8):
        opened = take(parts.opened(2 + k // 2), even)
        d_sum = [0.0, 0.0]
        for dx in range(2):
            for q in range(4):
                d_sum[q // 2] = d_sum[q // 2] + parts.joined(7 + 2 * k + dx, 1, q)
        damp = 0.125 * pack(d_sum)
        diag = 1.5 + damp
        coef = OMEGA * opened / diag
        send[k] = coef * fine_residue(v2, cc, cb, gg, k)
        send[8 + k] = 0.25 * coef
        send[16 + k] = (1.0 / OMEGA) * diag
        if k % 2 == 0:
            above = damp
        else:
            total = above + damp
            total = total + pltpu.roll(total, 64, 1)
            low = 0.375 + 0.125 * take(pair_lanes(total), even)
            send[24 + k // 2] = jnp.where(lane < 32, 0.0625 * (OMEGA * take(opened, even) / low), 0.0)


def window(core, far_low, second, own, first, far_high):
    even = core == 0

    def part(n, k):
        if n == 1:
            return jnp.where(even, second[k], first[k])
        if n == 3:
            return jnp.where(even, first[k], second[k])
        return (far_low, None, own, None, far_high)[n][k]

    return part


def middle_kernel(place, far_low, second, own, first, far_high, cc, cb, gg, v2, cc_r, cb_r, v2_r, v_out, c1, g1, c2, send,
                  cb1, w_a, w_b, cb2, u_a, u_b, v_a, v_b):
    part = window(place[1], far_low, second, own, first, far_high)
    for n in range(5):
        for k in range(8):
            cb1[8 * n + k] = part(n, k)
            c1[8 * n + k] = part(n, 8 + k)
            g1[8 * n + k] = part(n, 16 + k)
        for k in range(4):
            c2[4 * n + k] = part(n, 24 + k)
    levels_solve(c1, g1, c2, cb1, w_a, w_b, cb2, u_a, u_b)
    cc, cb, v2 = Rows(cc, cc_r, 5, 25), Rows(cb, cb_r, 5, 25), Rows(v2, v2_r, 6, 24)
    fine_correct(v2, v_a, w_a, cc, 13, 27)
    fine_sweep(v_a, v_b, cc, cb, 2, 28)
    fine_sweep(v_b, v_a, cc, cb, 3, 27)
    fine_sweep(v_a, v_b, cc, cb, 4, 26)
    fine_sweep(v_b, v_out, cc, cb, 5, 25)
    for k in range(8):
        send[k] = 4.0 * c1[16 + k] * fine_residue(v_out, cc, cb, gg, k)


def last_kernel(place, far_low, second, own, first, far_high, cc, cb, v2, c1, g1, c2, out,
                cb1, w_a, w_b, cb2, u_a, u_b, v_a, v_b, flat):
    part = window(place[1], far_low, second, own, first, far_high)
    for n in range(5):
        for k in range(8):
            cb1[8 * n + k] = part(n, k)
    levels_solve(c1, g1, c2, cb1, w_a, w_b, cb2, u_a, u_b)
    fine_correct(v2, v_a, w_a, cc, 15, 25)
    fine_sweep(v_a, v_b, cc, cb, 6, 24)
    fine_sweep(v_b, v_a, cc, cb, 7, 23)
    for x in range(CX):
        for q in range(4):
            flat[pl.ds(x * 32 + q, 8, stride=4), :] = v_a[7 + x, q]
    for x in range(CX):
        out[x] = flat[pl.ds(pl.multiple_of(x * 32 + 8 * place[0], 8), 8), :]


def call(kernel, outs, scratch, operands, smem_first=False, in_hbm=False, cost=1000000, limit=LIMIT):
    kind = pltpu.HBM if in_hbm else pltpu.VMEM
    specs = [pl.BlockSpec(memory_space=kind) for _ in operands]
    if smem_first:
        specs[0] = pl.BlockSpec(memory_space=pltpu.SMEM)
    shapes = [jax.ShapeDtypeStruct(shape, F32) for shape in outs]
    return pl.pallas_call(
        kernel,
        out_shape=shapes,
        in_specs=specs,
        out_specs=[pl.BlockSpec(memory_space=pltpu.VMEM) for _ in outs],
        scratch_shapes=[pltpu.VMEM(*piece) if isinstance(piece, tuple) else piece for piece in scratch],
        compiler_params=pltpu.CompilerParams(vmem_limit_bytes=limit),
        cost_estimate=pl.CostEstimate(flops=cost, bytes_accessed=cost, transcendentals=0),
    )(*operands)


def fetch(block, distance):
    count = lax.axis_size("box")
    return lax.ppermute(block, "box", [((i + distance) % count, i) for i in range(count)])


def swap(block):
    return lax.ppermute(block, "box", [(i ^ 1, i) for i in range(lax.axis_size("box"))])


def around(block, core, beside=None):
    far_low, far_high = fetch(block, -2), fetch(block, 2)
    first = swap(block)
    onward = jnp.where(core == 0, far_high, far_low)
    if beside is not None:
        onward, beside = lax.optimization_barrier((onward, beside))
    return [far_low, swap(onward), block, first, far_high], beside


def shards(volume, drag, momentum, offsets, cell_index, destinations, rhs, wall):
    core = lax.axis_index("box").astype(I32) % 2
    place = jnp.stack([lax.axis_index("slab").astype(I32), core])
    prev = fetch(jnp.concatenate([rhs[7:], wall[7:].astype(F32)], axis=0), -1)
    one = (1, PART)
    (outgoing,) = call(
        route_kernel,
        [(N_BOX, 1, 8 * CAP)],
        [(one, F32), (one, F32), ((2, PART), F32), ((3, PART), F32), (one, I32), (one, I32),
         ((24 * CAP, PART), BF16), ((N_BOX, 8 * CAP), F32), pltpu.SemaphoreType.DMA((6,))],
        [volume.reshape(one), drag.reshape(one), momentum, offsets, cell_index.reshape(one), destinations.reshape(one)],
        in_hbm=True,
        limit=62 * 1024 * 1024,
    )
    incoming = lax.all_to_all(outgoing, "box", split_axis=0, concat_axis=0, tiled=True)
    pay, craw = call(
        deposit_kernel,
        [(3 * XE + XE // 2, 8, NZ), (3, XE, 8, NZ)],
        [((13, CAP, NZ), F32), ((3, CAP, NZ), I32), ((XE, CAP, NZ), F32), ((768, NZ), F32)]
        + [((768, SLOTS // CHUNKS), BF16)] * CHUNKS + [((NZ, SLOTS // CHUNKS), BF16)] * CHUNKS,
        [incoming.reshape(N_BOX, 8 * CAP), rhs, wall, prev],
    )
    slabs = lax.all_gather(pay, "slab")
    sums = [((HEAD * 32, NZ), F32)] * 2
    (head,) = call(head_kernel, [(8 * HEAD + 3, 8, NZ)], sums, [slabs])
    next_head = fetch(head, 1)
    late, keep = call(
        late_kernel, [(8 * LATE + 28, 8, NZ), (43, 8, NZ)], sums, [place, slabs, craw], smem_first=True
    )
    next_late = fetch(late, 1)
    fine, mid, low = (T0, 4, 8, NZ), (T1, 8, NZ), (T2, 8, NZ)
    cc, cb, gg, v2, first = call(
        start_kernel, [fine, fine, (CX, 4, 8, NZ), fine, (28, 8, NZ)], [], [head, late, keep, next_head]
    )
    coupled, cc_r, cb_r, v2_r = call(
        rest_kernel,
        [(4, CX, 8, NZ), (10, 4, 8, NZ), (10, 4, 8, NZ), (12, 4, 8, NZ)],
        [((CX * 32, NZ), F32)],
        [place, head, late, keep, next_head, next_late, cc, cb],
        smem_first=True,
    )
    scratch = [(mid, F32), (mid, F32), (mid, F32), (low, F32), (low, F32), (low, F32), (fine, F32), (fine, F32)]
    parts, coupled = around(first, core, coupled)
    v3, c1, g1, c2, second = call(
        middle_kernel,
        [fine, mid, mid, low, (8, 8, NZ)],
        scratch,
        [place] + parts + [cc, cb, gg, v2, cc_r, cb_r, v2_r],
        smem_first=True,
    )
    parts, _ = around(second, core)
    (pressure,) = call(
        last_kernel,
        [(CX, 8, NZ)],
        scratch + [((CX * 32, NZ), F32)],
        [place] + parts + [cc, cb, v3, c1, g1, c2],
        smem_first=True,
    )
    return coupled, pressure


def solution(mesh):
    in_specs = (
        P(("box", "slab")),
        P(("box", "slab")),
        P(None, ("box", "slab")),
        P(None, ("box", "slab")),
        P(("box", "slab")),
        P(("box", "slab"), None),
        P("box", "slab", None),
        P("box", "slab", None),
    )
    out_specs = (P(None, "box", "slab", None), P("box", "slab", None))
    return jax.shard_map(shards, mesh=mesh, in_specs=in_specs, out_specs=out_specs, check_vma=False)
```

```python
import jax
import jax.numpy as jnp
from jax import lax
from jax.experimental import pallas as pl
from jax.experimental.pallas import tpu as pltpu
from jax.sharding import PartitionSpec as P

F32 = jnp.float32
BF16 = jnp.bfloat16
I32 = jnp.int32

CX, CY, NZ = 16, 8, 128
PART = 2048
N_BOX = 128
CAP = 32
SLOTS = N_BOX * CAP
XE = CX + 2
OMEGA = 0.8

T0, T1, T2 = 30, 40, 20

OTHERS = (0, 2, 3)
CHUNKS = 8

LIMIT = 48 * 1024 * 1024

NT = (((1,), (1,)), ((), ()))


def tap_weights(frac):
    return (
        0.5 * (0.5 - frac) * (0.5 - frac),
        0.75 - frac * frac,
        0.5 * (0.5 + frac) * (0.5 + frac),
    )


def spread(index, at, taps):
    return jnp.where(
        index == at,
        taps[0],
        jnp.where(index == at + 1, taps[1], jnp.where(index == at + 2, taps[2], 0.0)),
    )


def route_kernel(vol_in, drag_in, mom_in, off_in, cell_in, dest_in, out, vol, drag, mom, off, cell, dest, picked, ordered, sems):
    pairs = ((dest_in, dest), (vol_in, vol), (drag_in, drag), (mom_in, mom), (off_in, off), (cell_in, cell))
    copies = [pltpu.make_async_copy(a, b, sems.at[k]) for k, (a, b) in enumerate(pairs)]
    for copy in copies:
        copy.start()
    copies[0].wait()
    target = dest[...]
    hot = lax.broadcasted_iota(I32, (N_BOX, PART), 0) == target
    hot_f = jnp.where(hot, 1.0, 0.0)
    hot_b = hot_f.astype(BF16)
    width = 256
    above = lax.broadcasted_iota(I32, (width, width), 0) < lax.broadcasted_iota(I32, (width, width), 1)
    before = jnp.where(above, 1.0, 0.0).astype(BF16)
    carry = jnp.zeros((N_BOX, 1), F32)
    places = []
    for k in range(PART // width):
        cut = slice(k * width, (k + 1) * width)
        rank = jnp.dot(hot_b[:, cut], before, preferred_element_type=F32) + carry
        places.append(jnp.sum(rank * hot_f[:, cut], axis=0, keepdims=True))
        carry = carry + jnp.sum(hot_f[:, cut], axis=1, keepdims=True)
    place = jnp.concatenate(places, axis=1).astype(I32)
    at_place = lax.broadcasted_iota(I32, (CAP, PART), 0) == place
    for copy in copies[1:]:
        copy.wait()
    fields = [vol[...], drag[...], mom[0:1, :], mom[1:2, :]]
    fields += [off[0:1, :], off[1:2, :], off[2:3, :], cell[...].astype(F32)]
    for f, left in enumerate(fields):
        for part in range(3):
            rounded = left.astype(BF16).astype(F32)
            row = (part * 8 + f) * CAP
            picked[row : row + CAP, :] = jnp.where(at_place, rounded, 0.0).astype(BF16)
            left = left - rounded
    sums = lax.dot_general(picked[...], hot_b, NT, preferred_element_type=F32)
    half = 8 * CAP
    sums = sums[:half] + sums[half : 2 * half] + sums[2 * half :]
    ordered[...] = sums.T
    for r in range(N_BOX):
        out[r] = ordered[r : r + 1, :]


def deposit_kernel(recv, rhs, wall, prev, pay, craw, par, cells, xs, acc, *mats):
    amats, vmats = mats[:CHUNKS], mats[CHUNKS:]
    fields = recv[...].T
    for c in range(4):
        par[c] = fields[c * CAP : (c + 1) * CAP]
    cell = fields[7 * CAP :].astype(I32)
    x_cell = cell // (NZ * CY)
    cells[0] = x_cell
    cells[1] = (cell // NZ) % CY
    cells[2] = cell % NZ
    for d in range(3):
        for k, tap in enumerate(tap_weights(fields[(4 + d) * CAP : (5 + d) * CAP])):
            par[4 + 3 * d + k] = tap
    for x in range(XE):
        xs[x] = spread(x, x_cell, (par[4], par[5], par[6]))
    sub24 = lax.broadcasted_iota(I32, (24, NZ), 0)
    sub8 = lax.broadcasted_iota(I32, (8, NZ), 0)
    sub128 = lax.broadcasted_iota(I32, (NZ, NZ), 0)

    def one(w, amat, vmat, at):
        def row(k):
            return par[k, w : w + 1, :]

        lanes = slice(at, at + NZ)
        vals = [row(c) for c in range(4)]
        wx = [row(4 + k) for k in range(3)]
        wy = [row(7 + k) for k in range(3)]
        wz = [row(10 + k) for k in range(3)]
        xc, yc, zc = [cells[d, w : w + 1, :] for d in range(3)]
        y_tile = spread(sub8, yc - 1, wy)
        low = jnp.where(yc == 0, wy[0], 0.0)
        high = jnp.where(yc == CY - 1, wy[2], 0.0)
        x_tile = spread(sub24, xc, wx)
        edge = jnp.concatenate([x_tile * low, x_tile * high], axis=0)
        for c in range(4):
            amat[576 + 48 * c : 576 + 48 * (c + 1), lanes] = (vals[c] * edge).astype(BF16)
        for pair in range(XE // 2):
            plane = jnp.concatenate([xs[2 * pair + k, w : w + 1, :] * y_tile for k in range(2)], axis=0)
            for c in range(4):
                r = 144 * c + 16 * pair
                amat[r : r + 16, lanes] = (vals[c] * plane).astype(BF16)
        vmat[:, lanes] = spread(sub128, zc - 1, wz).astype(BF16)

    each = CAP // CHUNKS
    for n in range(CHUNKS):
        for k in range(each):
            one(n * each + k, amats[n], vmats[n], k * NZ)
        part = lax.dot_general(amats[n][...], vmats[n][...], NT, preferred_element_type=F32)
        acc[...] = part if n == 0 else acc[...] + part
    for x in range(XE):
        c = [acc[144 * k + 8 * x : 144 * k + 8 * x + 8, :] for k in range(4)]
        for k, channel in enumerate(OTHERS):
            craw[k, x] = c[channel]
        if x < 9:
            right, opened = prev[x], prev[9 + x]
        else:
            right, opened = rhs[x - 9], wall[x - 9].astype(F32)
        whole = right - c[0] * right if x < CX else -(c[0] * right)
        pay[x] = opened * (whole + c[2] + c[3])
        pay[XE + x] = c[1]
        pay[2 * XE + x] = acc[pl.ds(576 + x, 8, stride=24), :]
        extra = jnp.concatenate([right[0:1], right[7:8], opened[0:1], opened[4:5]], axis=0)
        pay[3 * XE + x // 2, (x % 2) * 4 : (x % 2) * 4 + 4, :] = extra


HEAD = 11
LATE = CX - HEAD


def slab_sums(got, rows, ssum, dsum):
    sub = lax.broadcasted_iota(I32, (8, NZ), 0)
    for n, x in enumerate(rows):
        g_row = (x % 2) * 4
        halos = [got[s, 2 * XE + x] for s in range(4)]
        for s in range(4):
            below, above = halos[(s + 3) % 4], halos[(s + 1) % 4]
            extra = got[s, 3 * XE + x // 2]
            rhs_f, rhs_l = extra[g_row : g_row + 1], extra[g_row + 1 : g_row + 2]
            o_f, o_l = extra[g_row + 2 : g_row + 3], extra[g_row + 3 : g_row + 4]
            from_below = o_f * (below[5:6] + below[7:8] - below[1:2] * rhs_f)
            from_above = o_l * (above[4:5] + above[6:7] - above[0:1] * rhs_l)
            at = n * 32 + s * 8
            ssum[at : at + 8, :] = edges(sub, got[s, x], from_below, from_above)
            dsum[at : at + 8, :] = edges(sub, got[s, XE + x], below[3:4], above[2:3])


def edges(sub, tile, to_first, to_last):
    return tile + jnp.where(sub == 0, to_first, 0.0) + jnp.where(sub == 7, to_last, 0.0)


def opened_block(got, x, out, at):
    g_row = (x % 2) * 4
    for s in range(4):
        out[at, 2 * s : 2 * s + 2, :] = got[s, 3 * XE + x // 2, g_row + 2 : g_row + 4, :]


def head_kernel(got, head, ssum, dsum):
    slab_sums(got, range(HEAD), ssum, dsum)
    for x in range(HEAD):
        for q in range(4):
            head[4 * x + q] = ssum[pl.ds(x * 32 + q, 8, stride=4), :]
            head[4 * (HEAD + x) + q] = dsum[pl.ds(x * 32 + q, 8, stride=4), :]
    for k, x in enumerate((1, 5, 9)):
        opened_block(got, x, head, 8 * HEAD + k)


def late_kernel(place, got, craw, late, keep, ssum, dsum):
    s_me = place[0]
    sub = lax.broadcasted_iota(I32, (8, NZ), 0)
    slab_sums(got, range(HEAD, XE), ssum, dsum)
    for n in range(XE - HEAD):
        for q in range(4):
            s_tile = ssum[pl.ds(n * 32 + q, 8, stride=4), :]
            d_tile = dsum[pl.ds(n * 32 + q, 8, stride=4), :]
            if n < LATE:
                late[4 * n + q] = s_tile
                late[4 * (LATE + n) + q] = d_tile
            else:
                keep[4 * (n - LATE) + q] = s_tile
                keep[4 * (n - LATE + 2) + q] = d_tile
    for x in range(XE):
        below = got[(s_me + 3) % 4, 2 * XE + x]
        above = got[(s_me + 1) % 4, 2 * XE + x]
        for k, c in enumerate(OTHERS):
            tile = edges(sub, craw[k, x], below[2 * c + 1 : 2 * c + 2], above[2 * c : 2 * c + 1])
            if x < 9:
                late[8 * LATE + 9 * k + x] = tile
            else:
                keep[16 + 9 * k + x - 9] = tile
    opened_block(got, 13, late, 8 * LATE + 27)


class Parts:
    def __init__(self, own_head, own_late, keep, next_head, next_late=None):
        self.own = (own_head, own_late, keep)
        self.next = (next_head, next_late)

    @staticmethod
    def tile(parts, x, kind, q):
        if x < HEAD:
            return parts[0][4 * (HEAD * kind + x) + q]
        if x < CX:
            return parts[1][4 * (LATE * kind + x - HEAD) + q]
        return parts[2][4 * (2 * kind + x - CX) + q]

    def joined(self, t, kind, q):
        if t < 14:
            return self.tile(self.own, t + 2, kind, q)
        other = self.tile(self.next, t - 14, kind, q)
        return other if t > 15 else other + self.tile(self.own, t + 2, kind, q)

    def opened(self, block):
        head, late = (self.own if block < 4 else self.next)[:2]
        k = block % 4
        return head[8 * HEAD + k] if k < 3 else late[8 * LATE + 27]

    def coefficient(self, t, q):
        diag = 6.0 + self.joined(t, 1, q)
        coef = OMEGA * self.opened((t + 1) // 4) / diag
        return coef, coef * self.joined(t, 0, q), diag


class Rows:
    def __init__(self, mid, rest, low, high):
        self.mid, self.rest, self.low, self.high = mid, rest, low, high

    def place(self, index):
        t, q = index
        if self.low <= t < self.high:
            return self.mid, (t, q)
        return self.rest, (t if t < self.low else t - self.high + self.low, q)

    def __getitem__(self, index):
        ref, at = self.place(index)
        return ref[at]

    def __setitem__(self, index, tile):
        ref, at = self.place(index)
        ref[at] = tile


def lane_index():
    return lax.broadcasted_iota(I32, (8, NZ), 1)


def take(tile, index):
    return jnp.take_along_axis(tile, index, axis=1)


def pair_lanes(tile):
    return tile + pltpu.roll(tile, NZ - 1, 1)


def fine_sums(ref, t):
    lane = lane_index()
    cur = [ref[t, q] for q in range(4)]
    sums = []
    for q in range(4):
        after = cur[q + 1] if q < 3 else pltpu.roll(cur[0], 7, 0)
        before = cur[q - 1] if q else pltpu.roll(cur[3], 1, 0)
        left = jnp.where(lane == 0, 0.0, pltpu.roll(cur[q], 1, 1))
        right = jnp.where(lane == NZ - 1, 0.0, pltpu.roll(cur[q], NZ - 1, 1))
        sums.append((ref[t - 1, q] + ref[t + 1, q]) + (after + before) + (left + right))
    return cur, sums


def fine_sweep(src, dst, coef, base, low, high):
    for t in range(low, high):
        cur, sums = fine_sums(src, t)
        for q in range(4):
            dst[t, q] = (1.0 - OMEGA) * cur[q] + base[t, q] + coef[t, q] * sums[q]


def fine_residue(src, coef, base, weight, k):
    total = [0.0, 0.0]
    for dx in range(2):
        t = 7 + 2 * k + dx
        cur, sums = fine_sums(src, t)
        for q in range(4):
            tile = weight[2 * k + dx, q] * (base[t, q] + coef[t, q] * sums[q] - OMEGA * cur[q])
            total[q // 2] = total[q // 2] + tile
    return 0.125 * pack(total)


def pack(total):
    lane = lane_index()
    even = (2 * lane) % NZ
    return jnp.where(lane < 64, take(pair_lanes(total[0]), even), take(pair_lanes(total[1]), even))


def fine_correct(v_in, v_out, w, coef, low, high):
    lane = lane_index()
    for a in range(low, high):
        for half in range(2):
            step = take(w[a], lane // 2 + 64 * half)
            for dx in range(2):
                t = 2 * a - 25 + dx
                for q in (2 * half, 2 * half + 1):
                    v_out[t, q] = v_in[t, q] + jnp.where(coef[t, q] > 0.0, step, 0.0)


def mid_sums(ref, a):
    lane = lane_index()
    cur = ref[a]
    turned = pltpu.roll(cur, 64, 1)
    beside = turned + jnp.where(lane < 64, pltpu.roll(turned, 1, 0), pltpu.roll(turned, 7, 0))
    left = jnp.where(lane % 64 == 0, 0.0, pltpu.roll(cur, 1, 1))
    right = jnp.where(lane % 64 == 63, 0.0, pltpu.roll(cur, NZ - 1, 1))
    return cur, (ref[a - 1] + ref[a + 1]) + beside + (left + right)


def mid_sweep(src, dst, coef, base, low, high):
    for a in range(low, high):
        cur, total = mid_sums(src, a)
        dst[a] = (1.0 - OMEGA) * cur + base[a] + coef[a] * total


def low_sweep(src, dst, coef, base, low, high):
    for m in range(low, high):
        cur = src[m]
        total = (src[m - 1] + src[m + 1]) + (pltpu.roll(cur, 1, 0) + pltpu.roll(cur, 7, 0))
        total = total + (pltpu.roll(cur, 1, 1) + pltpu.roll(cur, NZ - 1, 1))
        dst[m] = (1.0 - OMEGA) * cur + base[m] + coef[m] * total


def levels_solve(c1, g1, c2, cb1, w_a, w_b, cb2, u_a, u_b):
    lane = lane_index()
    even = (2 * lane) % NZ
    mid_sweep(cb1, w_a, c1, cb1, 3, 37)
    for m in range(2, 18):
        total = 0.0
        for a in (2 * m, 2 * m + 1):
            cur, beside = mid_sums(w_a, a)
            total = total + g1[a] * (cb1[a] + c1[a] * beside - OMEGA * cur)
        total = total + pltpu.roll(total, 64, 1)
        cb2[m] = 2.0 * c2[m] * take(pair_lanes(total), even)
    low_sweep(cb2, u_a, c2, cb2, 3, 17)
    low_sweep(u_a, u_b, c2, cb2, 4, 16)
    low_sweep(u_b, u_a, c2, cb2, 5, 15)
    for m in range(5, 15):
        step = take(u_a[m], (lane % 64) // 2)
        for a in (2 * m, 2 * m + 1):
            w_a[a] = w_a[a] + jnp.where(c1[a] > 0.0, step, 0.0)
    mid_sweep(w_a, w_b, c1, cb1, 12, 28)
    mid_sweep(w_b, w_a, c1, cb1, 13, 27)


def rest_kernel(place, own_head, own_late, keep, next_head, next_late, cc, cb, coupled, cc_r, cb_r, v2_r, flat):
    parts = Parts(own_head, own_late, keep, next_head, next_late)
    for k, c in enumerate(OTHERS):
        for x in range(CX):
            own, other = 16 + 9 * k + x, 8 * LATE + 9 * k + x - 7
            if x < 7:
                tile = keep[own]
            elif x < 9:
                tile = keep[own] + next_late[other]
            else:
                tile = next_late[other]
            coupled[c, x] = tile
    for x in range(CX):
        for q in range(4):
            flat[pl.ds(x * 32 + q, 8, stride=4), :] = parts.joined(7 + x, 1, q)
    for x in range(CX):
        coupled[1, x] = flat[pl.ds(pl.multiple_of(x * 32 + 8 * place[0], 8), 8), :]
    coefs, bases, v2 = Rows(cc, cc_r, 5, 25), Rows(cb, cb_r, 5, 25), Rows(None, v2_r, 6, 24)
    for t in (*range(5), *range(25, T0)):
        for q in range(4):
            coefs[t, q], bases[t, q], _ = parts.coefficient(t, q)
    fine_sweep(bases, v2, coefs, bases, 1, 6)
    fine_sweep(bases, v2, coefs, bases, 24, 29)


def start_kernel(own_head, own_late, keep, next_head, cc, cb, gg, v2, send):
    parts = Parts(own_head, own_late, keep, next_head)
    for t in range(5, 25):
        for q in range(4):
            cc[t, q], cb[t, q], diag = parts.coefficient(t, q)
            if 7 <= t < 23:
                gg[t - 7, q] = (1.0 / OMEGA) * diag
    fine_sweep(cb, v2, cc, cb, 6, 24)
    lane = lane_index()
    even = (2 * lane) % NZ
    for k in range(8):
        opened = take(parts.opened(2 + k // 2), even)
        d_sum = [0.0, 0.0]
        for dx in range(2):
            for q in range(4):
                d_sum[q // 2] = d_sum[q // 2] + parts.joined(7 + 2 * k + dx, 1, q)
        damp = 0.125 * pack(d_sum)
        diag = 1.5 + damp
        coef = OMEGA * opened / diag
        send[k] = coef * fine_residue(v2, cc, cb, gg, k)
        send[8 + k] = 0.25 * coef
        send[16 + k] = (1.0 / OMEGA) * diag
        if k % 2 == 0:
            above = damp
        else:
            total = above + damp
            total = total + pltpu.roll(total, 64, 1)
            low = 0.375 + 0.125 * take(pair_lanes(total), even)
            send[24 + k // 2] = jnp.where(lane < 32, 0.0625 * (OMEGA * take(opened, even) / low), 0.0)


def window(place, low_pair, second, own, first, high_pair):
    even_core, even_chip = place[1] == 0, place[2] == 0

    def part(n, k):
        if n == 2:
            return own[k]
        if n in (1, 3):
            return jnp.where(even_core == (n == 1), second[k], first[k])
        return jnp.where(even_chip == (n == 0), low_pair[k], high_pair[k])

    return part


def middle_kernel(place, low_pair, second, own, first, high_pair, cc, cb, gg, v2, cc_r, cb_r, v2_r, v_out, c1, g1, c2, send,
                  cb1, w_a, w_b, cb2, u_a, u_b, v_a, v_b):
    part = window(place, low_pair, second, own, first, high_pair)
    for n in range(5):
        for k in range(8):
            cb1[8 * n + k] = part(n, k)
            c1[8 * n + k] = part(n, 8 + k)
            g1[8 * n + k] = part(n, 16 + k)
        for k in range(4):
            c2[4 * n + k] = part(n, 24 + k)
    levels_solve(c1, g1, c2, cb1, w_a, w_b, cb2, u_a, u_b)
    cc, cb, v2 = Rows(cc, cc_r, 5, 25), Rows(cb, cb_r, 5, 25), Rows(v2, v2_r, 6, 24)
    fine_correct(v2, v_a, w_a, cc, 13, 27)
    fine_sweep(v_a, v_b, cc, cb, 2, 28)
    fine_sweep(v_b, v_a, cc, cb, 3, 27)
    fine_sweep(v_a, v_b, cc, cb, 4, 26)
    fine_sweep(v_b, v_out, cc, cb, 5, 25)
    for k in range(8):
        send[k] = 4.0 * c1[16 + k] * fine_residue(v_out, cc, cb, gg, k)


def last_kernel(place, low_pair, second, own, first, high_pair, cc, cb, v2, c1, g1, c2, out,
                cb1, w_a, w_b, cb2, u_a, u_b, v_a, v_b, flat):
    part = window(place, low_pair, second, own, first, high_pair)
    for n in range(5):
        for k in range(8):
            cb1[8 * n + k] = part(n, k)
    levels_solve(c1, g1, c2, cb1, w_a, w_b, cb2, u_a, u_b)
    fine_correct(v2, v_a, w_a, cc, 15, 25)
    fine_sweep(v_a, v_b, cc, cb, 6, 24)
    fine_sweep(v_b, v_a, cc, cb, 7, 23)
    for x in range(CX):
        for q in range(4):
            flat[pl.ds(x * 32 + q, 8, stride=4), :] = v_a[7 + x, q]
    for x in range(CX):
        out[x] = flat[pl.ds(pl.multiple_of(x * 32 + 8 * place[0], 8), 8), :]


def call(kernel, outs, scratch, operands, smem_first=False, in_hbm=False, cost=1000000, limit=LIMIT):
    kind = pltpu.HBM if in_hbm else pltpu.VMEM
    specs = [pl.BlockSpec(memory_space=kind) for _ in operands]
    if smem_first:
        specs[0] = pl.BlockSpec(memory_space=pltpu.SMEM)
    shapes = [jax.ShapeDtypeStruct(shape, F32) for shape in outs]
    return pl.pallas_call(
        kernel,
        out_shape=shapes,
        in_specs=specs,
        out_specs=[pl.BlockSpec(memory_space=pltpu.VMEM) for _ in outs],
        scratch_shapes=[pltpu.VMEM(*piece) if isinstance(piece, tuple) else piece for piece in scratch],
        compiler_params=pltpu.CompilerParams(vmem_limit_bytes=limit),
        cost_estimate=pl.CostEstimate(flops=cost, bytes_accessed=cost, transcendentals=0),
    )(*operands)


def fetch(block, distance):
    count = lax.axis_size("box")
    return lax.ppermute(block, "box", [((i + distance) % count, i) for i in range(count)])


def swap(block):
    return lax.ppermute(block, "box", [(i ^ 1, i) for i in range(lax.axis_size("box"))])


def meet(block, odd):
    count = lax.axis_size("box")
    chips = [((k + odd ^ 1) - odd) % (count // 2) for k in range(count // 2)]
    return lax.ppermute(block, "box", [(2 * chips[i // 2] + i % 2, i) for i in range(count)])


def around(block, place, beside=None):
    low_pair, high_pair = meet(block, 1), meet(block, 0)
    first = swap(block)
    onward = jnp.where(place[1] == place[2], high_pair, low_pair)
    if beside is not None:
        onward, beside = lax.optimization_barrier((onward, beside))
    return [low_pair, swap(onward), block, first, high_pair], beside


def shards(volume, drag, momentum, offsets, cell_index, destinations, rhs, wall):
    box = lax.axis_index("box").astype(I32)
    place = jnp.stack([lax.axis_index("slab").astype(I32), box % 2, box // 2 % 2])
    prev = fetch(jnp.concatenate([rhs[7:], wall[7:].astype(F32)], axis=0), -1)
    one = (1, PART)
    (outgoing,) = call(
        route_kernel,
        [(N_BOX, 1, 8 * CAP)],
        [(one, F32), (one, F32), ((2, PART), F32), ((3, PART), F32), (one, I32), (one, I32),
         ((24 * CAP, PART), BF16), ((N_BOX, 8 * CAP), F32), pltpu.SemaphoreType.DMA((6,))],
        [volume.reshape(one), drag.reshape(one), momentum, offsets, cell_index.reshape(one), destinations.reshape(one)],
        in_hbm=True,
        limit=62 * 1024 * 1024,
    )
    incoming = lax.all_to_all(outgoing, "box", split_axis=0, concat_axis=0, tiled=True)
    pay, craw = call(
        deposit_kernel,
        [(3 * XE + XE // 2, 8, NZ), (3, XE, 8, NZ)],
        [((13, CAP, NZ), F32), ((3, CAP, NZ), I32), ((XE, CAP, NZ), F32), ((768, NZ), F32)]
        + [((768, SLOTS // CHUNKS), BF16)] * CHUNKS + [((NZ, SLOTS // CHUNKS), BF16)] * CHUNKS,
        [incoming.reshape(N_BOX, 8 * CAP), rhs, wall, prev],
    )
    slabs = lax.all_gather(pay, "slab")
    sums = [((HEAD * 32, NZ), F32)] * 2
    (head,) = call(head_kernel, [(8 * HEAD + 3, 8, NZ)], sums, [slabs])
    next_head = fetch(head, 1)
    late, keep = call(
        late_kernel, [(8 * LATE + 28, 8, NZ), (43, 8, NZ)], sums, [place, slabs, craw], smem_first=True
    )
    next_late = fetch(late, 1)
    fine, mid, low = (T0, 4, 8, NZ), (T1, 8, NZ), (T2, 8, NZ)
    cc, cb, gg, v2, first = call(
        start_kernel, [fine, fine, (CX, 4, 8, NZ), fine, (28, 8, NZ)], [], [head, late, keep, next_head]
    )
    coupled, cc_r, cb_r, v2_r = call(
        rest_kernel,
        [(4, CX, 8, NZ), (10, 4, 8, NZ), (10, 4, 8, NZ), (12, 4, 8, NZ)],
        [((CX * 32, NZ), F32)],
        [place, head, late, keep, next_head, next_late, cc, cb],
        smem_first=True,
    )
    scratch = [(mid, F32), (mid, F32), (mid, F32), (low, F32), (low, F32), (low, F32), (fine, F32), (fine, F32)]
    parts, coupled = around(first, place, coupled)
    v3, c1, g1, c2, second = call(
        middle_kernel,
        [fine, mid, mid, low, (8, 8, NZ)],
        scratch,
        [place] + parts + [cc, cb, gg, v2, cc_r, cb_r, v2_r],
        smem_first=True,
    )
    parts, _ = around(second, place)
    (pressure,) = call(
        last_kernel,
        [(CX, 8, NZ)],
        scratch + [((CX * 32, NZ), F32)],
        [place] + parts + [cc, cb, v3, c1, g1, c2],
        smem_first=True,
    )
    return coupled, pressure


def solution(mesh):
    in_specs = (
        P(("box", "slab")),
        P(("box", "slab")),
        P(None, ("box", "slab")),
        P(None, ("box", "slab")),
        P(("box", "slab")),
        P(("box", "slab"), None),
        P("box", "slab", None),
        P("box", "slab", None),
    )
    out_specs = (P(None, "box", "slab", None), P("box", "slab", None))
    return jax.shard_map(shards, mesh=mesh, in_specs=in_specs, out_specs=out_specs, check_vma=False)
```

```python
import jax
import jax.numpy as jnp
from jax import lax
from jax.experimental import pallas as pl
from jax.experimental.pallas import tpu as pltpu
from jax.sharding import PartitionSpec as P

F32 = jnp.float32
BF16 = jnp.bfloat16
I32 = jnp.int32

CX, CY, NZ = 16, 8, 128
PART = 2048
N_BOX = 128
CAP = 32
SLOTS = N_BOX * CAP
XE = CX + 2
OMEGA = 0.8

T0, T1, T2 = 30, 40, 20

OTHERS = (0, 2, 3)
CHUNKS = 8

LIMIT = 48 * 1024 * 1024

NT = (((1,), (1,)), ((), ()))


def tap_weights(frac):
    return (
        0.5 * (0.5 - frac) * (0.5 - frac),
        0.75 - frac * frac,
        0.5 * (0.5 + frac) * (0.5 + frac),
    )


def spread(index, at, taps):
    return jnp.where(
        index == at,
        taps[0],
        jnp.where(index == at + 1, taps[1], jnp.where(index == at + 2, taps[2], 0.0)),
    )


def route_kernel(vol_in, drag_in, mom_in, off_in, cell_in, dest_in, out, vol, drag, mom, off, cell, dest, picked, ordered, sems):
    pairs = ((dest_in, dest), (vol_in, vol), (drag_in, drag), (mom_in, mom), (off_in, off), (cell_in, cell))
    copies = [pltpu.make_async_copy(a, b, sems.at[k]) for k, (a, b) in enumerate(pairs)]
    for copy in copies:
        copy.start()
    copies[0].wait()
    target = dest[...]
    hot = lax.broadcasted_iota(I32, (N_BOX, PART), 0) == target
    hot_f = jnp.where(hot, 1.0, 0.0)
    hot_b = hot_f.astype(BF16)
    width = 256
    above = lax.broadcasted_iota(I32, (width, width), 0) < lax.broadcasted_iota(I32, (width, width), 1)
    before = jnp.where(above, 1.0, 0.0).astype(BF16)
    carry = jnp.zeros((N_BOX, 1), F32)
    places = []
    for k in range(PART // width):
        cut = slice(k * width, (k + 1) * width)
        rank = jnp.dot(hot_b[:, cut], before, preferred_element_type=F32) + carry
        places.append(jnp.sum(rank * hot_f[:, cut], axis=0, keepdims=True))
        carry = carry + jnp.sum(hot_f[:, cut], axis=1, keepdims=True)
    place = jnp.concatenate(places, axis=1).astype(I32)
    at_place = lax.broadcasted_iota(I32, (CAP, PART), 0) == place
    for copy in copies[1:]:
        copy.wait()
    fields = [vol[...], drag[...], mom[0:1, :], mom[1:2, :]]
    fields += [off[0:1, :], off[1:2, :], off[2:3, :], cell[...].astype(F32)]
    for f, left in enumerate(fields):
        for part in range(3):
            rounded = left.astype(BF16).astype(F32)
            row = (part * 8 + f) * CAP
            picked[row : row + CAP, :] = jnp.where(at_place, rounded, 0.0).astype(BF16)
            left = left - rounded
    sums = lax.dot_general(picked[...], hot_b, NT, preferred_element_type=F32)
    half = 8 * CAP
    sums = sums[:half] + sums[half : 2 * half] + sums[2 * half :]
    ordered[...] = sums.T
    for r in range(N_BOX):
        out[r] = ordered[r : r + 1, :]


def deposit_kernel(recv, rhs, wall, prev, pay, craw, par, cells, xs, acc, *mats):
    amats, vmats = mats[:CHUNKS], mats[CHUNKS:]
    fields = recv[...].T
    for c in range(4):
        par[c] = fields[c * CAP : (c + 1) * CAP]
    cell = fields[7 * CAP :].astype(I32)
    x_cell = cell // (NZ * CY)
    cells[0] = x_cell
    cells[1] = (cell // NZ) % CY
    cells[2] = cell % NZ
    for d in range(3):
        for k, tap in enumerate(tap_weights(fields[(4 + d) * CAP : (5 + d) * CAP])):
            par[4 + 3 * d + k] = tap
    for x in range(XE):
        xs[x] = spread(x, x_cell, (par[4], par[5], par[6]))
    sub24 = lax.broadcasted_iota(I32, (24, NZ), 0)
    sub8 = lax.broadcasted_iota(I32, (8, NZ), 0)
    sub128 = lax.broadcasted_iota(I32, (NZ, NZ), 0)

    def one(w, amat, vmat, at):
        def row(k):
            return par[k, w : w + 1, :]

        lanes = slice(at, at + NZ)
        vals = [row(c) for c in range(4)]
        wx = [row(4 + k) for k in range(3)]
        wy = [row(7 + k) for k in range(3)]
        wz = [row(10 + k) for k in range(3)]
        xc, yc, zc = [cells[d, w : w + 1, :] for d in range(3)]
        y_tile = spread(sub8, yc - 1, wy)
        low = jnp.where(yc == 0, wy[0], 0.0)
        high = jnp.where(yc == CY - 1, wy[2], 0.0)
        x_tile = spread(sub24, xc, wx)
        edge = jnp.concatenate([x_tile * low, x_tile * high], axis=0)
        for c in range(4):
            amat[576 + 48 * c : 576 + 48 * (c + 1), lanes] = (vals[c] * edge).astype(BF16)
        for pair in range(XE // 2):
            plane = jnp.concatenate([xs[2 * pair + k, w : w + 1, :] * y_tile for k in range(2)], axis=0)
            for c in range(4):
                r = 144 * c + 16 * pair
                amat[r : r + 16, lanes] = (vals[c] * plane).astype(BF16)
        vmat[:, lanes] = spread(sub128, zc - 1, wz).astype(BF16)

    each = CAP // CHUNKS
    for n in range(CHUNKS):
        for k in range(each):
            one(n * each + k, amats[n], vmats[n], k * NZ)
        part = lax.dot_general(amats[n][...], vmats[n][...], NT, preferred_element_type=F32)
        acc[...] = part if n == 0 else acc[...] + part
    for x in range(XE):
        c = [acc[144 * k + 8 * x : 144 * k + 8 * x + 8, :] for k in range(4)]
        for k, channel in enumerate(OTHERS):
            craw[k, x] = c[channel]
        if x < 9:
            right, opened = prev[x], prev[9 + x]
        else:
            right, opened = rhs[x - 9], wall[x - 9].astype(F32)
        whole = right - c[0] * right if x < CX else -(c[0] * right)
        pay[x] = opened * (whole + c[2] + c[3])
        pay[XE + x] = c[1]
        pay[2 * XE + x] = acc[pl.ds(576 + x, 8, stride=24), :]
        extra = jnp.concatenate([right[0:1], right[7:8], opened[0:1], opened[4:5]], axis=0)
        pay[3 * XE + x // 2, (x % 2) * 4 : (x % 2) * 4 + 4, :] = extra


HEAD = 11
LATE = CX - HEAD


def slab_sums(got, rows, ssum, dsum):
    sub = lax.broadcasted_iota(I32, (8, NZ), 0)
    for n, x in enumerate(rows):
        g_row = (x % 2) * 4
        halos = [got[s, 2 * XE + x] for s in range(4)]
        for s in range(4):
            below, above = halos[(s + 3) % 4], halos[(s + 1) % 4]
            extra = got[s, 3 * XE + x // 2]
            rhs_f, rhs_l = extra[g_row : g_row + 1], extra[g_row + 1 : g_row + 2]
            o_f, o_l = extra[g_row + 2 : g_row + 3], extra[g_row + 3 : g_row + 4]
            from_below = o_f * (below[5:6] + below[7:8] - below[1:2] * rhs_f)
            from_above = o_l * (above[4:5] + above[6:7] - above[0:1] * rhs_l)
            at = n * 32 + s * 8
            ssum[at : at + 8, :] = edges(sub, got[s, x], from_below, from_above)
            dsum[at : at + 8, :] = edges(sub, got[s, XE + x], below[3:4], above[2:3])


def edges(sub, tile, to_first, to_last):
    return tile + jnp.where(sub == 0, to_first, 0.0) + jnp.where(sub == 7, to_last, 0.0)


def opened_block(got, x, out, at):
    g_row = (x % 2) * 4
    for s in range(4):
        out[at, 2 * s : 2 * s + 2, :] = got[s, 3 * XE + x // 2, g_row + 2 : g_row + 4, :]


def head_kernel(got, head, ssum, dsum):
    slab_sums(got, range(HEAD), ssum, dsum)
    for x in range(HEAD):
        for q in range(4):
            head[4 * x + q] = ssum[pl.ds(x * 32 + q, 8, stride=4), :]
            head[4 * (HEAD + x) + q] = dsum[pl.ds(x * 32 + q, 8, stride=4), :]
    for k, x in enumerate((1, 5, 9)):
        opened_block(got, x, head, 8 * HEAD + k)


def late_kernel(place, got, craw, late, keep, ssum, dsum):
    s_me = place[0]
    sub = lax.broadcasted_iota(I32, (8, NZ), 0)
    slab_sums(got, range(HEAD, XE), ssum, dsum)
    for n in range(XE - HEAD):
        for q in range(4):
            s_tile = ssum[pl.ds(n * 32 + q, 8, stride=4), :]
            d_tile = dsum[pl.ds(n * 32 + q, 8, stride=4), :]
            if n < LATE:
                late[4 * n + q] = s_tile
                late[4 * (LATE + n) + q] = d_tile
            else:
                keep[4 * (n - LATE) + q] = s_tile
                keep[4 * (n - LATE + 2) + q] = d_tile
    for x in range(XE):
        below = got[(s_me + 3) % 4, 2 * XE + x]
        above = got[(s_me + 1) % 4, 2 * XE + x]
        for k, c in enumerate(OTHERS):
            tile = edges(sub, craw[k, x], below[2 * c + 1 : 2 * c + 2], above[2 * c : 2 * c + 1])
            if x < 9:
                late[8 * LATE + 9 * k + x] = tile
            else:
                keep[16 + 9 * k + x - 9] = tile
    opened_block(got, 13, late, 8 * LATE + 27)


class Parts:
    def __init__(self, own_head, own_late, keep, next_head, next_late=None):
        self.own = (own_head, own_late, keep)
        self.next = (next_head, next_late)

    @staticmethod
    def tile(parts, x, kind, q):
        if x < HEAD:
            return parts[0][4 * (HEAD * kind + x) + q]
        if x < CX:
            return parts[1][4 * (LATE * kind + x - HEAD) + q]
        return parts[2][4 * (2 * kind + x - CX) + q]

    def joined(self, t, kind, q):
        if t < 14:
            return self.tile(self.own, t + 2, kind, q)
        other = self.tile(self.next, t - 14, kind, q)
        return other if t > 15 else other + self.tile(self.own, t + 2, kind, q)

    def opened(self, block):
        head, late = (self.own if block < 4 else self.next)[:2]
        k = block % 4
        return head[8 * HEAD + k] if k < 3 else late[8 * LATE + 27]

    def coefficient(self, t, q):
        diag = 6.0 + self.joined(t, 1, q)
        coef = OMEGA * self.opened((t + 1) // 4) * pl.reciprocal(diag)
        return coef, coef * self.joined(t, 0, q), diag


class Rows:
    def __init__(self, mid, rest, low, high):
        self.mid, self.rest, self.low, self.high = mid, rest, low, high

    def place(self, index):
        t, q = index
        if self.low <= t < self.high:
            return self.mid, (t, q)
        return self.rest, (t if t < self.low else t - self.high + self.low, q)

    def __getitem__(self, index):
        ref, at = self.place(index)
        return ref[at]

    def __setitem__(self, index, tile):
        ref, at = self.place(index)
        ref[at] = tile


def lane_index():
    return lax.broadcasted_iota(I32, (8, NZ), 1)


def take(tile, index):
    return jnp.take_along_axis(tile, index, axis=1)


def fine_sums(ref, t):
    lane = lane_index()
    cur = [ref[t, q] for q in range(4)]
    sums = []
    for q in range(4):
        after = cur[q + 1] if q < 3 else pltpu.roll(cur[0], 7, 0)
        before = cur[q - 1] if q else pltpu.roll(cur[3], 1, 0)
        left = jnp.where(lane == 0, 0.0, pltpu.roll(cur[q], 1, 1))
        right = jnp.where(lane == NZ - 1, 0.0, pltpu.roll(cur[q], NZ - 1, 1))
        sums.append((ref[t - 1, q] + ref[t + 1, q]) + (after + before) + (left + right))
    return cur, sums


def fine_sweep(src, dst, coef, base, low, high):
    for t in range(low, high):
        cur, sums = fine_sums(src, t)
        for q in range(4):
            dst[t, q] = (1.0 - OMEGA) * cur[q] + base[t, q] + coef[t, q] * sums[q]


def fine_residue(src, coef, base, weight):
    rows = []
    for k in range(8):
        total = [0.0, 0.0]
        for dx in range(2):
            t = 7 + 2 * k + dx
            cur, sums = fine_sums(src, t)
            for q in range(4):
                tile = weight[2 * k + dx, q] * (base[t, q] + coef[t, q] * sums[q] - OMEGA * cur[q])
                total[q // 2] = total[q // 2] + tile
        rows.append(jnp.concatenate(total, axis=1))
    return jnp.concatenate(rows, axis=0)


def choice(size, match):
    row = lax.broadcasted_iota(I32, (size, NZ), 0)
    column = lax.broadcasted_iota(I32, (size, NZ), 1)
    return jnp.where(match(row, column), 1.0, 0.0).astype(BF16)


def lane_sums(block, chosen):
    out, left = 0.0, block
    for _ in range(3):
        part = left.astype(BF16)
        out = out + jnp.dot(part, chosen, preferred_element_type=F32)
        left = left - part.astype(F32)
    return out


def pairs_packed():
    return choice(256, lambda r, c: r // 2 == c)


def fine_correct(v_in, v_out, w, coef, low, high):
    lane = lane_index()
    for a in range(low, high):
        for half in range(2):
            step = take(w[a], lane // 2 + 64 * half)
            for dx in range(2):
                t = 2 * a - 25 + dx
                for q in (2 * half, 2 * half + 1):
                    v_out[t, q] = v_in[t, q] + jnp.where(coef[t, q] > 0.0, step, 0.0)


def mid_sums(ref, a):
    lane = lane_index()
    cur = ref[a]
    turned = pltpu.roll(cur, 64, 1)
    beside = turned + jnp.where(lane < 64, pltpu.roll(turned, 1, 0), pltpu.roll(turned, 7, 0))
    left = jnp.where(lane % 64 == 0, 0.0, pltpu.roll(cur, 1, 1))
    right = jnp.where(lane % 64 == 63, 0.0, pltpu.roll(cur, NZ - 1, 1))
    return cur, (ref[a - 1] + ref[a + 1]) + beside + (left + right)


def mid_sweep(src, dst, coef, base, low, high):
    for a in range(low, high):
        cur, total = mid_sums(src, a)
        dst[a] = (1.0 - OMEGA) * cur + base[a] + coef[a] * total


def low_sweep(src, dst, coef, base, low, high):
    for m in range(low, high):
        cur = src[m]
        total = (src[m - 1] + src[m + 1]) + (pltpu.roll(cur, 1, 0) + pltpu.roll(cur, 7, 0))
        total = total + (pltpu.roll(cur, 1, 1) + pltpu.roll(cur, NZ - 1, 1))
        dst[m] = (1.0 - OMEGA) * cur + base[m] + coef[m] * total


def levels_solve(c1, g1, c2, cb1, w_a, w_b, cb2, u_a, u_b):
    lane = lane_index()
    mid_sweep(cb1, w_a, c1, cb1, 3, 37)
    totals = []
    for m in range(2, 18):
        total = 0.0
        for a in (2 * m, 2 * m + 1):
            cur, beside = mid_sums(w_a, a)
            total = total + g1[a] * (cb1[a] + c1[a] * beside - OMEGA * cur)
        totals.append(total)
    below = lane_sums(jnp.concatenate(totals, axis=0), choice(NZ, lambda r, c: r % 64 // 2 == c))
    for m in range(2, 18):
        cb2[m] = 2.0 * c2[m] * below[8 * (m - 2) : 8 * (m - 1)]
    low_sweep(cb2, u_a, c2, cb2, 3, 17)
    low_sweep(u_a, u_b, c2, cb2, 4, 16)
    low_sweep(u_b, u_a, c2, cb2, 5, 15)
    for m in range(5, 15):
        step = take(u_a[m], (lane % 64) // 2)
        for a in (2 * m, 2 * m + 1):
            w_a[a] = w_a[a] + jnp.where(c1[a] > 0.0, step, 0.0)
    mid_sweep(w_a, w_b, c1, cb1, 12, 28)
    mid_sweep(w_b, w_a, c1, cb1, 13, 27)


def rest_kernel(place, own_head, own_late, keep, next_head, next_late, cc, cb, coupled, cc_r, cb_r, v2_r, flat):
    parts = Parts(own_head, own_late, keep, next_head, next_late)
    for k, c in enumerate(OTHERS):
        for x in range(CX):
            own, other = 16 + 9 * k + x, 8 * LATE + 9 * k + x - 7
            if x < 7:
                tile = keep[own]
            elif x < 9:
                tile = keep[own] + next_late[other]
            else:
                tile = next_late[other]
            coupled[c, x] = tile
    for x in range(CX):
        for q in range(4):
            flat[pl.ds(x * 32 + q, 8, stride=4), :] = parts.joined(7 + x, 1, q)
    for x in range(CX):
        coupled[1, x] = flat[pl.ds(pl.multiple_of(x * 32 + 8 * place[0], 8), 8), :]
    coefs, bases, v2 = Rows(cc, cc_r, 5, 25), Rows(cb, cb_r, 5, 25), Rows(None, v2_r, 6, 24)
    for t in (*range(5), *range(25, T0)):
        for q in range(4):
            coefs[t, q], bases[t, q], _ = parts.coefficient(t, q)
    fine_sweep(bases, v2, coefs, bases, 1, 6)
    fine_sweep(bases, v2, coefs, bases, 24, 29)


def start_kernel(own_head, own_late, keep, next_head, cc, cb, gg, v2, send):
    parts = Parts(own_head, own_late, keep, next_head)
    for t in range(5, 25):
        for q in range(4):
            cc[t, q], cb[t, q], diag = parts.coefficient(t, q)
            if 7 <= t < 23:
                gg[t - 7, q] = (1.0 / OMEGA) * diag
    fine_sweep(cb, v2, cc, cb, 6, 24)
    damps = []
    for k in range(8):
        total = [0.0, 0.0]
        for dx in range(2):
            for q in range(4):
                total[q // 2] = total[q // 2] + parts.joined(7 + 2 * k + dx, 1, q)
        damps.append(jnp.concatenate(total, axis=1))
    lows = [damps[2 * m] + damps[2 * m + 1] for m in range(4)]
    opened = jnp.concatenate([parts.opened(2 + m) for m in range(4)], axis=0).astype(BF16)
    opened_1 = jnp.dot(opened, choice(NZ, lambda r, c: r == c % 64 * 2), preferred_element_type=F32)
    opened_2 = jnp.dot(opened, choice(NZ, lambda r, c: r == c * 4), preferred_element_type=F32)
    packed = pairs_packed()
    diag = 1.5 + 0.125 * lane_sums(jnp.concatenate(damps, axis=0), packed)
    low_diag = 0.375 + 0.015625 * lane_sums(
        jnp.concatenate(lows, axis=0), choice(256, lambda r, c: r % NZ // 4 == c)
    )
    source = 0.125 * lane_sums(fine_residue(v2, cc, cb, gg), packed)
    inverse = OMEGA * pl.reciprocal(diag)
    below = (0.0625 * OMEGA) * opened_2 * pl.reciprocal(low_diag)
    for k in range(8):
        rows = slice(8 * k, 8 * k + 8)
        coef = opened_1[8 * (k // 2) : 8 * (k // 2) + 8] * inverse[rows]
        send[k] = coef * source[rows]
        send[8 + k] = 0.25 * coef
        send[16 + k] = (1.0 / OMEGA) * diag[rows]
    for m in range(4):
        send[24 + m] = below[8 * m : 8 * m + 8]


def window(place, high_pair, second, own, first, low_pair):
    even_core, even_chip = place[1] == 0, place[2] == 0

    def part(n, k):
        if n == 2:
            return own[k]
        if n in (1, 3):
            return jnp.where(even_core == (n == 1), second[k], first[k])
        return jnp.where(even_chip == (n == 0), low_pair[k], high_pair[k])

    return part


def middle_kernel(place, high_pair, second, own, first, low_pair, cc, cb, gg, v2, cc_r, cb_r, v2_r, v_out, c1, g1, c2, send,
                  cb1, w_a, w_b, cb2, u_a, u_b, v_a, v_b):
    part = window(place, high_pair, second, own, first, low_pair)
    for n in range(5):
        for k in range(8):
            cb1[8 * n + k] = part(n, k)
            c1[8 * n + k] = part(n, 8 + k)
            g1[8 * n + k] = part(n, 16 + k)
        for k in range(4):
            c2[4 * n + k] = part(n, 24 + k)
    levels_solve(c1, g1, c2, cb1, w_a, w_b, cb2, u_a, u_b)
    cc, cb, v2 = Rows(cc, cc_r, 5, 25), Rows(cb, cb_r, 5, 25), Rows(v2, v2_r, 6, 24)
    fine_correct(v2, v_a, w_a, cc, 13, 27)
    fine_sweep(v_a, v_b, cc, cb, 2, 28)
    fine_sweep(v_b, v_a, cc, cb, 3, 27)
    fine_sweep(v_a, v_b, cc, cb, 4, 26)
    fine_sweep(v_b, v_out, cc, cb, 5, 25)
    source = lane_sums(fine_residue(v_out, cc, cb, gg), pairs_packed())
    for k in range(8):
        send[k] = 0.5 * c1[16 + k] * source[8 * k : 8 * k + 8]


def last_kernel(place, high_pair, second, own, first, low_pair, cc, cb, v2, c1, g1, c2, deposits, out, coupled,
                cb1, w_a, w_b, cb2, u_a, u_b, v_a, v_b, flat, sem):
    copy = pltpu.make_async_copy(deposits, coupled, sem)
    copy.start()
    part = window(place, high_pair, second, own, first, low_pair)
    for n in range(5):
        for k in range(8):
            cb1[8 * n + k] = part(n, k)
    levels_solve(c1, g1, c2, cb1, w_a, w_b, cb2, u_a, u_b)
    fine_correct(v2, v_a, w_a, cc, 15, 25)
    fine_sweep(v_a, v_b, cc, cb, 6, 24)
    fine_sweep(v_b, v_a, cc, cb, 7, 23)
    for x in range(CX):
        for q in range(4):
            flat[pl.ds(x * 32 + q, 8, stride=4), :] = v_a[7 + x, q]
    for x in range(CX):
        out[x] = flat[pl.ds(pl.multiple_of(x * 32 + 8 * place[0], 8), 8), :]
    copy.wait()


def call(kernel, outs, scratch, operands, smem_first=False, in_hbm=False, outs_hbm=0, cost=1000000, limit=LIMIT):
    kind = pltpu.HBM if in_hbm else pltpu.VMEM
    specs = [pl.BlockSpec(memory_space=kind) for _ in operands]
    if smem_first:
        specs[0] = pl.BlockSpec(memory_space=pltpu.SMEM)
    shapes = [jax.ShapeDtypeStruct(shape, F32) for shape in outs]
    return pl.pallas_call(
        kernel,
        out_shape=shapes,
        in_specs=specs,
        out_specs=[
            pl.BlockSpec(memory_space=pltpu.VMEM if n < len(outs) - outs_hbm else pltpu.HBM) for n in range(len(outs))
        ],
        scratch_shapes=[pltpu.VMEM(*piece) if isinstance(piece, tuple) else piece for piece in scratch],
        compiler_params=pltpu.CompilerParams(vmem_limit_bytes=limit),
        cost_estimate=pl.CostEstimate(flops=cost, bytes_accessed=cost, transcendentals=0),
    )(*operands)


def fetch(block, distance):
    count = lax.axis_size("box")
    return lax.ppermute(block, "box", [((i + distance) % count, i) for i in range(count)])


def swap(block):
    return lax.ppermute(block, "box", [(i ^ 1, i) for i in range(lax.axis_size("box"))])


def meet(block, odd):
    count = lax.axis_size("box")
    chips = [((k + odd ^ 1) - odd) % (count // 2) for k in range(count // 2)]
    return lax.ppermute(block, "box", [(2 * chips[i // 2] + i % 2, i) for i in range(count)])


def around(block, place, beside=None):
    low_pair, high_pair = meet(block, 1), meet(block, 0)
    first = swap(block)
    onward = jnp.where(place[1] == place[2], high_pair, low_pair)
    if beside is not None:
        onward, beside = lax.optimization_barrier((onward, beside))
    return [high_pair, swap(onward), block, first, low_pair], beside


def shards(volume, drag, momentum, offsets, cell_index, destinations, rhs, wall):
    box = lax.axis_index("box").astype(I32)
    place = jnp.stack([lax.axis_index("slab").astype(I32), box % 2, box // 2 % 2])
    prev = fetch(jnp.concatenate([rhs[7:], wall[7:].astype(F32)], axis=0), -1)
    one = (1, PART)
    (outgoing,) = call(
        route_kernel,
        [(N_BOX, 1, 8 * CAP)],
        [(one, F32), (one, F32), ((2, PART), F32), ((3, PART), F32), (one, I32), (one, I32),
         ((24 * CAP, PART), BF16), ((N_BOX, 8 * CAP), F32), pltpu.SemaphoreType.DMA((6,))],
        [volume.reshape(one), drag.reshape(one), momentum, offsets, cell_index.reshape(one), destinations.reshape(one)],
        in_hbm=True,
        limit=62 * 1024 * 1024,
    )
    incoming = lax.all_to_all(outgoing, "box", split_axis=0, concat_axis=0, tiled=True)
    pay, craw = call(
        deposit_kernel,
        [(3 * XE + XE // 2, 8, NZ), (3, XE, 8, NZ)],
        [((13, CAP, NZ), F32), ((3, CAP, NZ), I32), ((XE, CAP, NZ), F32), ((768, NZ), F32)]
        + [((768, SLOTS // CHUNKS), BF16)] * CHUNKS + [((NZ, SLOTS // CHUNKS), BF16)] * CHUNKS,
        [incoming.reshape(N_BOX, 8 * CAP), rhs, wall, prev],
    )
    slabs = lax.all_gather(pay, "slab")
    sums = [((HEAD * 32, NZ), F32)] * 2
    (head,) = call(head_kernel, [(8 * HEAD + 3, 8, NZ)], sums, [slabs])
    next_head = fetch(head, 1)
    late, keep = call(
        late_kernel, [(8 * LATE + 28, 8, NZ), (43, 8, NZ)], sums, [place, slabs, craw], smem_first=True
    )
    next_late = fetch(late, 1)
    fine, mid, low = (T0, 4, 8, NZ), (T1, 8, NZ), (T2, 8, NZ)
    cc, cb, gg, v2, first = call(
        start_kernel, [fine, fine, (CX, 4, 8, NZ), fine, (28, 8, NZ)], [], [head, late, keep, next_head]
    )
    deposits, cc_r, cb_r, v2_r = call(
        rest_kernel,
        [(4, CX, 8, NZ), (10, 4, 8, NZ), (10, 4, 8, NZ), (12, 4, 8, NZ)],
        [((CX * 32, NZ), F32)],
        [place, head, late, keep, next_head, next_late, cc, cb],
        smem_first=True,
    )
    scratch = [(mid, F32), (mid, F32), (mid, F32), (low, F32), (low, F32), (low, F32), (fine, F32), (fine, F32)]
    parts, deposits = around(first, place, deposits)
    v3, c1, g1, c2, second = call(
        middle_kernel,
        [fine, mid, mid, low, (8, 8, NZ)],
        scratch,
        [place] + parts + [cc, cb, gg, v2, cc_r, cb_r, v2_r],
        smem_first=True,
    )
    parts, _ = around(second, place)
    pressure, coupled = call(
        last_kernel,
        [(CX, 8, NZ), (4, CX, 8, NZ)],
        scratch + [((CX * 32, NZ), F32), pltpu.SemaphoreType.DMA],
        [place] + parts + [cc, cb, v3, c1, g1, c2, deposits],
        smem_first=True,
        outs_hbm=1,
    )
    return coupled, pressure


def solution(mesh):
    in_specs = (
        P(("box", "slab")),
        P(("box", "slab")),
        P(None, ("box", "slab")),
        P(None, ("box", "slab")),
        P(("box", "slab")),
        P(("box", "slab"), None),
        P("box", "slab", None),
        P("box", "slab", None),
    )
    out_specs = (P(None, "box", "slab", None), P("box", "slab", None))
    return jax.shard_map(shards, mesh=mesh, in_specs=in_specs, out_specs=out_specs, check_vma=False)
```

```python
import jax
import jax.numpy as jnp
from jax import lax
from jax.experimental import pallas as pl
from jax.experimental.pallas import tpu as pltpu
from jax.sharding import PartitionSpec as P

F32 = jnp.float32
BF16 = jnp.bfloat16
I32 = jnp.int32

CX, CY, NZ = 16, 8, 128
PART = 2048
N_BOX = 128
CAP = 32
SLOTS = N_BOX * CAP
XE = CX + 2
OMEGA = 0.8

T0, T1, T2 = 30, 40, 20

OTHERS = (0, 2, 3)
CHUNKS = 8

LIMIT = 24 * 1024 * 1024

NT = (((1,), (1,)), ((), ()))


def tap_weights(frac):
    return (
        0.5 * (0.5 - frac) * (0.5 - frac),
        0.75 - frac * frac,
        0.5 * (0.5 + frac) * (0.5 + frac),
    )


def spread(index, at, taps):
    return jnp.where(
        index == at,
        taps[0],
        jnp.where(index == at + 1, taps[1], jnp.where(index == at + 2, taps[2], 0.0)),
    )


def route_kernel(vol_in, drag_in, mom_in, off_in, cell_in, dest_in, out, vol, drag, mom, off, cell, dest, picked, ordered, sems):
    pairs = ((dest_in, dest), (vol_in, vol), (drag_in, drag), (mom_in, mom), (off_in, off), (cell_in, cell))
    copies = [pltpu.make_async_copy(a, b, sems.at[k]) for k, (a, b) in enumerate(pairs)]
    for copy in copies:
        copy.start()
    copies[0].wait()
    target = dest[...]
    hot = lax.broadcasted_iota(I32, (N_BOX, PART), 0) == target
    hot_f = jnp.where(hot, 1.0, 0.0)
    hot_b = hot_f.astype(BF16)
    width = 256
    above = lax.broadcasted_iota(I32, (width, width), 0) < lax.broadcasted_iota(I32, (width, width), 1)
    before = jnp.where(above, 1.0, 0.0).astype(BF16)
    carry = jnp.zeros((N_BOX, 1), F32)
    places = []
    for k in range(PART // width):
        cut = slice(k * width, (k + 1) * width)
        rank = jnp.dot(hot_b[:, cut], before, preferred_element_type=F32) + carry
        places.append(jnp.sum(rank * hot_f[:, cut], axis=0, keepdims=True))
        carry = carry + jnp.sum(hot_f[:, cut], axis=1, keepdims=True)
    place = jnp.concatenate(places, axis=1).astype(I32)
    at_place = lax.broadcasted_iota(I32, (CAP, PART), 0) == place
    for copy in copies[1:]:
        copy.wait()
    fields = [vol[...], drag[...], mom[0:1, :], mom[1:2, :]]
    fields += [off[0:1, :], off[1:2, :], off[2:3, :], cell[...].astype(F32)]
    for f, left in enumerate(fields):
        for part in range(3):
            rounded = left.astype(BF16).astype(F32)
            row = (part * 8 + f) * CAP
            picked[row : row + CAP, :] = jnp.where(at_place, rounded, 0.0).astype(BF16)
            left = left - rounded
    sums = lax.dot_general(picked[...], hot_b, NT, preferred_element_type=F32)
    half = 8 * CAP
    sums = sums[:half] + sums[half : 2 * half] + sums[2 * half :]
    ordered[...] = sums.T
    for r in range(N_BOX):
        out[r] = ordered[r : r + 1, :]


def deposit_kernel(recv, rhs, wall, prev, pay, craw, par, cells, xs, acc, *mats):
    amats, vmats = mats[:CHUNKS], mats[CHUNKS:]
    fields = recv[...].T
    for c in range(4):
        par[c] = fields[c * CAP : (c + 1) * CAP]
    cell = fields[7 * CAP :].astype(I32)
    x_cell = cell // (NZ * CY)
    cells[0] = x_cell
    cells[1] = (cell // NZ) % CY
    cells[2] = cell % NZ
    for d in range(3):
        for k, tap in enumerate(tap_weights(fields[(4 + d) * CAP : (5 + d) * CAP])):
            par[4 + 3 * d + k] = tap
    for x in range(XE):
        xs[x] = spread(x, x_cell, (par[4], par[5], par[6]))
    sub24 = lax.broadcasted_iota(I32, (24, NZ), 0)
    sub8 = lax.broadcasted_iota(I32, (8, NZ), 0)
    sub128 = lax.broadcasted_iota(I32, (NZ, NZ), 0)

    def one(w, amat, vmat, at):
        def row(k):
            return par[k, w : w + 1, :]

        lanes = slice(at, at + NZ)
        vals = [row(c) for c in range(4)]
        wx = [row(4 + k) for k in range(3)]
        wy = [row(7 + k) for k in range(3)]
        wz = [row(10 + k) for k in range(3)]
        xc, yc, zc = [cells[d, w : w + 1, :] for d in range(3)]
        y_tile = spread(sub8, yc - 1, wy)
        low = jnp.where(yc == 0, wy[0], 0.0)
        high = jnp.where(yc == CY - 1, wy[2], 0.0)
        x_tile = spread(sub24, xc, wx)
        edge = jnp.concatenate([x_tile * low, x_tile * high], axis=0)
        for c in range(4):
            amat[576 + 48 * c : 576 + 48 * (c + 1), lanes] = (vals[c] * edge).astype(BF16)
        for pair in range(XE // 2):
            plane = jnp.concatenate([xs[2 * pair + k, w : w + 1, :] * y_tile for k in range(2)], axis=0)
            for c in range(4):
                r = 144 * c + 16 * pair
                amat[r : r + 16, lanes] = (vals[c] * plane).astype(BF16)
        vmat[:, lanes] = spread(sub128, zc - 1, wz).astype(BF16)

    each = CAP // CHUNKS
    for n in range(CHUNKS):
        for k in range(each):
            one(n * each + k, amats[n], vmats[n], k * NZ)
        part = lax.dot_general(amats[n][...], vmats[n][...], NT, preferred_element_type=F32)
        acc[:768, :] = part if n == 0 else acc[:768, :] + part
    for x in range(XE):
        c = [acc[144 * k + 8 * x : 144 * k + 8 * x + 8, :] for k in range(4)]
        for k, channel in enumerate(OTHERS):
            craw[k, x] = c[channel]
        if x < 9:
            right, opened = prev[x], prev[9 + x]
        else:
            right, opened = rhs[x - 9], wall[x - 9].astype(F32)
        whole = right - c[0] * right if x < CX else -(c[0] * right)
        pay[x] = opened * (whole + c[2] + c[3])
        pay[XE + x] = c[1]
        pay[2 * XE + x] = acc[pl.ds(576 + x, 8, stride=24), :]
        extra = jnp.concatenate([right[0:1], right[7:8], opened[0:1], opened[4:5]], axis=0)
        pay[3 * XE + x // 2, (x % 2) * 4 : (x % 2) * 4 + 4, :] = extra


HEAD = 11
LATE = CX - HEAD


def slab_sums(got, rows, ssum, dsum):
    sub = lax.broadcasted_iota(I32, (8, NZ), 0)
    for n, x in enumerate(rows):
        g_row = (x % 2) * 4
        halos = [got[s, 2 * XE + x] for s in range(4)]
        for s in range(4):
            below, above = halos[(s + 3) % 4], halos[(s + 1) % 4]
            extra = got[s, 3 * XE + x // 2]
            rhs_f, rhs_l = extra[g_row : g_row + 1], extra[g_row + 1 : g_row + 2]
            o_f, o_l = extra[g_row + 2 : g_row + 3], extra[g_row + 3 : g_row + 4]
            from_below = o_f * (below[5:6] + below[7:8] - below[1:2] * rhs_f)
            from_above = o_l * (above[4:5] + above[6:7] - above[0:1] * rhs_l)
            at = n * 32 + s * 8
            ssum[at : at + 8, :] = edges(sub, got[s, x], from_below, from_above)
            dsum[at : at + 8, :] = edges(sub, got[s, XE + x], below[3:4], above[2:3])


def edges(sub, tile, to_first, to_last):
    return tile + jnp.where(sub == 0, to_first, 0.0) + jnp.where(sub == 7, to_last, 0.0)


def opened_block(got, x, out, at):
    g_row = (x % 2) * 4
    for s in range(4):
        out[at, 2 * s : 2 * s + 2, :] = got[s, 3 * XE + x // 2, g_row + 2 : g_row + 4, :]


def head_kernel(got, head, ssum, dsum):
    slab_sums(got, range(HEAD), ssum, dsum)
    for x in range(HEAD):
        for q in range(4):
            head[4 * x + q] = ssum[pl.ds(x * 32 + q, 8, stride=4), :]
            head[4 * (HEAD + x) + q] = dsum[pl.ds(x * 32 + q, 8, stride=4), :]
    for k, x in enumerate((1, 5, 9)):
        opened_block(got, x, head, 8 * HEAD + k)


def late_kernel(place, got, craw, late, keep, ssum, dsum):
    s_me = place[0]
    sub = lax.broadcasted_iota(I32, (8, NZ), 0)
    slab_sums(got, range(HEAD, XE), ssum, dsum)
    for n in range(XE - HEAD):
        for q in range(4):
            s_tile = ssum[pl.ds(n * 32 + q, 8, stride=4), :]
            d_tile = dsum[pl.ds(n * 32 + q, 8, stride=4), :]
            if n < LATE:
                late[4 * n + q] = s_tile
                late[4 * (LATE + n) + q] = d_tile
            else:
                keep[4 * (n - LATE) + q] = s_tile
                keep[4 * (n - LATE + 2) + q] = d_tile
    for x in range(XE):
        below = got[(s_me + 3) % 4, 2 * XE + x]
        above = got[(s_me + 1) % 4, 2 * XE + x]
        for k, c in enumerate(OTHERS):
            tile = edges(sub, craw[k, x], below[2 * c + 1 : 2 * c + 2], above[2 * c : 2 * c + 1])
            if x < 9:
                late[8 * LATE + 9 * k + x] = tile
            else:
                keep[16 + 9 * k + x - 9] = tile
    opened_block(got, 13, late, 8 * LATE + 27)


class Parts:
    def __init__(self, own_head, own_late, keep, next_head, next_late=None):
        self.own = (own_head, own_late, keep)
        self.next = (next_head, next_late)

    @staticmethod
    def tile(parts, x, kind, q):
        if x < HEAD:
            return parts[0][4 * (HEAD * kind + x) + q]
        if x < CX:
            return parts[1][4 * (LATE * kind + x - HEAD) + q]
        return parts[2][4 * (2 * kind + x - CX) + q]

    def joined(self, t, kind, q):
        if t < 14:
            return self.tile(self.own, t + 2, kind, q)
        other = self.tile(self.next, t - 14, kind, q)
        return other if t > 15 else other + self.tile(self.own, t + 2, kind, q)

    def opened(self, block):
        head, late = (self.own if block < 4 else self.next)[:2]
        k = block % 4
        return head[8 * HEAD + k] if k < 3 else late[8 * LATE + 27]

    def coefficient(self, t, q):
        diag = 6.0 + self.joined(t, 1, q)
        coef = OMEGA * self.opened((t + 1) // 4) * pl.reciprocal(diag)
        return coef, coef * self.joined(t, 0, q), diag


class Rows:
    def __init__(self, mid, rest, low, high):
        self.mid, self.rest, self.low, self.high = mid, rest, low, high

    def place(self, index):
        t, q = index
        if self.low <= t < self.high:
            return self.mid, (t, q)
        return self.rest, (t if t < self.low else t - self.high + self.low, q)

    def __getitem__(self, index):
        ref, at = self.place(index)
        return ref[at]

    def __setitem__(self, index, tile):
        ref, at = self.place(index)
        ref[at] = tile


def lane_index():
    return lax.broadcasted_iota(I32, (8, NZ), 1)


def take(tile, index):
    return jnp.take_along_axis(tile, index, axis=1)


def fine_sums(ref, t):
    lane = lane_index()
    cur = [ref[t, q] for q in range(4)]
    sums = []
    for q in range(4):
        after = cur[q + 1] if q < 3 else pltpu.roll(cur[0], 7, 0)
        before = cur[q - 1] if q else pltpu.roll(cur[3], 1, 0)
        left = jnp.where(lane == 0, 0.0, pltpu.roll(cur[q], 1, 1))
        right = jnp.where(lane == NZ - 1, 0.0, pltpu.roll(cur[q], NZ - 1, 1))
        sums.append((ref[t - 1, q] + ref[t + 1, q]) + (after + before) + (left + right))
    return cur, sums


def fine_sweep(src, dst, coef, base, low, high):
    for t in range(low, high):
        cur, sums = fine_sums(src, t)
        for q in range(4):
            dst[t, q] = (1.0 - OMEGA) * cur[q] + base[t, q] + coef[t, q] * sums[q]


def fine_residue(src, coef, base, weight):
    rows = []
    for k in range(8):
        total = [0.0, 0.0]
        for dx in range(2):
            t = 7 + 2 * k + dx
            cur, sums = fine_sums(src, t)
            for q in range(4):
                tile = weight[2 * k + dx, q] * (base[t, q] + coef[t, q] * sums[q] - OMEGA * cur[q])
                total[q // 2] = total[q // 2] + tile
        rows.append(jnp.concatenate(total, axis=1))
    return jnp.concatenate(rows, axis=0)


def choice(size, match):
    row = lax.broadcasted_iota(I32, (size, NZ), 0)
    column = lax.broadcasted_iota(I32, (size, NZ), 1)
    return jnp.where(match(row, column), 1.0, 0.0).astype(BF16)


def lane_sums(block, chosen):
    out, left = 0.0, block
    for _ in range(3):
        part = left.astype(BF16)
        out = out + jnp.dot(part, chosen, preferred_element_type=F32)
        left = left - part.astype(F32)
    return out


def pairs_packed():
    return choice(256, lambda r, c: r // 2 == c)


def fine_correct(v_in, v_out, w, coef, low, high):
    lane = lane_index()
    for a in range(low, high):
        for half in range(2):
            step = take(w[a], lane // 2 + 64 * half)
            for dx in range(2):
                t = 2 * a - 25 + dx
                for q in (2 * half, 2 * half + 1):
                    v_out[t, q] = v_in[t, q] + jnp.where(coef[t, q] > 0.0, step, 0.0)


def mid_sums(ref, a):
    lane = lane_index()
    cur = ref[a]
    turned = pltpu.roll(cur, 64, 1)
    beside = turned + jnp.where(lane < 64, pltpu.roll(turned, 1, 0), pltpu.roll(turned, 7, 0))
    left = jnp.where(lane % 64 == 0, 0.0, pltpu.roll(cur, 1, 1))
    right = jnp.where(lane % 64 == 63, 0.0, pltpu.roll(cur, NZ - 1, 1))
    return cur, (ref[a - 1] + ref[a + 1]) + beside + (left + right)


def mid_sweep(src, dst, coef, base, low, high):
    for a in range(low, high):
        cur, total = mid_sums(src, a)
        dst[a] = (1.0 - OMEGA) * cur + base[a] + coef[a] * total


def low_sweep(src, dst, coef, base, low, high):
    for m in range(low, high):
        cur = src[m]
        total = (src[m - 1] + src[m + 1]) + (pltpu.roll(cur, 1, 0) + pltpu.roll(cur, 7, 0))
        total = total + (pltpu.roll(cur, 1, 1) + pltpu.roll(cur, NZ - 1, 1))
        dst[m] = (1.0 - OMEGA) * cur + base[m] + coef[m] * total


def levels_solve(c1, g1, c2, cb1, w_a, w_b, cb2, u_a, u_b):
    lane = lane_index()
    mid_sweep(cb1, w_a, c1, cb1, 3, 37)
    totals = []
    for m in range(2, 18):
        total = 0.0
        for a in (2 * m, 2 * m + 1):
            cur, beside = mid_sums(w_a, a)
            total = total + g1[a] * (cb1[a] + c1[a] * beside - OMEGA * cur)
        totals.append(total)
    below = lane_sums(jnp.concatenate(totals, axis=0), choice(NZ, lambda r, c: r % 64 // 2 == c))
    for m in range(2, 18):
        cb2[m] = 2.0 * c2[m] * below[8 * (m - 2) : 8 * (m - 1)]
    low_sweep(cb2, u_a, c2, cb2, 3, 17)
    low_sweep(u_a, u_b, c2, cb2, 4, 16)
    low_sweep(u_b, u_a, c2, cb2, 5, 15)
    for m in range(5, 15):
        step = take(u_a[m], (lane % 64) // 2)
        for a in (2 * m, 2 * m + 1):
            w_a[a] = w_a[a] + jnp.where(c1[a] > 0.0, step, 0.0)
    mid_sweep(w_a, w_b, c1, cb1, 12, 28)
    mid_sweep(w_b, w_a, c1, cb1, 13, 27)


def rest_kernel(place, own_head, own_late, keep, next_head, next_late, cc, cb, coupled, cc_r, cb_r, v2_r, gg, flat):
    parts = Parts(own_head, own_late, keep, next_head, next_late)
    for k, c in enumerate(OTHERS):
        for x in range(CX):
            own, other = 16 + 9 * k + x, 8 * LATE + 9 * k + x - 7
            if x < 7:
                tile = keep[own]
            elif x < 9:
                tile = keep[own] + next_late[other]
            else:
                tile = next_late[other]
            coupled[c, x] = tile
    for x in range(CX):
        for q in range(4):
            flat[pl.ds(x * 32 + q, 8, stride=4), :] = parts.joined(7 + x, 1, q)
    for x in range(CX):
        coupled[1, x] = flat[pl.ds(pl.multiple_of(x * 32 + 8 * place[0], 8), 8), :]
    coefs, bases, v2 = Rows(cc, cc_r, 5, 25), Rows(cb, cb_r, 5, 25), Rows(None, v2_r, 6, 24)
    for t in (*range(5), *range(25, T0)):
        for q in range(4):
            coefs[t, q], bases[t, q], _ = parts.coefficient(t, q)
    fine_sweep(bases, v2, coefs, bases, 1, 6)
    fine_sweep(bases, v2, coefs, bases, 24, 29)
    for t in range(7, 23):
        for q in range(4):
            gg[t - 7, q] = (1.0 / OMEGA) * (6.0 + parts.joined(t, 1, q))


def start_kernel(own_head, own_late, keep, next_head, cc, cb, v2, send, gg):
    parts = Parts(own_head, own_late, keep, next_head)
    for t in range(5, 25):
        for q in range(4):
            cc[t, q], cb[t, q], diag = parts.coefficient(t, q)
            if 7 <= t < 23:
                gg[t - 7, q] = (1.0 / OMEGA) * diag
    fine_sweep(cb, v2, cc, cb, 6, 24)
    damps = []
    for k in range(8):
        total = [0.0, 0.0]
        for dx in range(2):
            for q in range(4):
                total[q // 2] = total[q // 2] + parts.joined(7 + 2 * k + dx, 1, q)
        damps.append(jnp.concatenate(total, axis=1))
    lows = [damps[2 * m] + damps[2 * m + 1] for m in range(4)]
    opened = jnp.concatenate([parts.opened(2 + m) for m in range(4)], axis=0).astype(BF16)
    opened_1 = jnp.dot(opened, choice(NZ, lambda r, c: r == c % 64 * 2), preferred_element_type=F32)
    opened_2 = jnp.dot(opened, choice(NZ, lambda r, c: r == c * 4), preferred_element_type=F32)
    packed = pairs_packed()
    diag = 1.5 + 0.125 * lane_sums(jnp.concatenate(damps, axis=0), packed)
    low_diag = 0.375 + 0.015625 * lane_sums(
        jnp.concatenate(lows, axis=0), choice(256, lambda r, c: r % NZ // 4 == c)
    )
    source = 0.125 * lane_sums(fine_residue(v2, cc, cb, gg), packed)
    inverse = OMEGA * pl.reciprocal(diag)
    below = (0.0625 * OMEGA) * opened_2 * pl.reciprocal(low_diag)
    for k in range(8):
        rows = slice(8 * k, 8 * k + 8)
        coef = opened_1[8 * (k // 2) : 8 * (k // 2) + 8] * inverse[rows]
        send[k] = coef * source[rows]
        send[8 + k] = 0.25 * coef
        send[16 + k] = (1.0 / OMEGA) * diag[rows]
    for m in range(4):
        send[24 + m] = below[8 * m : 8 * m + 8]


def window(place, high_pair, both, own, low_pair):
    even_core, even_chip = place[1] == 0, place[2] == 0
    size = own.shape[0]

    def part(n, k):
        if n == 2:
            return own[k]
        if n in (1, 3):
            return jnp.where(even_core == (n == 1), both[size + k], both[k])
        return jnp.where(even_chip == (n == 0), low_pair[k], high_pair[k])

    return part


def middle_kernel(place, high_pair, both, own, low_pair, cc, cb, gg, v2, cc_r, cb_r, v2_r, v_out, c1, g1, c2, send,
                  cb1, w_a, w_b, cb2, u_a, u_b, v_a, v_b):
    part = window(place, high_pair, both, own, low_pair)
    for n in range(5):
        for k in range(8):
            cb1[8 * n + k] = part(n, k)
            c1[8 * n + k] = part(n, 8 + k)
            g1[8 * n + k] = part(n, 16 + k)
        for k in range(4):
            c2[4 * n + k] = part(n, 24 + k)
    levels_solve(c1, g1, c2, cb1, w_a, w_b, cb2, u_a, u_b)
    cc, cb, v2 = Rows(cc, cc_r, 5, 25), Rows(cb, cb_r, 5, 25), Rows(v2, v2_r, 6, 24)
    fine_correct(v2, v_a, w_a, cc, 13, 27)
    fine_sweep(v_a, v_b, cc, cb, 2, 28)
    fine_sweep(v_b, v_a, cc, cb, 3, 27)
    fine_sweep(v_a, v_b, cc, cb, 4, 26)
    fine_sweep(v_b, v_out, cc, cb, 5, 25)
    source = lane_sums(fine_residue(v_out, cc, cb, gg), pairs_packed())
    for k in range(8):
        send[k] = 0.5 * c1[16 + k] * source[8 * k : 8 * k + 8]


def last_kernel(place, high_pair, both, own, low_pair, cc, cb, v2, c1, g1, c2, deposits, out, coupled,
                cb1, w_a, w_b, cb2, u_a, u_b, v_a, v_b, flat, sem):
    copy = pltpu.make_async_copy(deposits, coupled, sem)
    copy.start()
    part = window(place, high_pair, both, own, low_pair)
    for n in range(5):
        for k in range(8):
            cb1[8 * n + k] = part(n, k)
    levels_solve(c1, g1, c2, cb1, w_a, w_b, cb2, u_a, u_b)
    fine_correct(v2, v_a, w_a, cc, 15, 25)
    fine_sweep(v_a, v_b, cc, cb, 6, 24)
    fine_sweep(v_b, v_a, cc, cb, 7, 23)
    for x in range(CX):
        for q in range(4):
            flat[pl.ds(x * 32 + q, 8, stride=4), :] = v_a[7 + x, q]
    for x in range(CX):
        out[x] = flat[pl.ds(pl.multiple_of(x * 32 + 8 * place[0], 8), 8), :]
    copy.wait()


def call(kernel, outs, scratch, operands, smem_first=False, in_hbm=False, outs_hbm=0, cost=1000000, limit=LIMIT):
    kind = pltpu.HBM if in_hbm else pltpu.VMEM
    specs = [pl.BlockSpec(memory_space=kind) for _ in operands]
    if smem_first:
        specs[0] = pl.BlockSpec(memory_space=pltpu.SMEM)
    shapes = [jax.ShapeDtypeStruct(shape, F32) for shape in outs]
    return pl.pallas_call(
        kernel,
        out_shape=shapes,
        in_specs=specs,
        out_specs=[
            pl.BlockSpec(memory_space=pltpu.VMEM if n < len(outs) - outs_hbm else pltpu.HBM) for n in range(len(outs))
        ],
        scratch_shapes=[pltpu.VMEM(*piece) if isinstance(piece, tuple) else piece for piece in scratch],
        compiler_params=pltpu.CompilerParams(vmem_limit_bytes=limit),
        cost_estimate=pl.CostEstimate(flops=cost, bytes_accessed=cost, transcendentals=0),
    )(*operands)


def fetch(block, distance):
    count = lax.axis_size("box")
    return lax.ppermute(block, "box", [((i + distance) % count, i) for i in range(count)])


def swap(block):
    return lax.ppermute(block, "box", [(i ^ 1, i) for i in range(lax.axis_size("box"))])


def meet(block, odd):
    count = lax.axis_size("box")
    chips = [((k + odd ^ 1) - odd) % (count // 2) for k in range(count // 2)]
    return lax.ppermute(block, "box", [(2 * chips[i // 2] + i % 2, i) for i in range(count)])


def around(block, place, beside=None):
    low_pair, high_pair = meet(block, 1), meet(block, 0)
    onward = jnp.concatenate([block, jnp.where(place[1] == place[2], high_pair, low_pair)], axis=0)
    if beside is not None:
        onward, beside = lax.optimization_barrier((onward, beside))
    return [high_pair, swap(onward), block, low_pair], beside


def shards(volume, drag, momentum, offsets, cell_index, destinations, rhs, wall):
    box = lax.axis_index("box").astype(I32)
    place = jnp.stack([lax.axis_index("slab").astype(I32), box % 2, box // 2 % 2])
    prev = fetch(jnp.concatenate([rhs[7:], wall[7:].astype(F32)], axis=0), -1)
    one = (1, PART)
    (outgoing,) = call(
        route_kernel,
        [(N_BOX, 1, 8 * CAP)],
        [(one, F32), (one, F32), ((2, PART), F32), ((3, PART), F32), (one, I32), (one, I32),
         ((24 * CAP, PART), BF16), ((N_BOX, 8 * CAP), F32), pltpu.SemaphoreType.DMA((6,))],
        [volume.reshape(one), drag.reshape(one), momentum, offsets, cell_index.reshape(one), destinations.reshape(one)],
        in_hbm=True,
        limit=62 * 1024 * 1024,
    )
    incoming = lax.all_to_all(outgoing, "box", split_axis=0, concat_axis=0, tiled=True)
    pay, craw = call(
        deposit_kernel,
        [(3 * XE + XE // 2, 8, NZ), (3, XE, 8, NZ)],
        [((13, CAP, NZ), F32), ((3, CAP, NZ), I32), ((XE, CAP, NZ), F32), ((800, NZ), F32)]
        + [((768, SLOTS // CHUNKS), BF16)] * CHUNKS + [((NZ, SLOTS // CHUNKS), BF16)] * CHUNKS,
        [incoming.reshape(N_BOX, 8 * CAP), rhs, wall, prev],
    )
    slabs = lax.all_gather(pay, "slab")
    sums = [((HEAD * 32 + 8, NZ), F32)] * 2
    (head,) = call(head_kernel, [(8 * HEAD + 3, 8, NZ)], sums, [slabs])
    next_head = fetch(head, 1)
    late, keep = call(
        late_kernel, [(8 * LATE + 28, 8, NZ), (43, 8, NZ)], sums, [place, slabs, craw], smem_first=True
    )
    next_late = fetch(late, 1)
    fine, mid, low = (T0, 4, 8, NZ), (T1, 8, NZ), (T2, 8, NZ)
    weights = (CX, 4, 8, NZ)
    cc, cb, v2, first = call(
        start_kernel, [fine, fine, fine, (28, 8, NZ)], [(weights, F32)], [head, late, keep, next_head]
    )
    deposits, cc_r, cb_r, v2_r, gg = call(
        rest_kernel,
        [(4, CX, 8, NZ), (10, 4, 8, NZ), (10, 4, 8, NZ), (12, 4, 8, NZ), weights],
        [((CX * 32 + 8, NZ), F32)],
        [place, head, late, keep, next_head, next_late, cc, cb],
        smem_first=True,
    )
    scratch = [(mid, F32), (mid, F32), (mid, F32), (low, F32), (low, F32), (low, F32), (fine, F32), (fine, F32)]
    parts, deposits = around(first, place, deposits)
    v3, c1, g1, c2, second = call(
        middle_kernel,
        [fine, mid, mid, low, (8, 8, NZ)],
        scratch,
        [place] + parts + [cc, cb, gg, v2, cc_r, cb_r, v2_r],
        smem_first=True,
    )
    parts, _ = around(second, place)
    pressure, coupled = call(
        last_kernel,
        [(CX, 8, NZ), (4, CX, 8, NZ)],
        scratch + [((CX * 32 + 8, NZ), F32), pltpu.SemaphoreType.DMA],
        [place] + parts + [cc, cb, v3, c1, g1, c2, deposits],
        smem_first=True,
        outs_hbm=1,
    )
    return coupled, pressure


def solution(mesh):
    in_specs = (
        P(("box", "slab")),
        P(("box", "slab")),
        P(None, ("box", "slab")),
        P(None, ("box", "slab")),
        P(("box", "slab")),
        P(("box", "slab"), None),
        P("box", "slab", None),
        P("box", "slab", None),
    )
    out_specs = (P(None, "box", "slab", None), P("box", "slab", None))
    return jax.shard_map(shards, mesh=mesh, in_specs=in_specs, out_specs=out_specs, check_vma=False)
```

```python
import jax
import jax.numpy as jnp
from jax import lax
from jax.experimental import pallas as pl
from jax.experimental.pallas import tpu as pltpu
from jax.sharding import PartitionSpec as P

F32 = jnp.float32
BF16 = jnp.bfloat16
I32 = jnp.int32

CX, CY, NZ = 16, 8, 128
PART = 2048
N_BOX = 128
CAP = 32
SLOTS = N_BOX * CAP
XE = CX + 2
OMEGA = 0.8

T0, T1, T2 = 30, 40, 20

OTHERS = (0, 2, 3)
CHUNKS = 8

LIMIT = 24 * 1024 * 1024

NT = (((1,), (1,)), ((), ()))


def tap_weights(frac):
    return (
        0.5 * (0.5 - frac) * (0.5 - frac),
        0.75 - frac * frac,
        0.5 * (0.5 + frac) * (0.5 + frac),
    )


def spread(index, at, taps):
    return jnp.where(
        index == at,
        taps[0],
        jnp.where(index == at + 1, taps[1], jnp.where(index == at + 2, taps[2], 0.0)),
    )


def route_kernel(vol_in, drag_in, mom_in, off_in, cell_in, dest_in, out, vol, drag, mom, off, cell, dest, picked, ordered, sems):
    pairs = ((dest_in, dest), (vol_in, vol), (drag_in, drag), (mom_in, mom), (off_in, off), (cell_in, cell))
    copies = [pltpu.make_async_copy(a, b, sems.at[k]) for k, (a, b) in enumerate(pairs)]
    for copy in copies:
        copy.start()
    copies[0].wait()
    target = dest[...]
    hot = lax.broadcasted_iota(I32, (N_BOX, PART), 0) == target
    hot_f = jnp.where(hot, 1.0, 0.0)
    hot_b = hot_f.astype(BF16)
    width = 256
    above = lax.broadcasted_iota(I32, (width, width), 0) < lax.broadcasted_iota(I32, (width, width), 1)
    before = jnp.where(above, 1.0, 0.0).astype(BF16)
    carry = jnp.zeros((N_BOX, 1), F32)
    places = []
    for k in range(PART // width):
        cut = slice(k * width, (k + 1) * width)
        rank = jnp.dot(hot_b[:, cut], before, preferred_element_type=F32) + carry
        places.append(jnp.sum(rank * hot_f[:, cut], axis=0, keepdims=True))
        carry = carry + jnp.sum(hot_f[:, cut], axis=1, keepdims=True)
    place = jnp.concatenate(places, axis=1).astype(I32)
    at_place = lax.broadcasted_iota(I32, (CAP, PART), 0) == place
    for copy in copies[1:]:
        copy.wait()
    fields = [vol[...], drag[...], mom[0:1, :], mom[1:2, :]]
    fields += [off[0:1, :], off[1:2, :], off[2:3, :], cell[...].astype(F32)]
    for f, left in enumerate(fields):
        for part in range(3):
            rounded = left.astype(BF16).astype(F32)
            row = (part * 8 + f) * CAP
            picked[row : row + CAP, :] = jnp.where(at_place, rounded, 0.0).astype(BF16)
            left = left - rounded
    sums = lax.dot_general(picked[...], hot_b, NT, preferred_element_type=F32)
    half = 8 * CAP
    sums = sums[:half] + sums[half : 2 * half] + sums[2 * half :]
    ordered[...] = sums.T
    for r in range(N_BOX):
        out[r] = ordered[r : r + 1, :]


def deposit_kernel(recv, rhs, wall, prev, pay, craw, par, cells, xs, acc, *mats):
    amats, vmats = mats[:CHUNKS], mats[CHUNKS:]
    fields = recv[...].T
    for c in range(4):
        par[c] = fields[c * CAP : (c + 1) * CAP]
    cell = fields[7 * CAP :].astype(I32)
    x_cell = cell // (NZ * CY)
    cells[0] = x_cell
    cells[1] = (cell // NZ) % CY
    cells[2] = cell % NZ
    for d in range(3):
        for k, tap in enumerate(tap_weights(fields[(4 + d) * CAP : (5 + d) * CAP])):
            par[4 + 3 * d + k] = tap
    for x in range(XE):
        xs[x] = spread(x, x_cell, (par[4], par[5], par[6]))
    sub24 = lax.broadcasted_iota(I32, (24, NZ), 0)
    sub8 = lax.broadcasted_iota(I32, (8, NZ), 0)
    sub128 = lax.broadcasted_iota(I32, (NZ, NZ), 0)

    def one(w, amat, vmat, at):
        def row(k):
            return par[k, w : w + 1, :]

        lanes = slice(at, at + NZ)
        vals = [row(c) for c in range(4)]
        wx = [row(4 + k) for k in range(3)]
        wy = [row(7 + k) for k in range(3)]
        wz = [row(10 + k) for k in range(3)]
        xc, yc, zc = [cells[d, w : w + 1, :] for d in range(3)]
        y_tile = spread(sub8, yc - 1, wy)
        low = jnp.where(yc == 0, wy[0], 0.0)
        high = jnp.where(yc == CY - 1, wy[2], 0.0)
        x_tile = spread(sub24, xc, wx)
        edge = jnp.concatenate([x_tile * low, x_tile * high], axis=0)
        for c in range(4):
            amat[576 + 48 * c : 576 + 48 * (c + 1), lanes] = (vals[c] * edge).astype(BF16)
        for pair in range(XE // 2):
            plane = jnp.concatenate([xs[2 * pair + k, w : w + 1, :] * y_tile for k in range(2)], axis=0)
            for c in range(4):
                r = 144 * c + 16 * pair
                amat[r : r + 16, lanes] = (vals[c] * plane).astype(BF16)
        vmat[:, lanes] = spread(sub128, zc - 1, wz).astype(BF16)

    each = CAP // CHUNKS
    for n in range(CHUNKS):
        for k in range(each):
            one(n * each + k, amats[n], vmats[n], k * NZ)
        part = lax.dot_general(amats[n][...], vmats[n][...], NT, preferred_element_type=F32)
        acc[:768, :] = part if n == 0 else acc[:768, :] + part
    for x in range(XE):
        c = [acc[144 * k + 8 * x : 144 * k + 8 * x + 8, :] for k in range(4)]
        for k, channel in enumerate(OTHERS):
            craw[k, x] = c[channel]
        if x < 9:
            right, opened = prev[x], prev[9 + x]
        else:
            right, opened = rhs[x - 9], wall[x - 9].astype(F32)
        whole = right - c[0] * right if x < CX else -(c[0] * right)
        pay[x] = opened * (whole + c[2] + c[3])
        pay[XE + x] = c[1]
        pay[2 * XE + x] = acc[pl.ds(576 + x, 8, stride=24), :]
        extra = jnp.concatenate([right[0:1], right[7:8], opened[0:1], opened[4:5]], axis=0)
        pay[3 * XE + x // 2, (x % 2) * 4 : (x % 2) * 4 + 4, :] = extra


HEAD = 11
LATE = CX - HEAD


def slab_sums(got, rows, ssum, dsum):
    sub = lax.broadcasted_iota(I32, (8, NZ), 0)
    for n, x in enumerate(rows):
        g_row = (x % 2) * 4
        halos = [got[s, 2 * XE + x] for s in range(4)]
        for s in range(4):
            below, above = halos[(s + 3) % 4], halos[(s + 1) % 4]
            extra = got[s, 3 * XE + x // 2]
            rhs_f, rhs_l = extra[g_row : g_row + 1], extra[g_row + 1 : g_row + 2]
            o_f, o_l = extra[g_row + 2 : g_row + 3], extra[g_row + 3 : g_row + 4]
            from_below = o_f * (below[5:6] + below[7:8] - below[1:2] * rhs_f)
            from_above = o_l * (above[4:5] + above[6:7] - above[0:1] * rhs_l)
            at = n * 32 + s * 8
            ssum[at : at + 8, :] = edges(sub, got[s, x], from_below, from_above)
            dsum[at : at + 8, :] = edges(sub, got[s, XE + x], below[3:4], above[2:3])


def edges(sub, tile, to_first, to_last):
    return tile + jnp.where(sub == 0, to_first, 0.0) + jnp.where(sub == 7, to_last, 0.0)


def opened_block(got, x, out, at):
    g_row = (x % 2) * 4
    for s in range(4):
        out[at, 2 * s : 2 * s + 2, :] = got[s, 3 * XE + x // 2, g_row + 2 : g_row + 4, :]


def head_kernel(got, head, ssum, dsum):
    slab_sums(got, range(HEAD), ssum, dsum)
    for x in range(HEAD):
        for q in range(4):
            head[4 * x + q] = ssum[pl.ds(x * 32 + q, 8, stride=4), :]
            head[4 * (HEAD + x) + q] = dsum[pl.ds(x * 32 + q, 8, stride=4), :]
    for k, x in enumerate((1, 5, 9)):
        opened_block(got, x, head, 8 * HEAD + k)


def late_kernel(place, got, craw, late, keep, ssum, dsum):
    s_me = place[0]
    sub = lax.broadcasted_iota(I32, (8, NZ), 0)
    slab_sums(got, range(HEAD, XE), ssum, dsum)
    for n in range(XE - HEAD):
        for q in range(4):
            s_tile = ssum[pl.ds(n * 32 + q, 8, stride=4), :]
            d_tile = dsum[pl.ds(n * 32 + q, 8, stride=4), :]
            if n < LATE:
                late[4 * n + q] = s_tile
                late[4 * (LATE + n) + q] = d_tile
            else:
                keep[4 * (n - LATE) + q] = s_tile
                keep[4 * (n - LATE + 2) + q] = d_tile
    for x in range(XE):
        below = got[(s_me + 3) % 4, 2 * XE + x]
        above = got[(s_me + 1) % 4, 2 * XE + x]
        for k, c in enumerate(OTHERS):
            tile = edges(sub, craw[k, x], below[2 * c + 1 : 2 * c + 2], above[2 * c : 2 * c + 1])
            if x < 9:
                late[8 * LATE + 9 * k + x] = tile
            else:
                keep[16 + 9 * k + x - 9] = tile
    opened_block(got, 13, late, 8 * LATE + 27)


class Parts:
    def __init__(self, own_head, own_late, keep, next_head, next_late=None):
        self.own = (own_head, own_late, keep)
        self.next = (next_head, next_late)

    @staticmethod
    def tile(parts, x, kind, q):
        if x < HEAD:
            return parts[0][4 * (HEAD * kind + x) + q]
        if x < CX:
            return parts[1][4 * (LATE * kind + x - HEAD) + q]
        return parts[2][4 * (2 * kind + x - CX) + q]

    def joined(self, t, kind, q):
        if t < 14:
            return self.tile(self.own, t + 2, kind, q)
        other = self.tile(self.next, t - 14, kind, q)
        return other if t > 15 else other + self.tile(self.own, t + 2, kind, q)

    def opened(self, block):
        head, late = (self.own if block < 4 else self.next)[:2]
        k = block % 4
        return head[8 * HEAD + k] if k < 3 else late[8 * LATE + 27]

    def coefficient(self, t, q):
        diag = 6.0 + self.joined(t, 1, q)
        coef = OMEGA * self.opened((t + 1) // 4) * pl.reciprocal(diag)
        return coef, coef * self.joined(t, 0, q), diag


class Rows:
    def __init__(self, mid, rest, low, high):
        self.mid, self.rest, self.low, self.high = mid, rest, low, high

    def place(self, index):
        t, q = index
        if self.low <= t < self.high:
            return self.mid, (t, q)
        return self.rest, (t if t < self.low else t - self.high + self.low, q)

    def __getitem__(self, index):
        ref, at = self.place(index)
        return ref[at]

    def __setitem__(self, index, tile):
        ref, at = self.place(index)
        ref[at] = tile


def lane_index():
    return lax.broadcasted_iota(I32, (8, NZ), 1)


def take(tile, index):
    return jnp.take_along_axis(tile, index, axis=1)


def fine_sums(ref, t):
    lane = lane_index()
    cur = [ref[t, q] for q in range(4)]
    sums = []
    for q in range(4):
        after = cur[q + 1] if q < 3 else pltpu.roll(cur[0], 7, 0)
        before = cur[q - 1] if q else pltpu.roll(cur[3], 1, 0)
        left = jnp.where(lane == 0, 0.0, pltpu.roll(cur[q], 1, 1))
        right = jnp.where(lane == NZ - 1, 0.0, pltpu.roll(cur[q], NZ - 1, 1))
        sums.append((ref[t - 1, q] + ref[t + 1, q]) + (after + before) + (left + right))
    return cur, sums


def fine_sweep(src, dst, coef, base, low, high):
    for t in range(low, high):
        cur, sums = fine_sums(src, t)
        for q in range(4):
            dst[t, q] = (1.0 - OMEGA) * cur[q] + base[t, q] + coef[t, q] * sums[q]


def fine_residue(src, coef, base, weight):
    rows = []
    for k in range(8):
        total = [0.0, 0.0]
        for dx in range(2):
            t = 7 + 2 * k + dx
            cur, sums = fine_sums(src, t)
            for q in range(4):
                tile = weight[2 * k + dx, q] * (base[t, q] + coef[t, q] * sums[q] - OMEGA * cur[q])
                total[q // 2] = total[q // 2] + tile
        rows.append(jnp.concatenate(total, axis=1))
    return jnp.concatenate(rows, axis=0)


def choice(size, match):
    row = lax.broadcasted_iota(I32, (size, NZ), 0)
    column = lax.broadcasted_iota(I32, (size, NZ), 1)
    return jnp.where(match(row, column), 1.0, 0.0).astype(BF16)


def lane_sums(block, chosen):
    out, left = 0.0, block
    for _ in range(3):
        part = left.astype(BF16)
        out = out + jnp.dot(part, chosen, preferred_element_type=F32)
        left = left - part.astype(F32)
    return out


def pairs_packed():
    return choice(256, lambda r, c: r // 2 == c)


def fine_correct(v_in, v_out, w, coef, low, high):
    lane = lane_index()
    for a in range(low, high):
        for half in range(2):
            step = take(w[a], lane // 2 + 64 * half)
            for dx in range(2):
                t = 2 * a - 25 + dx
                for q in (2 * half, 2 * half + 1):
                    v_out[t, q] = v_in[t, q] + jnp.where(coef[t, q] > 0.0, step, 0.0)


def mid_sums(ref, a):
    lane = lane_index()
    cur = ref[a]
    turned = pltpu.roll(cur, 64, 1)
    beside = turned + jnp.where(lane < 64, pltpu.roll(turned, 1, 0), pltpu.roll(turned, 7, 0))
    left = jnp.where(lane % 64 == 0, 0.0, pltpu.roll(cur, 1, 1))
    right = jnp.where(lane % 64 == 63, 0.0, pltpu.roll(cur, NZ - 1, 1))
    return cur, (ref[a - 1] + ref[a + 1]) + beside + (left + right)


def mid_sweep(src, dst, coef, base, low, high):
    for a in range(low, high):
        cur, total = mid_sums(src, a)
        dst[a] = (1.0 - OMEGA) * cur + base[a] + coef[a] * total


def low_sweep(src, dst, coef, base, low, high):
    for m in range(low, high):
        cur = src[m]
        total = (src[m - 1] + src[m + 1]) + (pltpu.roll(cur, 1, 0) + pltpu.roll(cur, 7, 0))
        total = total + (pltpu.roll(cur, 1, 1) + pltpu.roll(cur, NZ - 1, 1))
        dst[m] = (1.0 - OMEGA) * cur + base[m] + coef[m] * total


def levels_solve(c1, g1, c2, cb1, w_a, w_b, cb2, u_a, u_b):
    lane = lane_index()
    mid_sweep(cb1, w_a, c1, cb1, 3, 37)
    totals = []
    for m in range(2, 18):
        total = 0.0
        for a in (2 * m, 2 * m + 1):
            cur, beside = mid_sums(w_a, a)
            total = total + g1[a] * (cb1[a] + c1[a] * beside - OMEGA * cur)
        totals.append(total)
    below = lane_sums(jnp.concatenate(totals, axis=0), choice(NZ, lambda r, c: r % 64 // 2 == c))
    for m in range(2, 18):
        cb2[m] = 2.0 * c2[m] * below[8 * (m - 2) : 8 * (m - 1)]
    low_sweep(cb2, u_a, c2, cb2, 3, 17)
    low_sweep(u_a, u_b, c2, cb2, 4, 16)
    low_sweep(u_b, u_a, c2, cb2, 5, 15)
    for m in range(5, 15):
        step = take(u_a[m], (lane % 64) // 2)
        for a in (2 * m, 2 * m + 1):
            w_a[a] = w_a[a] + jnp.where(c1[a] > 0.0, step, 0.0)
    mid_sweep(w_a, w_b, c1, cb1, 12, 28)
    mid_sweep(w_b, w_a, c1, cb1, 13, 27)


def rest_kernel(place, own_head, own_late, keep, next_head, next_late, cc, cb, coupled, cc_r, cb_r, v2_r, gg, flat):
    parts = Parts(own_head, own_late, keep, next_head, next_late)
    for k, c in enumerate(OTHERS):
        for x in range(CX):
            own, other = 16 + 9 * k + x, 8 * LATE + 9 * k + x - 7
            if x < 7:
                tile = keep[own]
            elif x < 9:
                tile = keep[own] + next_late[other]
            else:
                tile = next_late[other]
            coupled[c, x] = tile
    for x in range(CX):
        for q in range(4):
            flat[pl.ds(x * 32 + q, 8, stride=4), :] = parts.joined(7 + x, 1, q)
    for x in range(CX):
        coupled[1, x] = flat[pl.ds(pl.multiple_of(x * 32 + 8 * place[0], 8), 8), :]
    coefs, bases, v2 = Rows(cc, cc_r, 5, 25), Rows(cb, cb_r, 5, 25), Rows(None, v2_r, 6, 24)
    for t in (*range(5), *range(25, T0)):
        for q in range(4):
            coefs[t, q], bases[t, q], _ = parts.coefficient(t, q)
    fine_sweep(bases, v2, coefs, bases, 1, 6)
    fine_sweep(bases, v2, coefs, bases, 24, 29)
    for t in range(7, 23):
        for q in range(4):
            gg[t - 7, q] = (1.0 / OMEGA) * (6.0 + parts.joined(t, 1, q))


def start_kernel(own_head, own_late, keep, next_head, cc, cb, v2, send, gg):
    parts = Parts(own_head, own_late, keep, next_head)
    for t in range(5, 25):
        for q in range(4):
            cc[t, q], cb[t, q], diag = parts.coefficient(t, q)
            if 7 <= t < 23:
                gg[t - 7, q] = (1.0 / OMEGA) * diag
    fine_sweep(cb, v2, cc, cb, 6, 24)
    damps = []
    for k in range(8):
        total = [0.0, 0.0]
        for dx in range(2):
            for q in range(4):
                total[q // 2] = total[q // 2] + parts.joined(7 + 2 * k + dx, 1, q)
        damps.append(jnp.concatenate(total, axis=1))
    lows = [damps[2 * m] + damps[2 * m + 1] for m in range(4)]
    opened = jnp.concatenate([parts.opened(2 + m) for m in range(4)], axis=0).astype(BF16)
    opened_1 = jnp.dot(opened, choice(NZ, lambda r, c: r == c % 64 * 2), preferred_element_type=F32)
    opened_2 = jnp.dot(opened, choice(NZ, lambda r, c: r == c * 4), preferred_element_type=F32)
    packed = pairs_packed()
    diag = 1.5 + 0.125 * lane_sums(jnp.concatenate(damps, axis=0), packed)
    low_diag = 0.375 + 0.015625 * lane_sums(
        jnp.concatenate(lows, axis=0), choice(256, lambda r, c: r % NZ // 4 == c)
    )
    source = 0.125 * lane_sums(fine_residue(v2, cc, cb, gg), packed)
    inverse = OMEGA * pl.reciprocal(diag)
    below = (0.0625 * OMEGA) * opened_2 * pl.reciprocal(low_diag)
    for k in range(8):
        rows = slice(8 * k, 8 * k + 8)
        coef = opened_1[8 * (k // 2) : 8 * (k // 2) + 8] * inverse[rows]
        send[k] = coef * source[rows]
        send[8 + k] = 0.25 * coef
    for m in range(4):
        send[16 + m] = below[8 * m : 8 * m + 8]


def window(place, high_pair, both, own, low_pair):
    even_core, even_chip = place[1] == 0, place[2] == 0
    size = own.shape[0]

    def part(n, k):
        if n == 2:
            return own[k]
        if n in (1, 3):
            return jnp.where(even_core == (n == 1), both[size + k], both[k])
        return jnp.where(even_chip == (n == 0), low_pair[k], high_pair[k])

    return part


def middle_kernel(place, high_pair, both, own, low_pair, cc, cb, gg, v2, cc_r, cb_r, v2_r, v_out, c1, g1, c2, send,
                  cb1, w_a, w_b, cb2, u_a, u_b, v_a, v_b):
    part = window(place, high_pair, both, own, low_pair)
    for n in range(5):
        for k in range(8):
            cb1[8 * n + k] = part(n, k)
            c1[8 * n + k] = part(n, 8 + k)
            g1[8 * n + k] = 0.25 * pl.reciprocal(jnp.where(c1[8 * n + k] > 0.0, c1[8 * n + k], 1.0))
        for k in range(4):
            c2[4 * n + k] = part(n, 16 + k)
    levels_solve(c1, g1, c2, cb1, w_a, w_b, cb2, u_a, u_b)
    cc, cb, v2 = Rows(cc, cc_r, 5, 25), Rows(cb, cb_r, 5, 25), Rows(v2, v2_r, 6, 24)
    fine_correct(v2, v_a, w_a, cc, 13, 27)
    fine_sweep(v_a, v_b, cc, cb, 2, 28)
    fine_sweep(v_b, v_a, cc, cb, 3, 27)
    fine_sweep(v_a, v_b, cc, cb, 4, 26)
    fine_sweep(v_b, v_out, cc, cb, 5, 25)
    source = lane_sums(fine_residue(v_out, cc, cb, gg), pairs_packed())
    for k in range(8):
        send[k] = 0.5 * c1[16 + k] * source[8 * k : 8 * k + 8]


def last_kernel(place, high_pair, both, own, low_pair, cc, cb, v2, c1, g1, c2, deposits, out, coupled,
                cb1, w_a, w_b, cb2, u_a, u_b, v_a, v_b, flat, sem):
    copy = pltpu.make_async_copy(deposits, coupled, sem)
    copy.start()
    part = window(place, high_pair, both, own, low_pair)
    for n in range(5):
        for k in range(8):
            cb1[8 * n + k] = part(n, k)
    levels_solve(c1, g1, c2, cb1, w_a, w_b, cb2, u_a, u_b)
    fine_correct(v2, v_a, w_a, cc, 15, 25)
    fine_sweep(v_a, v_b, cc, cb, 6, 24)
    fine_sweep(v_b, v_a, cc, cb, 7, 23)
    for x in range(CX):
        for q in range(4):
            flat[pl.ds(x * 32 + q, 8, stride=4), :] = v_a[7 + x, q]
    for x in range(CX):
        out[x] = flat[pl.ds(pl.multiple_of(x * 32 + 8 * place[0], 8), 8), :]
    copy.wait()


def call(kernel, outs, scratch, operands, smem_first=False, in_hbm=False, outs_hbm=0, cost=1000000, limit=LIMIT):
    kind = pltpu.HBM if in_hbm else pltpu.VMEM
    specs = [pl.BlockSpec(memory_space=kind) for _ in operands]
    if smem_first:
        specs[0] = pl.BlockSpec(memory_space=pltpu.SMEM)
    shapes = [jax.ShapeDtypeStruct(shape, F32) for shape in outs]
    return pl.pallas_call(
        kernel,
        out_shape=shapes,
        in_specs=specs,
        out_specs=[
            pl.BlockSpec(memory_space=pltpu.VMEM if n < len(outs) - outs_hbm else pltpu.HBM) for n in range(len(outs))
        ],
        scratch_shapes=[pltpu.VMEM(*piece) if isinstance(piece, tuple) else piece for piece in scratch],
        compiler_params=pltpu.CompilerParams(vmem_limit_bytes=limit),
        cost_estimate=pl.CostEstimate(flops=cost, bytes_accessed=cost, transcendentals=0),
    )(*operands)


def fetch(block, distance):
    count = lax.axis_size("box")
    return lax.ppermute(block, "box", [((i + distance) % count, i) for i in range(count)])


def swap(block):
    return lax.ppermute(block, "box", [(i ^ 1, i) for i in range(lax.axis_size("box"))])


def meet(block, odd):
    count = lax.axis_size("box")
    chips = [((k + odd ^ 1) - odd) % (count // 2) for k in range(count // 2)]
    return lax.ppermute(block, "box", [(2 * chips[i // 2] + i % 2, i) for i in range(count)])


def around(block, place, beside=None):
    low_pair, high_pair = meet(block, 1), meet(block, 0)
    onward = jnp.concatenate([block, jnp.where(place[1] == place[2], high_pair, low_pair)], axis=0)
    if beside is not None:
        onward, beside = lax.optimization_barrier((onward, beside))
    return [high_pair, swap(onward), block, low_pair], beside


def shards(volume, drag, momentum, offsets, cell_index, destinations, rhs, wall):
    box = lax.axis_index("box").astype(I32)
    place = jnp.stack([lax.axis_index("slab").astype(I32), box % 2, box // 2 % 2])
    prev = fetch(jnp.concatenate([rhs[7:], wall[7:].astype(F32)], axis=0), -1)
    one = (1, PART)
    (outgoing,) = call(
        route_kernel,
        [(N_BOX, 1, 8 * CAP)],
        [(one, F32), (one, F32), ((2, PART), F32), ((3, PART), F32), (one, I32), (one, I32),
         ((24 * CAP, PART), BF16), ((N_BOX, 8 * CAP), F32), pltpu.SemaphoreType.DMA((6,))],
        [volume.reshape(one), drag.reshape(one), momentum, offsets, cell_index.reshape(one), destinations.reshape(one)],
        in_hbm=True,
        limit=62 * 1024 * 1024,
    )
    incoming = lax.all_to_all(outgoing, "box", split_axis=0, concat_axis=0, tiled=True)
    pay, craw = call(
        deposit_kernel,
        [(3 * XE + XE // 2, 8, NZ), (3, XE, 8, NZ)],
        [((13, CAP, NZ), F32), ((3, CAP, NZ), I32), ((XE, CAP, NZ), F32), ((800, NZ), F32)]
        + [((768, SLOTS // CHUNKS), BF16)] * CHUNKS + [((NZ, SLOTS // CHUNKS), BF16)] * CHUNKS,
        [incoming.reshape(N_BOX, 8 * CAP), rhs, wall, prev],
    )
    slabs = lax.all_gather(pay, "slab")
    sums = [((HEAD * 32 + 8, NZ), F32)] * 2
    (head,) = call(head_kernel, [(8 * HEAD + 3, 8, NZ)], sums, [slabs])
    next_head = fetch(head, 1)
    late, keep = call(
        late_kernel, [(8 * LATE + 28, 8, NZ), (43, 8, NZ)], sums, [place, slabs, craw], smem_first=True
    )
    next_late = fetch(late, 1)
    fine, mid, low = (T0, 4, 8, NZ), (T1, 8, NZ), (T2, 8, NZ)
    weights = (CX, 4, 8, NZ)
    cc, cb, v2, first = call(
        start_kernel, [fine, fine, fine, (20, 8, NZ)], [(weights, F32)], [head, late, keep, next_head]
    )
    deposits, cc_r, cb_r, v2_r, gg = call(
        rest_kernel,
        [(4, CX, 8, NZ), (10, 4, 8, NZ), (10, 4, 8, NZ), (12, 4, 8, NZ), weights],
        [((CX * 32 + 8, NZ), F32)],
        [place, head, late, keep, next_head, next_late, cc, cb],
        smem_first=True,
    )
    scratch = [(mid, F32), (mid, F32), (mid, F32), (low, F32), (low, F32), (low, F32), (fine, F32), (fine, F32)]
    parts, deposits = around(first, place, deposits)
    v3, c1, g1, c2, second = call(
        middle_kernel,
        [fine, mid, mid, low, (8, 8, NZ)],
        scratch,
        [place] + parts + [cc, cb, gg, v2, cc_r, cb_r, v2_r],
        smem_first=True,
    )
    parts, _ = around(second, place)
    pressure, coupled = call(
        last_kernel,
        [(CX, 8, NZ), (4, CX, 8, NZ)],
        scratch + [((CX * 32 + 8, NZ), F32), pltpu.SemaphoreType.DMA],
        [place] + parts + [cc, cb, v3, c1, g1, c2, deposits],
        smem_first=True,
        outs_hbm=1,
    )
    return coupled, pressure


def solution(mesh):
    in_specs = (
        P(("box", "slab")),
        P(("box", "slab")),
        P(None, ("box", "slab")),
        P(None, ("box", "slab")),
        P(("box", "slab")),
        P(("box", "slab"), None),
        P("box", "slab", None),
        P("box", "slab", None),
    )
    out_specs = (P(None, "box", "slab", None), P("box", "slab", None))
    return jax.shard_map(shards, mesh=mesh, in_specs=in_specs, out_specs=out_specs, check_vma=False)
```
